128 devices in a mesh: grp: 8 (over z_hi, x), resp: 16 (over z_lo, y, core).
Axes of the slice: x: 4, y: 4, z: 4 (z_hi: 2, z_lo: 2; z = z_hi * 2 + z_lo), core: 2. Of those that a mesh axis runs over, the one named last changes fastest.
Arguments:
- queries: bfloat16 [8, 16, 256, 2560], P('grp', 'resp'), may hold values from -5 to 5
- resp_keys: bfloat16 [8, 16, 256, 512], P('grp', 'resp'), may hold values from -5 to 5
- resp_values: bfloat16 [8, 16, 256, 512], P('grp', 'resp'), may hold values from -5 to 5
- prompt_keys: bfloat16 [8, 2048, 512], P('grp', 'resp'), may hold values from -5 to 5
- prompt_values: bfloat16 [8, 2048, 512], P('grp', 'resp'), may hold values from -5 to 5
- out_grad: bfloat16 [8, 16, 256, 2560], P('grp', 'resp'), may hold values from -2.390625 to 2.390625
- lengths: int32 [8, 16], P('grp', 'resp'), may hold values from 32 to 256, as said below
- rewards: int32 [8, 16], P('grp', 'resp'), may hold values from 0 to 12, as said below
Outputs:
- attended: bfloat16 [8, 16, 256, 2560], P('grp', 'resp')
- grad_queries: bfloat16 [8, 16, 256, 2560], P('grp', 'resp')
- grad_resp_keys: bfloat16 [8, 16, 256, 512], P('grp', 'resp')
- grad_resp_values: bfloat16 [8, 16, 256, 512], P('grp', 'resp')
- grad_prompt_keys: bfloat16 [8, 2048, 512], P('grp', 'resp')
- grad_prompt_values: bfloat16 [8, 2048, 512], P('grp', 'resp')
The draws below stay inside these ranges and needn't reach their ends.
Inputs may be any that keep to these rules, and one draw needn't show every extreme that they name: `lengths`: some response in every draw has the full length 256. Each group's rewards run from 0 up to a top score of that group, which some response reaches; one group's top is 12 and another's is 1.
All inputs are finite; a program needn't handle non-finite values.
Results may differ from the reference program's by a relative error of at most 0.03.
Values may be sent and summed in bfloat16 or wider, within the bound.
A program may use at most 128 MiB of HBM per device.

```python
import jax
import jax.numpy as jnp
from jax import lax

H = 20
KVH = 4
DH = 128
R = 256
PROMPT = 2048
N_GRP = 8
N_RESP = 16


def draw_queries(key, part):
    key = jax.random.fold_in(key, 11)
    full_shape = (N_GRP, N_RESP, R, H * DH)
    values_drawn = jax.random.truncated_normal(key, -5.0, 5.0, full_shape, jnp.float32)
    return values_drawn.astype(jnp.bfloat16)


def draw_prompt_keys(key, part):
    key = jax.random.fold_in(key, 23)
    full_shape = (N_GRP, PROMPT, KVH * DH)
    values_drawn = jax.random.truncated_normal(key, -5.0, 5.0, full_shape, jnp.float32)
    return values_drawn.astype(jnp.bfloat16)


def draw_lengths(key, part):
    key = jax.random.fold_in(key, 37)
    count = N_GRP * N_RESP
    flat_index = jnp.arange(count).reshape(N_GRP, N_RESP)
    low_end = R // 8
    top_length = low_end + (R - low_end) * (flat_index + 1) // count
    jitter = jax.random.randint(key, (N_GRP, N_RESP), 0, R // 16 + 1)
    drawn = jnp.maximum(top_length - jitter, low_end)
    return jnp.where(flat_index == count - 1, R, drawn).astype(jnp.int32)


def draw_rewards(key, part):
    key = jax.random.fold_in(key, 53)
    keys_split = jax.random.split(key, 5)
    top_score = jax.random.randint(keys_split[0], (N_GRP,), 1, 13)
    high_group = jax.random.randint(keys_split[1], (), 0, N_GRP)
    low_group = (high_group + 1 + jax.random.randint(keys_split[2], (), 0, N_GRP - 1)) % N_GRP
    group_index = jnp.arange(N_GRP)
    top_score = jnp.where(group_index == high_group, 12, top_score)
    top_score = jnp.where(group_index == low_group, 1, top_score)
    drawn = jax.random.randint(keys_split[3], (N_GRP, N_RESP), 0, top_score[:, None] + 1)
    holder = jax.random.randint(keys_split[4], (N_GRP,), 0, N_RESP)
    drawn = jnp.where(jnp.arange(N_RESP)[None, :] == holder[:, None], top_score[:, None], drawn)
    return drawn.astype(jnp.int32)


def levels(stream_key, extent, shards, smallest, largest):
    def one(dim, shards_of):
        heights = jax.random.uniform(jax.random.fold_in(jax.random.fold_in(stream_key, 6), dim), (shards_of,), jnp.float32, smallest / len(shards), largest / len(shards))
        return jnp.repeat(jnp.exp(heights), extent[dim] // shards_of).reshape((-1,) + (1,) * (len(extent) - dim - 1))

    factor_of = one(*shards[0])
    for cut in shards[1:]:
        factor_of = factor_of * one(*cut)
    return factor_of


def gaussian(own_key, shape, scale, bound, pieces=(), held_as=jnp.bfloat16):
    factor_of = levels(own_key, shape, pieces, -0.22, 0.18) if pieces else 1.0
    entries = jax.random.normal(own_key, shape, jnp.float32) * scale * factor_of
    return jnp.minimum(jnp.maximum(entries, -bound), bound).astype(held_as)


def setup_inputs(seed: int = 0) -> dict:
    arg_keys = jax.random.split(jax.random.key(seed), 9)
    return {
        "queries": draw_queries(jax.random.fold_in(arg_keys[8], 71), 0),
        "resp_keys": gaussian(arg_keys[1], (N_GRP, N_RESP, R, KVH * DH), 1.0, 5.0, ((0, 8), (1, 16))),
        "resp_values": gaussian(arg_keys[2], (N_GRP, N_RESP, R, KVH * DH), 1.0, 5.0, ((0, 8), (1, 16))),
        "prompt_keys": draw_prompt_keys(jax.random.fold_in(arg_keys[8], 71), 0),
        "prompt_values": gaussian(arg_keys[4], (N_GRP, PROMPT, KVH * DH), 1.0, 5.0, ((0, 8), (1, 16))),
        "out_grad": gaussian(arg_keys[5], (N_GRP, N_RESP, R, H * DH), 0.4, 2.390625, ((0, 8), (1, 16))),
        "lengths": draw_lengths(jax.random.fold_in(arg_keys[8], 71), 0),
        "rewards": draw_rewards(jax.random.fold_in(arg_keys[8], 71), 0),
    }


def rounded(values):
    return lax.optimization_barrier(values.astype(jnp.bfloat16)).astype(jnp.float32)

def response_pass(query_one, prompt_k, prompt_v, resp_k, resp_v, grad_one, weight_one):
    inv_root = DH ** (-0.5)
    prompt_len = prompt_k.shape[0]
    query_heads = query_one.astype(jnp.float32).reshape(R, KVH, H // KVH, DH)
    keys_all = jnp.concatenate([prompt_k, resp_k], axis=0).astype(jnp.float32).reshape(-1, KVH, DH)
    values_all = jnp.concatenate([prompt_v, resp_v], axis=0).astype(jnp.float32).reshape(-1, KVH, DH)
    position = jnp.arange(R)[:, None]
    key_index = jnp.arange(prompt_len + R)[None, :]
    visible = (key_index < prompt_len) | (key_index - prompt_len <= position)
    logits = jnp.einsum('tghd,ngd->ghtn', query_heads, keys_all) * inv_root
    logits = jnp.where(visible, logits, -jnp.inf)
    log_total = jax.nn.logsumexp(logits, axis=-1)
    weights_soft = jnp.exp(logits - log_total[..., None])
    soft_low = rounded(weights_soft)
    output_heads = jnp.einsum('ghtn,ngd->tghd', soft_low, values_all)
    attended = output_heads.reshape(R, H * DH).astype(jnp.bfloat16)
    attended_heads = rounded(output_heads)
    grad_heads = rounded(grad_one.astype(jnp.float32) * weight_one[:, None]).reshape(R, KVH, H // KVH, DH)
    row_delta = lax.optimization_barrier(jnp.sum(grad_heads * attended_heads, axis=-1)).transpose(1, 2, 0)
    grad_soft = jnp.einsum('tghd,ngd->ghtn', grad_heads, values_all)
    grad_logits = rounded(weights_soft * (grad_soft - row_delta[..., None]))
    grad_query = (jnp.einsum('ghtn,ngd->tghd', grad_logits, keys_all) * inv_root).reshape(R, H * DH).astype(jnp.bfloat16)
    grad_keys = jnp.einsum('ghtn,tghd->ngd', grad_logits, query_heads).reshape(-1, KVH * DH) * inv_root
    grad_values = jnp.einsum('ghtn,tghd->ngd', soft_low, grad_heads).reshape(-1, KVH * DH)
    return (attended, grad_query, grad_keys[prompt_len:].astype(jnp.bfloat16), grad_values[prompt_len:].astype(jnp.bfloat16), grad_keys[:prompt_len], grad_values[:prompt_len])

def reference(queries, resp_keys, resp_values, prompt_keys, prompt_values, out_grad, lengths, rewards):
    reward_float = rewards.astype(jnp.float32)
    sum_one = lax.optimization_barrier(jnp.sum(rewards, axis=1)).astype(jnp.float32)
    sum_two = lax.optimization_barrier(jnp.sum(rewards * rewards, axis=1)).astype(jnp.float32)
    mean_reward = sum_one / N_RESP
    variance = (N_RESP * sum_two - sum_one * sum_one) / (N_RESP * N_RESP)
    advantage = (reward_float - mean_reward[:, None]) / jnp.maximum(jnp.sqrt(variance), 1.0)[:, None]
    live_total = jnp.sum(lengths).astype(jnp.float32)
    norm_factor = N_GRP * N_RESP * R / live_total
    live_rows = (jnp.arange(R)[None, None, :] < lengths[:, :, None]).astype(jnp.float32)
    weights = advantage[:, :, None] * norm_factor * live_rows

    def one_group(inputs_group):
        query_group, rk_group, rv_group, grad_group, weight_group, pk_group, pv_group = inputs_group

        def one_response(state_now, item_now):
            results_one = response_pass(item_now[0], pk_group, pv_group, item_now[1], item_now[2], item_now[3], item_now[4])
            return ((state_now[0] + results_one[4], state_now[1] + results_one[5]), results_one[:4])
        empty_sums = jnp.zeros(pk_group.shape, jnp.float32)
        sums_out, per_response = lax.scan(one_response, (empty_sums, empty_sums), (query_group, rk_group, rv_group, grad_group, weight_group))
        return per_response + (sums_out[0].astype(jnp.bfloat16), sums_out[1].astype(jnp.bfloat16))
    results = lax.map(one_group, (queries, resp_keys, resp_values, out_grad, weights, prompt_keys, prompt_values))
    return (results[0], results[1], results[2], results[3], results[4], results[5])
```

```python
import math

import jax
import jax.numpy as jnp
from jax import lax
from jax.experimental import pallas as pl
from jax.experimental.pallas import tpu as pltpu
from jax.sharding import PartitionSpec as P

DH = 128
F32 = jnp.float32
BF16 = jnp.bfloat16
MESH = pl.DeviceIdType.MESH

SLOTS = ((0, 0), (0, 3), (0, 1), (1, 0), (1, 3), (0, 2), (1, 1), (1, 2))
OWN, YM, YP, ZZ, ZYM, YY, ZYP, ZYY = range(8)


def nn(a, b):
    return jnp.dot(a, b, preferred_element_type=F32)


def nt(a, b):
    return lax.dot_general(a, b, (((1,), (1,)), ((), ())), preferred_element_type=F32)


def kernel(
    n_grp, heads_per, q_hbm, rk_hbm, rv_hbm, pk_hbm, pv_hbm, og_hbm, len_ref, rew_ref,
    att_hbm, dq_hbm, drk_hbm, drv_hbm, dpk_hbm, dpv_hbm,
    qn, gn, rkn, rvn, kvn, qT, gT, e_st, m_st, m_cur, l_cur, acc, dqa, ds, aux,
    stat_out, stat_in, glen_out, glen_in, snd, rcv, own_part, att_n, dq_n, rg_n, pg_n,
    sem_l, sem_ps, sem_pr, sem_as, sem_ar, sem_ss, sem_sr, sem_gs, sem_gr,
    sem_ms, sem_mr, sem_ol, sem_os, sem_or,
):
    rows = qn.shape[1]
    half_q = qn.shape[2]
    half_k = rkn.shape[2]
    piece = pk_hbm.shape[1]
    blk = 2 * piece
    width = heads_per * rows
    inv_root = DH ** (-0.5)
    scale2 = inv_root * math.log2(math.e)
    me = lax.axis_index("resp")
    grp = lax.axis_index("grp")
    z = me // 8
    y = (me // 2) % 4
    c = me % 2

    def at(dz, dy, dc):
        return {"resp": ((z + dz) % 2) * 8 + ((y + dy) % 4) * 2 + (c + dc) % 2}

    def to(src, dst, s_sem, r_sem, target):
        return pltpu.make_async_remote_copy(
            src_ref=src, dst_ref=dst, send_sem=s_sem, recv_sem=r_sem,
            device_id=target, device_id_type=MESH,
        )

    cq = pl.ds(pl.multiple_of(c * half_q, half_q), half_q)
    oq = pl.ds(pl.multiple_of((1 - c) * half_q, half_q), half_q)
    ck = pl.ds(pl.multiple_of(c * half_k, half_k), half_k)
    ok = pl.ds(pl.multiple_of((1 - c) * half_k, half_k), half_k)
    my_rows = pl.ds(pl.multiple_of(c * piece, piece), piece)

    local = [
        pltpu.make_async_copy(pk_hbm.at[0, :, ck], kvn.at[OWN, 0, my_rows, :], sem_l.at[0]),
        pltpu.make_async_copy(pv_hbm.at[0, :, ck], kvn.at[OWN, 1, my_rows, :], sem_l.at[1]),
        pltpu.make_async_copy(q_hbm.at[0, 0, :, cq], qn.at[0], sem_l.at[2]),
        pltpu.make_async_copy(rk_hbm.at[0, 0, :, ck], rkn.at[0], sem_l.at[3]),
        pltpu.make_async_copy(rv_hbm.at[0, 0, :, ck], rvn.at[0], sem_l.at[4]),
        pltpu.make_async_copy(og_hbm.at[0, 0, :, cq], gn.at[0], sem_l.at[5]),
    ]
    for cp in local:
        cp.start()

    row_id = lax.broadcasted_iota(jnp.int32, (8, 128), 0)
    stat_out[...] = jnp.where(row_id == 0, len_ref[0, 0], rew_ref[0, 0])

    others = [
        (dz, dy, dc) for dz in range(2) for dy in range(4) for dc in range(2) if dz or dy or dc
    ]
    barrier = pltpu.get_barrier_semaphore()
    for dz, dy, dc in others:
        pl.semaphore_signal(barrier, inc=1, device_id=at(dz, dy, dc), device_id_type=MESH)
    for dg in range(1, n_grp):
        pl.semaphore_signal(
            barrier, inc=1, device_id={"grp": (grp + dg) % n_grp}, device_id_type=MESH
        )
    pl.semaphore_wait(barrier, len(others) + n_grp - 1)

    twin = at(0, 0, 1)
    pair = [
        to(pk_hbm.at[0, :, ok], kvn.at[OWN, 0, my_rows, :], sem_ps.at[0], sem_pr.at[0], twin),
        to(pv_hbm.at[0, :, ok], kvn.at[OWN, 1, my_rows, :], sem_ps.at[1], sem_pr.at[1], twin),
        to(q_hbm.at[0, 0, :, oq], qn.at[1], sem_ps.at[2], sem_pr.at[2], twin),
        to(rk_hbm.at[0, 0, :, ok], rkn.at[1], sem_ps.at[3], sem_pr.at[3], twin),
        to(rv_hbm.at[0, 0, :, ok], rvn.at[1], sem_ps.at[4], sem_pr.at[4], twin),
        to(og_hbm.at[0, 0, :, oq], gn.at[1], sem_ps.at[5], sem_pr.at[5], twin),
    ]
    for cp in pair:
        cp.start()

    z_to, up, down = at(1, 0, 0), at(0, 1, 0), at(0, 3, 0)
    ag_plan = (
        (OWN, ZZ, 0, z_to), (OWN, YM, 0, up), (OWN, YP, 0, down),
        (OWN, ZZ, 1, z_to), (OWN, YM, 1, up), (OWN, YP, 1, down),
        (YM, YY, 0, up), (YM, ZYM, 0, z_to), (YM, ZYM, 1, z_to),
        (YP, YY, 1, down), (ZZ, ZYP, 0, down), (ZZ, ZYP, 1, down),
        (ZYM, ZYY, 0, up), (ZYM, ZYY, 1, up),
    )
    ag = {}
    for src, dst, kv, target in ag_plan:
        ag[dst, kv] = to(
            kvn.at[src, kv], kvn.at[dst, kv], sem_as.at[dst, kv], sem_ar.at[dst, kv], target
        )

    for i in (0, 1):
        local[i].wait()
        pair[i].wait_recv()
    for kv in (0, 1):
        for dst in (ZZ, YM, YP):
            ag[dst, kv].start()

    stats = []
    for n, (dz, dy, dc) in enumerate(others):
        slot = ((-dz) % 2) * 8 + ((-dy) % 4) * 2 + dc
        stats.append(
            to(stat_out, stat_in.at[slot], sem_ss.at[slot], sem_sr.at[slot], at(dz, dy, dc))
        )
        stats[-1].start()

    def turn(src, dst, r):
        for j in range(2):
            for h in range(heads_per):
                dst[2 * r + j, :, h * rows:(h + 1) * rows] = src[
                    r, :, (j * heads_per + h) * DH:(j * heads_per + h + 1) * DH
                ].T

    def forward(k, vt, u, block, first):
        for h in range(heads_per):
            cols = slice(h * rows, (h + 1) * rows)
            s = nn(k, qT[u, :, cols])
            if first:
                seen = lax.broadcasted_iota(jnp.int32, s.shape, 0) <= (
                    lax.broadcasted_iota(jnp.int32, s.shape, 1)
                )
                s = jnp.where(seen, s, -jnp.inf)
                m_new = jnp.max(s, axis=0, keepdims=True)
            else:
                m_old = m_cur[u:u + 1, cols]
                m_new = jnp.maximum(m_old, jnp.max(s, axis=0, keepdims=True))
            e = jnp.exp2(s * scale2 - m_new * scale2)
            total = jnp.sum(e, axis=0, keepdims=True)
            low = e.astype(BF16)
            e_st[block, u, :, cols] = low
            part = nn(vt, low)
            if first:
                l_cur[u:u + 1, cols] = total
                acc[u, :, cols] = part
            else:
                alpha = jnp.exp2((m_old - m_new) * scale2)
                l_cur[u:u + 1, cols] = l_cur[u:u + 1, cols] * alpha + total
                acc[u, :, cols] = acc[u, :, cols] * alpha + part
            m_cur[u:u + 1, cols] = m_new
            m_st[block, u:u + 1, cols] = m_new

    n_blocks = 8
    for r in range(2):
        if r == 0:
            for i in (2, 3, 4):
                local[i].wait()
        else:
            for i in (2, 3, 4):
                pair[i].wait_recv()
        turn(qn, qT, r)
        for j in range(2):
            heads = slice(j * DH, (j + 1) * DH)
            forward(rkn[r, :, heads], rvn[r, :, heads].T, 2 * r + j, n_blocks, True)

    for cp in stats:
        cp.wait_recv()
    sum_one = stat_out[1:2, :]
    sum_two = sum_one * sum_one
    live = stat_out[0:1, :]
    for slot in range(1, 16):
        one = stat_in[slot, 1:2, :]
        sum_one = sum_one + one
        sum_two = sum_two + one * one
        live = live + stat_in[slot, 0:1, :]
    glen_out[...] = jnp.broadcast_to(live, (8, 128))
    glens = []
    for dg in range(1, n_grp):
        glens.append(
            to(
                glen_out, glen_in.at[n_grp - dg], sem_gs.at[n_grp - dg], sem_gr.at[n_grp - dg],
                {"grp": (grp + dg) % n_grp},
            )
        )
        glens[-1].start()

    def pass_on(waits, starts):
        for key in waits:
            ag[key].wait_recv()
        for key in starts:
            ag[key].start()

    @pl.loop(0, n_blocks)
    def forward_step(step):
        @pl.when(step == 1)
        def _():
            pass_on([(YM, 0)], [(YY, 0), (ZYM, 0)])
            pass_on([(ZZ, 0)], [(ZYP, 0)])
            pass_on([(YM, 1)], [(ZYM, 1)])
            pass_on([(YP, 0), (YP, 1)], [(YY, 1)])
            pass_on([(ZZ, 1)], [(ZYP, 1)])

        @pl.when(step == 4)
        def _():
            pass_on([(ZYM, 0)], [(ZYY, 0)])
            pass_on([(ZYM, 1)], [(ZYY, 1)])

        @pl.when(step == 5)
        def _():
            pass_on([(YY, 0), (YY, 1)], [])

        @pl.when(step == 6)
        def _():
            pass_on([(ZYP, 0), (ZYP, 1)], [])

        @pl.when(step == 7)
        def _():
            pass_on([(ZYY, 0), (ZYY, 1)], [])

        for j in range(2):
            heads = slice(j * DH, (j + 1) * DH)
            k = kvn[step, 0, :, heads]
            vt = kvn[step, 1, :, heads].T
            for r in range(2):
                forward(k, vt, 2 * r + j, step, False)

    for cp in glens:
        cp.wait_recv()
    for slot in range(1, n_grp):
        live = live + glen_in[slot, 0:1, :]
    n_resp = 16
    sum_one = sum_one.astype(F32)
    sum_two = sum_two.astype(F32)
    mean = sum_one / n_resp
    variance = (n_resp * sum_two - sum_one * sum_one) / (n_resp * n_resp)
    spread = jnp.maximum(jnp.sqrt(variance), 1.0)
    norm = (n_grp * n_resp * rows) / live.astype(F32)
    local[5].wait()
    pair[5].wait_recv()
    for r in range(2):
        turn(gn, gT, r)
        length = stat_out[0:1, :] if r == 0 else stat_in[1, 0:1, :]
        reward = stat_out[1:2, :] if r == 0 else stat_in[1, 1:2, :]
        strength = (reward.astype(F32) - mean) / spread * norm
        weight = jnp.concatenate(
            [
                jnp.where(
                    lax.broadcasted_iota(jnp.int32, (1, 128), 1) + start < length, strength, 0.0
                )
                for start in range(0, rows, 128)
            ],
            axis=1,
        )
        for j in range(2):
            u = 2 * r + j
            for h in range(heads_per):
                cols = slice(h * rows, (h + 1) * rows)
                inv = 1.0 / l_cur[u:u + 1, cols]
                out = (acc[u, :, cols] * inv).astype(BF16)
                col = slice((j * heads_per + h) * DH, (j * heads_per + h + 1) * DH)
                att_n[r, :, col] = out.T
                delta = jnp.sum(
                    out.astype(F32) * gT[u, :, cols].astype(F32), axis=0, keepdims=True
                )
                aux[0, u:u + 1, cols] = inv * weight
                aux[1, u:u + 1, cols] = delta
                dqa[u, :, cols] = jnp.zeros((DH, rows), F32)

    att_own = pltpu.make_async_copy(att_n.at[0], att_hbm.at[0, 0, :, cq], sem_ol.at[0])
    att_twin = to(att_n.at[1], att_hbm.at[0, 0, :, cq], sem_os.at[0], sem_or.at[0], twin)
    att_own.start()
    att_twin.start()

    def backward(k, v, kt, u, block, tmp):
        scaled = []
        for h in range(heads_per):
            cols = slice(h * rows, (h + 1) * rows)
            m_fin = m_cur[u:u + 1, cols]
            factor = jnp.exp2((m_st[block, u:u + 1, cols] - m_fin) * scale2) * aux[0, u:u + 1, cols]
            g = (gT[u, :, cols].astype(F32) * factor).astype(BF16)
            scaled.append(g)
            d = nn(v, g) - factor * aux[1, u:u + 1, cols]
            low = (e_st[block, u, :, cols].astype(F32) * d).astype(BF16)
            ds[tmp, :, cols] = low
            dqa[u, :, cols] = dqa[u, :, cols] + nn(kt, low)
        g_all = jnp.concatenate(scaled, axis=1)
        return nt(qT[u], ds[tmp]) * inv_root, nt(g_all, e_st[block, u])

    names = ("m1", "m6", "m3", "m2", "m7", "m5", "m4")
    route = {
        "m1": (down, down), "m6": (up, up), "m3": (down, up), "m2": (z_to, z_to),
        "m7": (z_to, z_to), "m5": (up, up), "m4": (down, down),
    }
    msg = {}
    for n, name in enumerate(names):
        for kv in range(2):
            msg[name, kv] = to(
                snd.at[n, kv], rcv.at[n, kv], sem_ms.at[n, kv], sem_mr.at[n, kv], route[name][kv]
            )

    needs = {
        0: ((), ()), 1: ((), ()), 2: ((), ()), 3: (("m1",), ("m1",)), 4: (("m6",), ("m6",)),
        5: ((), ("m3",)), 6: (("m2", "m3"), ("m2",)),
    }

    @pl.loop(0, n_blocks)
    def backward_step(step):
        block = n_blocks - 1 - step
        for j in range(2):
            heads = slice(j * DH, (j + 1) * DH)
            k = kvn[block, 0, :, heads]
            v = kvn[block, 1, :, heads]
            kt = k.T
            first = backward(k, v, kt, j, block, 2 * j)
            second = backward(k, v, kt, 2 + j, block, 2 * j + 1)
            own_part[0, heads, :] = first[0] + second[0]
            own_part[1, heads, :] = first[1] + second[1]

        for n, name in enumerate(names):
            @pl.when(step == n)
            def _():
                for kv in range(2):
                    total = own_part[kv]
                    for other in needs[n][kv]:
                        msg[other, kv].wait_recv()
                        total = total + rcv[names.index(other), kv].astype(F32)
                    snd[n, kv] = total.astype(BF16)
                    msg[name, kv].start()

    for r in range(2):
        for j in range(2):
            heads = slice(j * DH, (j + 1) * DH)
            k = rkn[r, :, heads]
            v = rvn[r, :, heads]
            grad_k, grad_v = backward(k, v, k.T, 2 * r + j, n_blocks, j)
            rg_n[r, 0, :, heads] = grad_k.astype(BF16).T
            rg_n[r, 1, :, heads] = grad_v.astype(BF16).T
    outs_own = [
        pltpu.make_async_copy(rg_n.at[0, 0], drk_hbm.at[0, 0, :, ck], sem_ol.at[1]),
        pltpu.make_async_copy(rg_n.at[0, 1], drv_hbm.at[0, 0, :, ck], sem_ol.at[2]),
        pltpu.make_async_copy(dq_n.at[0], dq_hbm.at[0, 0, :, cq], sem_ol.at[3]),
    ]
    outs_twin = [
        to(rg_n.at[1, 0], drk_hbm.at[0, 0, :, ck], sem_os.at[1], sem_or.at[1], twin),
        to(rg_n.at[1, 1], drv_hbm.at[0, 0, :, ck], sem_os.at[2], sem_or.at[2], twin),
        to(dq_n.at[1], dq_hbm.at[0, 0, :, cq], sem_os.at[3], sem_or.at[3], twin),
    ]
    for cp in outs_own[:2] + outs_twin[:2]:
        cp.start()
    for r in (1, 0):
        for j in range(2):
            for h in range(heads_per):
                col = slice((j * heads_per + h) * DH, (j * heads_per + h + 1) * DH)
                grad = dqa[2 * r + j, :, h * rows:(h + 1) * rows] * inv_root
                dq_n[r, :, col] = grad.astype(BF16).T
        (outs_twin if r else outs_own)[2].start()

    for kv, out in enumerate((dpk_hbm, dpv_hbm)):
        total = own_part[kv]
        for name in ("m5", "m7", "m4"):
            msg[name, kv].wait_recv()
            total = total + rcv[names.index(name), kv].astype(F32)
        pg_n[kv] = total.astype(BF16).T
        twin_rows = pl.ds(pl.multiple_of((1 - c) * piece, piece), piece)
        outs_own.append(
            pltpu.make_async_copy(pg_n.at[kv, my_rows, :], out.at[0, :, ck], sem_ol.at[4 + kv])
        )
        outs_twin.append(
            to(
                pg_n.at[kv, twin_rows, :], out.at[0, :, ck],
                sem_os.at[4 + kv], sem_or.at[4 + kv], twin,
            )
        )
        outs_twin[-1].start()
        outs_own[-1].start()

    for cp in [att_own] + outs_own:
        cp.wait()
    for cp in [att_twin] + outs_twin:
        cp.wait()
    for cp in pair + stats + glens + list(ag.values()) + list(msg.values()):
        cp.wait_send()


def on_device(n_grp, queries, resp_keys, resp_values, prompt_keys, prompt_values, out_grad,
              lengths, rewards):
    rows = queries.shape[2]
    half_q = queries.shape[3] // 2
    half_k = resp_keys.shape[3] // 2
    heads_per = half_q // half_k
    piece = prompt_keys.shape[1]
    blk = 2 * piece
    width = heads_per * rows
    anywhere = pl.BlockSpec(memory_space=pl.ANY)
    scalar = pl.BlockSpec(memory_space=pltpu.SMEM)
    dma = pltpu.SemaphoreType.DMA
    vmem = pltpu.VMEM
    scratch = [
        vmem((2, rows, half_q), BF16), vmem((2, rows, half_q), BF16),
        vmem((2, rows, half_k), BF16), vmem((2, rows, half_k), BF16),
        vmem((8, 2, blk, half_k), BF16),
        vmem((4, DH, width), BF16), vmem((4, DH, width), BF16),
        vmem((9, 4, blk, width), BF16),
        vmem((9, 8, width), F32), vmem((8, width), F32), vmem((8, width), F32),
        vmem((4, DH, width), F32), vmem((4, DH, width), F32),
        vmem((4, blk, width), BF16), vmem((2, 8, width), F32),
        vmem((8, 128), jnp.int32), vmem((16, 8, 128), jnp.int32),
        vmem((8, 128), jnp.int32), vmem((n_grp, 8, 128), jnp.int32),
        vmem((7, 2, half_k, blk), BF16), vmem((7, 2, half_k, blk), BF16),
        vmem((2, half_k, blk), F32),
        vmem((2, rows, half_q), BF16), vmem((2, rows, half_q), BF16),
        vmem((2, 2, rows, half_k), BF16), vmem((2, blk, half_k), BF16),
        dma((6,)), dma((6,)), dma((6,)), dma((8, 2)), dma((8, 2)),
        dma((16,)), dma((16,)), dma((n_grp,)), dma((n_grp,)),
        dma((7, 2)), dma((7, 2)), dma((6,)), dma((6,)), dma((6,)),
    ]
    like = lambda a: jax.ShapeDtypeStruct(a.shape, a.dtype)
    return pl.pallas_call(
        lambda *refs: kernel(n_grp, heads_per, *refs),
        out_shape=(
            like(queries), like(queries), like(resp_keys), like(resp_values),
            like(prompt_keys), like(prompt_values),
        ),
        in_specs=[anywhere] * 6 + [scalar] * 2,
        out_specs=(anywhere,) * 6,
        scratch_shapes=scratch,
        compiler_params=pltpu.CompilerParams(
            collective_id=0, has_side_effects=True, vmem_limit_bytes=60 * 2**20
        ),
        name="grpo_attention",
    )(queries, resp_keys, resp_values, prompt_keys, prompt_values, out_grad, lengths, rewards)


def solution(mesh):
    n_grp = mesh.shape["grp"]
    wide = P("grp", "resp", None, None)
    tall = P("grp", "resp", None)
    return jax.shard_map(
        lambda *arrays: on_device(n_grp, *arrays),
        mesh=mesh,
        in_specs=(wide, wide, wide, tall, tall, wide, P("grp", "resp"), P("grp", "resp")),
        out_specs=(wide, wide, wide, wide, tall, tall),
        check_vma=False,
    )
```

```python
import math

import jax
import jax.numpy as jnp
from jax import lax
from jax.experimental import pallas as pl
from jax.experimental.pallas import tpu as pltpu
from jax.sharding import PartitionSpec as P

DH = 128
F32 = jnp.float32
BF16 = jnp.bfloat16
MESH = pl.DeviceIdType.MESH

SLOTS = ((0, 0), (0, 3), (0, 1), (1, 0), (1, 3), (0, 2), (1, 1), (1, 2))
OWN, YM, YP, ZZ, ZYM, YY, ZYP, ZYY = range(8)


def nn(a, b):
    return jnp.dot(a, b, preferred_element_type=F32)


def nt(a, b):
    return lax.dot_general(a, b, (((1,), (1,)), ((), ())), preferred_element_type=F32)


def kernel(
    n_grp, heads_per, q_hbm, rk_hbm, rv_hbm, pk_hbm, pv_hbm, og_hbm, len_ref, rew_ref,
    att_hbm, dq_hbm, drk_hbm, drv_hbm, dpk_hbm, dpv_hbm,
    qn, gn, rkn, rvn, kvn, qT, q2, gT, e_st, m_st, m_cur, l_cur, acc, dqa, aux,
    stat_out, stat_in, glen_out, glen_in, snd, rcv, own_part, att_n, dq_n, rg_n, pg_n,
    sem_l, sem_ps, sem_pr, sem_as, sem_ar, sem_ss, sem_sr, sem_gs, sem_gr,
    sem_ms, sem_mr, sem_ol, sem_os, sem_or,
):
    rows = qn.shape[1]
    half_q = qn.shape[2]
    half_k = rkn.shape[2]
    piece = pk_hbm.shape[1]
    blk = 2 * piece
    width = heads_per * rows
    inv_root = DH ** (-0.5)
    scale2 = inv_root * math.log2(math.e)
    me = lax.axis_index("resp")
    grp = lax.axis_index("grp")
    z = me // 8
    y = (me // 2) % 4
    c = me % 2

    def at(dz, dy, dc):
        return {"resp": ((z + dz) % 2) * 8 + ((y + dy) % 4) * 2 + (c + dc) % 2}

    def to(src, dst, s_sem, r_sem, target):
        return pltpu.make_async_remote_copy(
            src_ref=src, dst_ref=dst, send_sem=s_sem, recv_sem=r_sem,
            device_id=target, device_id_type=MESH,
        )

    cq = pl.ds(pl.multiple_of(c * half_q, half_q), half_q)
    oq = pl.ds(pl.multiple_of((1 - c) * half_q, half_q), half_q)
    ck = pl.ds(pl.multiple_of(c * half_k, half_k), half_k)
    ok = pl.ds(pl.multiple_of((1 - c) * half_k, half_k), half_k)
    my_rows = pl.ds(pl.multiple_of(c * piece, piece), piece)

    local = [
        pltpu.make_async_copy(pk_hbm.at[0, :, ck], kvn.at[OWN, 0, my_rows, :], sem_l.at[0]),
        pltpu.make_async_copy(pv_hbm.at[0, :, ck], kvn.at[OWN, 1, my_rows, :], sem_l.at[1]),
        pltpu.make_async_copy(q_hbm.at[0, 0, :, cq], qn.at[0], sem_l.at[2]),
        pltpu.make_async_copy(rk_hbm.at[0, 0, :, ck], rkn.at[0], sem_l.at[3]),
        pltpu.make_async_copy(rv_hbm.at[0, 0, :, ck], rvn.at[0], sem_l.at[4]),
        pltpu.make_async_copy(og_hbm.at[0, 0, :, cq], gn.at[0], sem_l.at[5]),
    ]
    for cp in local:
        cp.start()

    row_id = lax.broadcasted_iota(jnp.int32, (8, 128), 0)
    stat_out[...] = jnp.where(row_id == 0, len_ref[0, 0], rew_ref[0, 0])

    others = [
        (dz, dy, dc) for dz in range(2) for dy in range(4) for dc in range(2) if dz or dy or dc
    ]
    barrier = pltpu.get_barrier_semaphore()
    for dz, dy, dc in others:
        pl.semaphore_signal(barrier, inc=1, device_id=at(dz, dy, dc), device_id_type=MESH)
    for dg in range(1, n_grp):
        pl.semaphore_signal(
            barrier, inc=1, device_id={"grp": (grp + dg) % n_grp}, device_id_type=MESH
        )
    pl.semaphore_wait(barrier, len(others) + n_grp - 1)

    twin = at(0, 0, 1)
    pair = [
        to(pk_hbm.at[0, :, ok], kvn.at[OWN, 0, my_rows, :], sem_ps.at[0], sem_pr.at[0], twin),
        to(pv_hbm.at[0, :, ok], kvn.at[OWN, 1, my_rows, :], sem_ps.at[1], sem_pr.at[1], twin),
        to(q_hbm.at[0, 0, :, oq], qn.at[1], sem_ps.at[2], sem_pr.at[2], twin),
        to(rk_hbm.at[0, 0, :, ok], rkn.at[1], sem_ps.at[3], sem_pr.at[3], twin),
        to(rv_hbm.at[0, 0, :, ok], rvn.at[1], sem_ps.at[4], sem_pr.at[4], twin),
        to(og_hbm.at[0, 0, :, oq], gn.at[1], sem_ps.at[5], sem_pr.at[5], twin),
    ]
    for cp in pair:
        cp.start()

    z_to, up, down = at(1, 0, 0), at(0, 1, 0), at(0, 3, 0)
    ag_plan = (
        (OWN, ZZ, 0, z_to), (OWN, YM, 0, up), (OWN, YP, 0, down),
        (OWN, ZZ, 1, z_to), (OWN, YM, 1, up), (OWN, YP, 1, down),
        (YM, YY, 0, up), (YM, ZYM, 0, z_to), (YM, ZYM, 1, z_to),
        (YP, YY, 1, down), (ZZ, ZYP, 0, down), (ZZ, ZYP, 1, down),
        (ZYM, ZYY, 0, up), (ZYM, ZYY, 1, up),
    )
    ag = {}
    for src, dst, kv, target in ag_plan:
        ag[dst, kv] = to(
            kvn.at[src, kv], kvn.at[dst, kv], sem_as.at[dst, kv], sem_ar.at[dst, kv], target
        )

    for i in (0, 1):
        local[i].wait()
        pair[i].wait_recv()
    for kv in (0, 1):
        for dst in (ZZ, YM, YP):
            ag[dst, kv].start()

    stats = []
    for n, (dz, dy, dc) in enumerate(others):
        slot = ((-dz) % 2) * 8 + ((-dy) % 4) * 2 + dc
        stats.append(
            to(stat_out, stat_in.at[slot], sem_ss.at[slot], sem_sr.at[slot], at(dz, dy, dc))
        )
        stats[-1].start()

    def turn(src, dst, r):
        for j in range(2):
            for h in range(heads_per):
                dst[2 * r + j, :, h * rows:(h + 1) * rows] = src[
                    r, :, (j * heads_per + h) * DH:(j * heads_per + h + 1) * DH
                ].T

    def split_queries(r):
        for u in (2 * r, 2 * r + 1):
            for h in range(heads_per):
                cols = slice(h * rows, (h + 1) * rows)
                full = qT[u, :, cols].astype(F32) * scale2
                high = full.astype(BF16)
                q2[u, 0:DH, cols] = high
                q2[u, DH:2 * DH, cols] = (full - high.astype(F32)).astype(BF16)

    ones = jnp.ones((16, blk), BF16)

    def forward(units, keys, values, block, first):
        keys = {u: jnp.concatenate([k, k], axis=1) for u, k in keys.items()}
        values = {u: jnp.concatenate([v.T, ones], axis=0) for u, v in values.items()}
        todo = [(u, slice(h * rows, (h + 1) * rows)) for u in units for h in range(heads_per)]
        logits, lows = {}, {}

        def start(i):
            u, cols = todo[i]
            logits[i] = nn(keys[u], q2[u, :, cols])

        def finish(i):
            u, cols = todo[i]
            low, alpha = lows.pop(i)
            part = nn(values[u], low)
            if first:
                l_cur[u:u + 1, cols] = part[DH:DH + 1]
                acc[u, :, cols] = part[0:DH]
            else:
                l_cur[u:u + 1, cols] = l_cur[u:u + 1, cols] * alpha + part[DH:DH + 1]
                acc[u, :, cols] = acc[u, :, cols] * alpha + part[0:DH]

        for i in range(3):
            start(i)
        for i, (u, cols) in enumerate(todo):
            if i + 3 < len(todo):
                start(i + 3)
            s = logits.pop(i)
            if first:
                seen = lax.broadcasted_iota(jnp.int32, s.shape, 0) <= (
                    lax.broadcasted_iota(jnp.int32, s.shape, 1)
                )
                s = jnp.where(seen, s, -jnp.inf)
                m_new = jnp.max(s, axis=0, keepdims=True)
                alpha = None
            else:
                m_old = m_cur[u:u + 1, cols]
                m_new = jnp.maximum(m_old, jnp.max(s, axis=0, keepdims=True))
                alpha = jnp.exp2(m_old - m_new)
            low = jnp.exp2(s - m_new).astype(BF16)
            e_st[block, u, :, cols] = low
            m_cur[u:u + 1, cols] = m_new
            m_st[block, u:u + 1, cols] = m_new
            lows[i] = (low, alpha)
            if i >= 2:
                finish(i - 2)
        for i in sorted(lows):
            finish(i)

    n_blocks = 8
    for r in range(2):
        if r == 0:
            for i in (2, 3, 4):
                local[i].wait()
        else:
            for i in (2, 3, 4):
                pair[i].wait_recv()
        turn(qn, qT, r)
        split_queries(r)
        units = (2 * r, 2 * r + 1)
        forward(
            units,
            {u: rkn[r, :, (u % 2) * DH:(u % 2 + 1) * DH] for u in units},
            {u: rvn[r, :, (u % 2) * DH:(u % 2 + 1) * DH] for u in units},
            n_blocks, True,
        )
    local[5].wait()
    pair[5].wait_recv()
    for r in range(2):
        turn(gn, gT, r)

    for cp in stats:
        cp.wait_recv()
    sum_one = stat_out[1:2, :]
    sum_two = sum_one * sum_one
    live = stat_out[0:1, :]
    for slot in range(1, 16):
        one = stat_in[slot, 1:2, :]
        sum_one = sum_one + one
        sum_two = sum_two + one * one
        live = live + stat_in[slot, 0:1, :]
    glen_out[...] = jnp.broadcast_to(live, (8, 128))
    glens = []
    for dg in range(1, n_grp):
        glens.append(
            to(
                glen_out, glen_in.at[n_grp - dg], sem_gs.at[n_grp - dg], sem_gr.at[n_grp - dg],
                {"grp": (grp + dg) % n_grp},
            )
        )
        glens[-1].start()

    def pass_on(waits, starts):
        for key in waits:
            ag[key].wait_recv()
        for key in starts:
            ag[key].start()

    @pl.loop(0, n_blocks)
    def forward_step(step):
        @pl.when(step == 1)
        def _():
            pass_on([(YM, 0)], [(YY, 0), (ZYM, 0)])
            pass_on([(ZZ, 0)], [(ZYP, 0)])
            pass_on([(YM, 1)], [(ZYM, 1)])
            pass_on([(YP, 0), (YP, 1)], [(YY, 1)])
            pass_on([(ZZ, 1)], [(ZYP, 1)])

        @pl.when(step == 4)
        def _():
            pass_on([(ZYM, 0)], [(ZYY, 0)])
            pass_on([(ZYM, 1)], [(ZYY, 1)])

        @pl.when(step == 5)
        def _():
            pass_on([(YY, 0), (YY, 1)], [])

        @pl.when(step == 6)
        def _():
            pass_on([(ZYP, 0), (ZYP, 1)], [])

        @pl.when(step == 7)
        def _():
            pass_on([(ZYY, 0), (ZYY, 1)], [])

        order = (0, 2, 1, 3)
        forward(
            order,
            {u: kvn[step, 0, :, (u % 2) * DH:(u % 2 + 1) * DH] for u in order},
            {u: kvn[step, 1, :, (u % 2) * DH:(u % 2 + 1) * DH] for u in order},
            step, False,
        )

    for cp in glens:
        cp.wait_recv()
    for slot in range(1, n_grp):
        live = live + glen_in[slot, 0:1, :]
    n_resp = 16
    sum_one = sum_one.astype(F32)
    sum_two = sum_two.astype(F32)
    mean = sum_one / n_resp
    variance = (n_resp * sum_two - sum_one * sum_one) / (n_resp * n_resp)
    spread = jnp.maximum(jnp.sqrt(variance), 1.0)
    norm = (n_grp * n_resp * rows) / live.astype(F32)
    for r in range(2):
        length = stat_out[0:1, :] if r == 0 else stat_in[1, 0:1, :]
        reward = stat_out[1:2, :] if r == 0 else stat_in[1, 1:2, :]
        strength = (reward.astype(F32) - mean) / spread * norm
        weight = jnp.concatenate(
            [
                jnp.where(
                    lax.broadcasted_iota(jnp.int32, (1, 128), 1) + start < length, strength, 0.0
                )
                for start in range(0, rows, 128)
            ],
            axis=1,
        )
        for j in range(2):
            u = 2 * r + j
            for h in range(heads_per):
                cols = slice(h * rows, (h + 1) * rows)
                inv = 1.0 / l_cur[u:u + 1, cols]
                out = (acc[u, :, cols] * inv).astype(BF16)
                col = slice((j * heads_per + h) * DH, (j * heads_per + h + 1) * DH)
                att_n[r, :, col] = out.T
                delta = jnp.sum(
                    out.astype(F32) * gT[u, :, cols].astype(F32), axis=0, keepdims=True
                )
                aux[0, u:u + 1, cols] = inv * weight
                aux[1, u:u + 1, cols] = delta
                dqa[u, :, cols] = jnp.zeros((DH, rows), F32)

    att_own = pltpu.make_async_copy(att_n.at[0], att_hbm.at[0, 0, :, cq], sem_ol.at[0])
    att_twin = to(att_n.at[1], att_hbm.at[0, 0, :, cq], sem_os.at[0], sem_or.at[0], twin)
    att_own.start()
    att_twin.start()

    def backward(units, keys, values, block, place):
        flat = {u: k.T for u, k in keys.items()}
        todo = [(u, h, slice(h * rows, (h + 1) * rows)) for u in units for h in range(heads_per)]
        scaled, shift, dots, lows, sums = {}, {}, {}, {}, {}

        def start(i):
            u, h, cols = todo[i]
            factor = jnp.exp2(m_st[block, u:u + 1, cols] - m_cur[u:u + 1, cols])
            factor = factor * aux[0, u:u + 1, cols]
            scaled[i] = (gT[u, :, cols].astype(F32) * factor).astype(BF16)
            shift[i] = factor * aux[1, u:u + 1, cols]
            dots[i] = nn(values[u], scaled[i])

        def add(key, term):
            sums[key] = sums[key] + term if key in sums else term

        def finish(i):
            u, h, cols = todo[i]
            low = lows.pop(i)
            col = (u % 2) * heads_per + h
            dqa[u, :, cols] = dqa[u, :, cols] + nn(flat[u], low)
            add((place(u), 0), nn(low, qn[u // 2, :, col * DH:(col + 1) * DH]))
            add((place(u), 1), nt(scaled.pop(i), e_st[block, u, :, cols]))

        for i in range(2):
            start(i)
        for i, (u, h, cols) in enumerate(todo):
            if i + 2 < len(todo):
                start(i + 2)
            d = dots.pop(i) - shift.pop(i)
            lows[i] = (e_st[block, u, :, cols].astype(F32) * d).astype(BF16)
            if i >= 1:
                finish(i - 1)
        finish(len(todo) - 1)
        return {
            key: term.T * inv_root if key[1] == 0 else term for key, term in sums.items()
        }

    names = ("m1", "m6", "m3", "m2", "m7", "m5", "m4")
    route = {
        "m1": (down, down), "m6": (up, up), "m3": (down, up), "m2": (z_to, z_to),
        "m7": (z_to, z_to), "m5": (up, up), "m4": (down, down),
    }
    msg = {}
    for n, name in enumerate(names):
        for kv in range(2):
            msg[name, kv] = to(
                snd.at[n, kv], rcv.at[n, kv], sem_ms.at[n, kv], sem_mr.at[n, kv], route[name][kv]
            )

    needs = {
        0: ((), ()), 1: ((), ()), 2: ((), ()), 3: (("m1",), ("m1",)), 4: (("m6",), ("m6",)),
        5: ((), ("m3",)), 6: (("m2", "m3"), ("m2",)),
    }

    @pl.loop(0, n_blocks)
    def backward_step(step):
        block = n_blocks - 1 - step
        order = (0, 2, 1, 3)
        sums = backward(
            order,
            {u: kvn[block, 0, :, (u % 2) * DH:(u % 2 + 1) * DH] for u in order},
            {u: kvn[block, 1, :, (u % 2) * DH:(u % 2 + 1) * DH] for u in order},
            block, lambda u: u % 2,
        )
        for (j, kv), term in sums.items():
            own_part[kv, j * DH:(j + 1) * DH, :] = term

        for n, name in enumerate(names):
            @pl.when(step == n)
            def _():
                for kv in range(2):
                    total = own_part[kv]
                    for other in needs[n][kv]:
                        msg[other, kv].wait_recv()
                        total = total + rcv[names.index(other), kv].astype(F32)
                    snd[n, kv] = total.astype(BF16)
                    msg[name, kv].start()

    units = (0, 1, 2, 3)
    sums = backward(
        units,
        {u: rkn[u // 2, :, (u % 2) * DH:(u % 2 + 1) * DH] for u in units},
        {u: rvn[u // 2, :, (u % 2) * DH:(u % 2 + 1) * DH] for u in units},
        n_blocks, lambda u: u,
    )
    for (u, kv), term in sums.items():
        rg_n[u // 2, kv, :, (u % 2) * DH:(u % 2 + 1) * DH] = term.astype(BF16).T
    outs_own = [
        pltpu.make_async_copy(rg_n.at[0, 0], drk_hbm.at[0, 0, :, ck], sem_ol.at[1]),
        pltpu.make_async_copy(rg_n.at[0, 1], drv_hbm.at[0, 0, :, ck], sem_ol.at[2]),
        pltpu.make_async_copy(dq_n.at[0], dq_hbm.at[0, 0, :, cq], sem_ol.at[3]),
    ]
    outs_twin = [
        to(rg_n.at[1, 0], drk_hbm.at[0, 0, :, ck], sem_os.at[1], sem_or.at[1], twin),
        to(rg_n.at[1, 1], drv_hbm.at[0, 0, :, ck], sem_os.at[2], sem_or.at[2], twin),
        to(dq_n.at[1], dq_hbm.at[0, 0, :, cq], sem_os.at[3], sem_or.at[3], twin),
    ]
    for cp in outs_own[:2] + outs_twin[:2]:
        cp.start()
    for r in (1, 0):
        for j in range(2):
            for h in range(heads_per):
                col = slice((j * heads_per + h) * DH, (j * heads_per + h + 1) * DH)
                grad = dqa[2 * r + j, :, h * rows:(h + 1) * rows] * inv_root
                dq_n[r, :, col] = grad.astype(BF16).T
        (outs_twin if r else outs_own)[2].start()

    for kv, out in enumerate((dpk_hbm, dpv_hbm)):
        total = own_part[kv]
        for name in ("m5", "m7", "m4"):
            msg[name, kv].wait_recv()
            total = total + rcv[names.index(name), kv].astype(F32)
        pg_n[kv] = total.astype(BF16).T
        twin_rows = pl.ds(pl.multiple_of((1 - c) * piece, piece), piece)
        outs_own.append(
            pltpu.make_async_copy(pg_n.at[kv, my_rows, :], out.at[0, :, ck], sem_ol.at[4 + kv])
        )
        outs_twin.append(
            to(
                pg_n.at[kv, twin_rows, :], out.at[0, :, ck],
                sem_os.at[4 + kv], sem_or.at[4 + kv], twin,
            )
        )
        outs_twin[-1].start()
        outs_own[-1].start()

    for cp in [att_own] + outs_own:
        cp.wait()
    for cp in [att_twin] + outs_twin:
        cp.wait()
    for cp in pair + stats + glens + list(ag.values()) + list(msg.values()):
        cp.wait_send()


def on_device(n_grp, queries, resp_keys, resp_values, prompt_keys, prompt_values, out_grad,
              lengths, rewards):
    rows = queries.shape[2]
    half_q = queries.shape[3] // 2
    half_k = resp_keys.shape[3] // 2
    heads_per = half_q // half_k
    piece = prompt_keys.shape[1]
    blk = 2 * piece
    width = heads_per * rows
    anywhere = pl.BlockSpec(memory_space=pl.ANY)
    scalar = pl.BlockSpec(memory_space=pltpu.SMEM)
    dma = pltpu.SemaphoreType.DMA
    vmem = pltpu.VMEM
    scratch = [
        vmem((2, rows, half_q), BF16), vmem((2, rows, half_q), BF16),
        vmem((2, rows, half_k), BF16), vmem((2, rows, half_k), BF16),
        vmem((8, 2, blk, half_k), BF16),
        vmem((4, DH, width), BF16), vmem((4, 2 * DH, width), BF16), vmem((4, DH, width), BF16),
        vmem((9, 4, blk, width), BF16),
        vmem((9, 8, width), F32), vmem((8, width), F32), vmem((8, width), F32),
        vmem((4, DH, width), F32), vmem((4, DH, width), F32),
        vmem((2, 8, width), F32),
        vmem((8, 128), jnp.int32), vmem((16, 8, 128), jnp.int32),
        vmem((8, 128), jnp.int32), vmem((n_grp, 8, 128), jnp.int32),
        vmem((7, 2, half_k, blk), BF16), vmem((7, 2, half_k, blk), BF16),
        vmem((2, half_k, blk), F32),
        vmem((2, rows, half_q), BF16), vmem((2, rows, half_q), BF16),
        vmem((2, 2, rows, half_k), BF16), vmem((2, blk, half_k), BF16),
        dma((6,)), dma((6,)), dma((6,)), dma((8, 2)), dma((8, 2)),
        dma((16,)), dma((16,)), dma((n_grp,)), dma((n_grp,)),
        dma((7, 2)), dma((7, 2)), dma((6,)), dma((6,)), dma((6,)),
    ]
    like = lambda a: jax.ShapeDtypeStruct(a.shape, a.dtype)
    return pl.pallas_call(
        lambda *refs: kernel(n_grp, heads_per, *refs),
        out_shape=(
            like(queries), like(queries), like(resp_keys), like(resp_values),
            like(prompt_keys), like(prompt_values),
        ),
        in_specs=[anywhere] * 6 + [scalar] * 2,
        out_specs=(anywhere,) * 6,
        scratch_shapes=scratch,
        compiler_params=pltpu.CompilerParams(
            collective_id=0, has_side_effects=True, vmem_limit_bytes=60 * 2**20
        ),
        name="grpo_attention",
    )(queries, resp_keys, resp_values, prompt_keys, prompt_values, out_grad, lengths, rewards)


def solution(mesh):
    n_grp = mesh.shape["grp"]
    wide = P("grp", "resp", None, None)
    tall = P("grp", "resp", None)
    return jax.shard_map(
        lambda *arrays: on_device(n_grp, *arrays),
        mesh=mesh,
        in_specs=(wide, wide, wide, tall, tall, wide, P("grp", "resp"), P("grp", "resp")),
        out_specs=(wide, wide, wide, wide, tall, tall),
        check_vma=False,
    )
```

```python
import math

import jax
import jax.numpy as jnp
from jax import lax
from jax.experimental import pallas as pl
from jax.experimental.pallas import tpu as pltpu
from jax.sharding import PartitionSpec as P

DH = 128
F32 = jnp.float32
BF16 = jnp.bfloat16
MESH = pl.DeviceIdType.MESH

SLOTS = ((0, 0), (0, 3), (0, 1), (1, 0), (1, 3), (0, 2), (1, 1), (1, 2))
OWN, YM, YP, ZZ, ZYM, YY, ZYP, ZYY = range(8)


def nn(a, b):
    return jnp.dot(a, b, preferred_element_type=F32)


def nt(a, b):
    return lax.dot_general(a, b, (((1,), (1,)), ((), ())), preferred_element_type=F32)


def kernel(
    n_grp, heads_per, q_hbm, rk_hbm, rv_hbm, pk_hbm, pv_hbm, og_hbm, len_hbm, rew_hbm,
    att_hbm, dq_hbm, drk_hbm, drv_hbm, dpk_hbm, dpv_hbm,
    len_ref, rew_ref, qn, gn, rkn, rvn, kvn, qT, q2, gT, e_st, m_st, m_cur, l_cur, acc, dqa, aux,
    stat_out, stat_in, snd, rcv, own_part, att_n, dq_n, rg_n, pg_n,
    sem_l, sem_ps, sem_pr, sem_as, sem_ar, sem_bs, sem_br, sem_ss, sem_sr,
    sem_ms, sem_mr, sem_ol, sem_os, sem_or,
):
    rows = qn.shape[1]
    half_q = qn.shape[2]
    half_k = rkn.shape[2]
    piece = pk_hbm.shape[1]
    blk = 2 * piece
    width = heads_per * rows
    inv_root = DH ** (-0.5)
    scale2 = inv_root * math.log2(math.e)
    me = lax.axis_index("resp")
    grp = lax.axis_index("grp")
    z = me // 8
    y = (me // 2) % 4
    c = me % 2

    def at(dz, dy, dc):
        return {"resp": ((z + dz) % 2) * 8 + ((y + dy) % 4) * 2 + (c + dc) % 2}

    def to(src, dst, s_sem, r_sem, target):
        return pltpu.make_async_remote_copy(
            src_ref=src, dst_ref=dst, send_sem=s_sem, recv_sem=r_sem,
            device_id=target, device_id_type=MESH,
        )

    cq = pl.ds(pl.multiple_of(c * half_q, half_q), half_q)
    oq = pl.ds(pl.multiple_of((1 - c) * half_q, half_q), half_q)
    ck = pl.ds(pl.multiple_of(c * half_k, half_k), half_k)
    ok = pl.ds(pl.multiple_of((1 - c) * half_k, half_k), half_k)
    my_rows = pl.ds(pl.multiple_of(c * piece, piece), piece)

    local = [
        pltpu.make_async_copy(pk_hbm.at[0, :, ck], kvn.at[OWN, 0, my_rows, :], sem_l.at[0]),
        pltpu.make_async_copy(pv_hbm.at[0, :, ck], kvn.at[OWN, 1, my_rows, :], sem_l.at[1]),
        pltpu.make_async_copy(q_hbm.at[0, 0, :, cq], qn.at[0], sem_l.at[2]),
        pltpu.make_async_copy(rk_hbm.at[0, 0, :, ck], rkn.at[0], sem_l.at[3]),
        pltpu.make_async_copy(rv_hbm.at[0, 0, :, ck], rvn.at[0], sem_l.at[4]),
        pltpu.make_async_copy(og_hbm.at[0, 0, :, cq], gn.at[0], sem_l.at[5]),
        pltpu.make_async_copy(len_hbm, len_ref, sem_l.at[6]),
        pltpu.make_async_copy(rew_hbm, rew_ref, sem_l.at[7]),
    ]
    for cp in local:
        cp.start()

    twin = at(0, 0, 1)
    z_to, up, down = at(1, 0, 0), at(0, 1, 0), at(0, 3, 0)
    ring = min(4, n_grp)
    base = (grp // ring) * ring
    x_up = {"grp": base + (grp - base + 1) % ring}
    x_down = {"grp": base + (grp - base + ring - 1) % ring}
    across = {"grp": (grp + ring) % n_grp}
    friends = [twin, z_to, up, down]
    if ring == 4:
        friends += [x_up, x_down]
    if n_grp > ring:
        friends.append(across)
    barrier = pltpu.get_barrier_semaphore()
    for friend in friends:
        pl.semaphore_signal(barrier, inc=1, device_id=friend, device_id_type=MESH)

    def turn(src, dst, r):
        for j in range(2):
            for h in range(heads_per):
                dst[2 * r + j, :, h * rows:(h + 1) * rows] = src[
                    r, :, (j * heads_per + h) * DH:(j * heads_per + h + 1) * DH
                ].T

    def split_queries(r):
        for u in (2 * r, 2 * r + 1):
            for h in range(heads_per):
                cols = slice(h * rows, (h + 1) * rows)
                full = qT[u, :, cols].astype(F32) * scale2
                high = full.astype(BF16)
                q2[u, 0:DH, cols] = high
                q2[u, DH:2 * DH, cols] = (full - high.astype(F32)).astype(BF16)

    ones = jnp.ones((16, blk), BF16)

    def forward(units, keys, values, block, first):
        keys = {u: jnp.concatenate([k, k], axis=1) for u, k in keys.items()}
        values = {u: jnp.concatenate([v.T, ones], axis=0) for u, v in values.items()}
        todo = [(u, slice(h * rows, (h + 1) * rows)) for u in units for h in range(heads_per)]
        logits, lows = {}, {}

        def start(i):
            u, cols = todo[i]
            logits[i] = nn(keys[u], q2[u, :, cols])

        def finish(i):
            u, cols = todo[i]
            low, alpha = lows.pop(i)
            part = nn(values[u], low)
            if first:
                l_cur[u:u + 1, cols] = part[DH:DH + 1]
                acc[u, :, cols] = part[0:DH]
            else:
                l_cur[u:u + 1, cols] = l_cur[u:u + 1, cols] * alpha + part[DH:DH + 1]
                acc[u, :, cols] = acc[u, :, cols] * alpha + part[0:DH]

        for i in range(3):
            start(i)
        for i, (u, cols) in enumerate(todo):
            if i + 3 < len(todo):
                start(i + 3)
            s = logits.pop(i)
            if first:
                seen = lax.broadcasted_iota(jnp.int32, s.shape, 0) <= (
                    lax.broadcasted_iota(jnp.int32, s.shape, 1)
                )
                s = jnp.where(seen, s, -jnp.inf)
                m_new = jnp.max(s, axis=0, keepdims=True)
                alpha = None
            else:
                m_old = m_cur[u:u + 1, cols]
                m_new = jnp.maximum(m_old, jnp.max(s, axis=0, keepdims=True))
                alpha = jnp.exp2(m_old - m_new)
            low = jnp.exp2(s - m_new).astype(BF16)
            e_st[block, u, :, cols] = low
            m_cur[u:u + 1, cols] = m_new
            m_st[block, u:u + 1, cols] = m_new
            lows[i] = (low, alpha)
            if i >= 2:
                finish(i - 2)
        for i in sorted(lows):
            finish(i)

    def own_block(r):
        turn(qn, qT, r)
        split_queries(r)
        units = (2 * r, 2 * r + 1)
        forward(
            units,
            {u: rkn[r, :, (u % 2) * DH:(u % 2 + 1) * DH] for u in units},
            {u: rvn[r, :, (u % 2) * DH:(u % 2 + 1) * DH] for u in units},
            n_blocks, True,
        )

    n_blocks = 8
    for i in (2, 3, 4):
        local[i].wait()
    own_block(0)

    pl.semaphore_wait(barrier, len(friends))

    pair = [
        to(pk_hbm.at[0, :, ok], kvn.at[OWN, 0, my_rows, :], sem_ps.at[0], sem_pr.at[0], twin),
        to(pv_hbm.at[0, :, ok], kvn.at[OWN, 1, my_rows, :], sem_ps.at[1], sem_pr.at[1], twin),
        to(q_hbm.at[0, 0, :, oq], qn.at[1], sem_ps.at[2], sem_pr.at[2], twin),
        to(rk_hbm.at[0, 0, :, ok], rkn.at[1], sem_ps.at[3], sem_pr.at[3], twin),
        to(rv_hbm.at[0, 0, :, ok], rvn.at[1], sem_ps.at[4], sem_pr.at[4], twin),
        to(og_hbm.at[0, 0, :, oq], gn.at[1], sem_ps.at[5], sem_pr.at[5], twin),
    ]
    for cp in pair:
        cp.start()

    twin_rows = pl.ds(pl.multiple_of((1 - c) * piece, piece), piece)
    ag = {}
    for kv in (0, 1):
        for dst, target in ((YM, up), (YP, down), (ZZ, z_to)):
            ag[dst, kv] = [
                to(
                    kvn.at[OWN, kv, part, :], kvn.at[dst, kv, part, :],
                    s_sem.at[dst, kv], r_sem.at[dst, kv], target,
                )
                for part, s_sem, r_sem in (
                    (my_rows, sem_as, sem_ar), (twin_rows, sem_bs, sem_br),
                )
            ]
    ag_plan = (
        (YM, YY, 0, up), (YM, ZYM, 0, z_to), (YM, ZYM, 1, z_to),
        (YP, YY, 1, down), (ZZ, ZYP, 0, down), (ZZ, ZYP, 1, down),
        (ZYM, ZYY, 0, up), (ZYM, ZYY, 1, up),
    )
    for src, dst, kv, target in ag_plan:
        ag[dst, kv] = [
            to(kvn.at[src, kv], kvn.at[dst, kv], sem_as.at[dst, kv], sem_ar.at[dst, kv], target)
        ]

    for half in (0, 1):
        for kv in (0, 1):
            if half == 0:
                local[kv].wait()
            else:
                pair[kv].wait_recv()
            for dst in (YM, YP, ZZ):
                ag[dst, kv][half].start()


    hops = [((twin,), False), ((z_to,), False), ((up, down), False), ((up,), True)]
    if ring == 4:
        hops += [((x_up, x_down), False), ((x_up,), True)]
    if n_grp > ring:
        hops.append(((across,), False))

    def hop_copies(n):
        targets, relay = hops[n]
        src = stat_in.at[n - 1, 1] if relay else stat_out.at[n]
        copies = []
        for i, target in enumerate(targets):
            slot = 1 - i if len(targets) == 2 else 0
            copies.append(
                to(src, stat_in.at[n, slot], sem_ss.at[n, slot], sem_sr.at[n, slot], target)
            )
        return copies

    def hop_start(n):
        for cp in hop_copies(n):
            cp.start()

    def hop_end(n):
        for cp in hop_copies(n):
            cp.wait_recv()
        total = stat_out[n]
        for slot in range(len(hops[n][0])):
            total = total + stat_in[n, slot]
        stat_out[n + 1] = total

    local[6].wait()
    local[7].wait()
    row_id = lax.broadcasted_iota(jnp.int32, (8, 128), 0)
    reward_own = rew_ref[0, 0]
    stat_out[0] = jnp.where(
        row_id == 0, len_ref[0, 0], jnp.where(row_id == 1, reward_own, reward_own * reward_own)
    )
    hop_start(0)

    for i in (2, 3, 4):
        pair[i].wait_recv()
    own_block(1)
    local[5].wait()
    pair[5].wait_recv()
    for r in range(2):
        turn(gn, gT, r)
    hop_end(0)
    hop_start(1)

    def pass_on(waits, starts):
        for key in waits:
            for cp in ag[key]:
                cp.wait_recv()
        for key in starts:
            for cp in ag[key]:
                cp.start()

    @pl.loop(0, n_blocks)
    def forward_step(step):
        @pl.when(step == 1)
        def _():
            pass_on([(YM, 0)], [(YY, 0), (ZYM, 0)])
            pass_on([(ZZ, 0)], [(ZYP, 0)])
            pass_on([(YM, 1)], [(ZYM, 1)])
            pass_on([(YP, 0), (YP, 1)], [(YY, 1)])
            pass_on([(ZZ, 1)], [(ZYP, 1)])

        @pl.when(step == 3)
        def _():
            pass_on([(ZYM, 0)], [(ZYY, 0)])

        @pl.when(step == 4)
        def _():
            pass_on([(ZYM, 1)], [(ZYY, 1)])

        @pl.when(step == 5)
        def _():
            pass_on([(YY, 0), (YY, 1)], [])

        @pl.when(step == 6)
        def _():
            pass_on([(ZYP, 0), (ZYP, 1)], [])

        @pl.when(step == 7)
        def _():
            pass_on([(ZYY, 0), (ZYY, 1)], [])

        for n in range(1, len(hops)):
            @pl.when(step == n)
            def _():
                hop_end(n)
                if n + 1 < len(hops):
                    hop_start(n + 1)

        order = (0, 2, 1, 3)
        forward(
            order,
            {u: kvn[step, 0, :, (u % 2) * DH:(u % 2 + 1) * DH] for u in order},
            {u: kvn[step, 1, :, (u % 2) * DH:(u % 2 + 1) * DH] for u in order},
            step, False,
        )

    resp_hops = 4
    sum_one = stat_out[resp_hops, 1:2, :]
    sum_two = stat_out[resp_hops, 2:3, :]
    live = stat_out[len(hops), 0:1, :]
    n_resp = 16
    sum_one = sum_one.astype(F32)
    sum_two = sum_two.astype(F32)
    mean = sum_one / n_resp
    variance = (n_resp * sum_two - sum_one * sum_one) / (n_resp * n_resp)
    spread = jnp.maximum(jnp.sqrt(variance), 1.0)
    norm = (n_grp * n_resp * rows) / live.astype(F32)
    for r in range(2):
        length = stat_out[0, 0:1, :] if r == 0 else stat_in[0, 0, 0:1, :]
        reward = stat_out[0, 1:2, :] if r == 0 else stat_in[0, 0, 1:2, :]
        strength = (reward.astype(F32) - mean) / spread * norm
        weight = jnp.concatenate(
            [
                jnp.where(
                    lax.broadcasted_iota(jnp.int32, (1, 128), 1) + start < length, strength, 0.0
                )
                for start in range(0, rows, 128)
            ],
            axis=1,
        )
        for j in range(2):
            u = 2 * r + j
            for h in range(heads_per):
                cols = slice(h * rows, (h + 1) * rows)
                inv = 1.0 / l_cur[u:u + 1, cols]
                out = (acc[u, :, cols] * inv).astype(BF16)
                q2[u, 0:DH, cols] = out
                delta = jnp.sum(
                    out.astype(F32) * gT[u, :, cols].astype(F32), axis=0, keepdims=True
                )
                aux[0, u:u + 1, cols] = inv * weight
                aux[1, u:u + 1, cols] = delta
                dqa[u, :, cols] = jnp.zeros((DH, rows), F32)

    def backward(units, keys, values, block, place):
        flat = {u: k.T for u, k in keys.items()}
        todo = [(u, h, slice(h * rows, (h + 1) * rows)) for u in units for h in range(heads_per)]
        scaled, shift, dots, lows, sums = {}, {}, {}, {}, {}

        def start(i):
            u, h, cols = todo[i]
            factor = jnp.exp2(m_st[block, u:u + 1, cols] - m_cur[u:u + 1, cols])
            factor = factor * aux[0, u:u + 1, cols]
            scaled[i] = (gT[u, :, cols].astype(F32) * factor).astype(BF16)
            shift[i] = factor * aux[1, u:u + 1, cols]
            dots[i] = nn(values[u], scaled[i])

        def add(key, term):
            sums[key] = sums[key] + term if key in sums else term

        def finish(i):
            u, h, cols = todo[i]
            low = lows.pop(i)
            col = (u % 2) * heads_per + h
            dqa[u, :, cols] = dqa[u, :, cols] + nn(flat[u], low)
            add((place(u), 0), nn(low, qn[u // 2, :, col * DH:(col + 1) * DH]))
            add((place(u), 1), nt(scaled.pop(i), e_st[block, u, :, cols]))

        for i in range(2):
            start(i)
        for i, (u, h, cols) in enumerate(todo):
            if i + 2 < len(todo):
                start(i + 2)
            d = dots.pop(i) - shift.pop(i)
            lows[i] = (e_st[block, u, :, cols].astype(F32) * d).astype(BF16)
            if i >= 1:
                finish(i - 1)
        finish(len(todo) - 1)
        return {
            key: term.T * inv_root if key[1] == 0 else term for key, term in sums.items()
        }

    names = ("m1", "m6", "m3", "m2", "m7", "m5", "m4")
    route = {
        "m1": (down, down), "m6": (up, up), "m3": (down, up), "m2": (z_to, z_to),
        "m7": (z_to, z_to), "m5": (up, up), "m4": (down, down),
    }
    msg = {}
    for n, name in enumerate(names):
        for kv in range(2):
            msg[name, kv] = to(
                snd.at[n, kv], rcv.at[n, kv], sem_ms.at[n, kv], sem_mr.at[n, kv], route[name][kv]
            )

    needs = {
        0: ((), ()), 1: ((), ()), 2: ((), ()), 3: (("m1",), ("m1",)), 4: (("m6",), ("m6",)),
        5: ((), ("m3",)), 6: (("m2", "m3"), ("m2",)),
    }

    @pl.loop(0, n_blocks)
    def backward_step(step):
        block = n_blocks - 1 - step
        order = (0, 2, 1, 3)
        sums = backward(
            order,
            {u: kvn[block, 0, :, (u % 2) * DH:(u % 2 + 1) * DH] for u in order},
            {u: kvn[block, 1, :, (u % 2) * DH:(u % 2 + 1) * DH] for u in order},
            block, lambda u: u % 2,
        )
        total_heads = 4 * heads_per
        for i in range(3):
            head = jnp.minimum(3 * step + i, total_heads - 1)
            u = head // heads_per
            h = head % heads_per
            col = pl.multiple_of(((u % 2) * heads_per + h) * DH, DH)
            att_n[u // 2, :, pl.ds(col, DH)] = q2[
                u, 0:DH, pl.ds(pl.multiple_of(h * rows, rows), rows)
            ].T
        for (j, kv), term in sums.items():
            own_part[kv, j * DH:(j + 1) * DH, :] = term

        for n, name in enumerate(names):
            @pl.when(step == n)
            def _():
                for kv in range(2):
                    total = own_part[kv]
                    for other in needs[n][kv]:
                        msg[other, kv].wait_recv()
                        total = total + rcv[names.index(other), kv].astype(F32)
                    snd[n, kv] = total.astype(BF16)
                    msg[name, kv].start()

    att_own = pltpu.make_async_copy(att_n.at[0], att_hbm.at[0, 0, :, cq], sem_ol.at[0])
    att_twin = to(att_n.at[1], att_hbm.at[0, 0, :, cq], sem_os.at[0], sem_or.at[0], twin)
    att_own.start()
    att_twin.start()

    outs_own = [
        pltpu.make_async_copy(rg_n.at[0, 0], drk_hbm.at[0, 0, :, ck], sem_ol.at[1]),
        pltpu.make_async_copy(rg_n.at[0, 1], drv_hbm.at[0, 0, :, ck], sem_ol.at[2]),
        pltpu.make_async_copy(dq_n.at[0], dq_hbm.at[0, 0, :, cq], sem_ol.at[3]),
    ]
    outs_twin = [
        to(rg_n.at[1, 0], drk_hbm.at[0, 0, :, ck], sem_os.at[1], sem_or.at[1], twin),
        to(rg_n.at[1, 1], drv_hbm.at[0, 0, :, ck], sem_os.at[2], sem_or.at[2], twin),
        to(dq_n.at[1], dq_hbm.at[0, 0, :, cq], sem_os.at[3], sem_or.at[3], twin),
    ]
    for r in (1, 0):
        units = (2 * r, 2 * r + 1)
        sums = backward(
            units,
            {u: rkn[r, :, (u % 2) * DH:(u % 2 + 1) * DH] for u in units},
            {u: rvn[r, :, (u % 2) * DH:(u % 2 + 1) * DH] for u in units},
            n_blocks, lambda u: u,
        )
        for j in range(2):
            for h in range(heads_per):
                col = slice((j * heads_per + h) * DH, (j * heads_per + h + 1) * DH)
                grad = dqa[2 * r + j, :, h * rows:(h + 1) * rows] * inv_root
                dq_n[r, :, col] = grad.astype(BF16).T
        for (u, kv), term in sums.items():
            rg_n[r, kv, :, (u % 2) * DH:(u % 2 + 1) * DH] = term.astype(BF16).T
        for cp in outs_twin if r else outs_own:
            cp.start()

    for kv, out in enumerate((dpk_hbm, dpv_hbm)):
        total = own_part[kv]
        for name in ("m5", "m7", "m4"):
            msg[name, kv].wait_recv()
            total = total + rcv[names.index(name), kv].astype(F32)
        pg_n[kv] = total.astype(BF16).T
        outs_own.append(
            pltpu.make_async_copy(pg_n.at[kv, my_rows, :], out.at[0, :, ck], sem_ol.at[4 + kv])
        )
        outs_twin.append(
            to(
                pg_n.at[kv, twin_rows, :], out.at[0, :, ck],
                sem_os.at[4 + kv], sem_or.at[4 + kv], twin,
            )
        )
        outs_twin[-1].start()
        outs_own[-1].start()

    for cp in [att_own] + outs_own:
        cp.wait()
    for cp in [att_twin] + outs_twin:
        cp.wait()
    stats = [cp for n in range(len(hops)) for cp in hop_copies(n)]
    for cp in pair + stats + sum(ag.values(), []) + list(msg.values()):
        cp.wait_send()


def finish(*refs):
    ins, outs, sems = refs[:6], refs[6:12], refs[12]
    copies = []
    for src, dst in zip(ins, outs):
        total = src.shape[-2]
        pieces = 4 if src.shape[-1] > 1024 else 2
        step = total // pieces
        lead = (0,) * (len(src.shape) - 2)
        for i in range(pieces):
            part = lead + (pl.ds(i * step, step),)
            copies.append(
                pltpu.make_async_copy(src.at[part], dst.at[part], sems.at[len(copies)])
            )
            copies[-1].start()
    for cp in copies:
        cp.wait()


def on_device(n_grp, queries, resp_keys, resp_values, prompt_keys, prompt_values, out_grad,
              lengths, rewards):
    rows = queries.shape[2]
    half_q = queries.shape[3] // 2
    half_k = resp_keys.shape[3] // 2
    heads_per = half_q // half_k
    piece = prompt_keys.shape[1]
    blk = 2 * piece
    width = heads_per * rows
    anywhere = pl.BlockSpec(memory_space=pl.ANY)
    dma = pltpu.SemaphoreType.DMA
    vmem = pltpu.VMEM
    scratch = [
        pltpu.SMEM((1, 1), jnp.int32), pltpu.SMEM((1, 1), jnp.int32),
        vmem((2, rows, half_q), BF16), vmem((2, rows, half_q), BF16),
        vmem((2, rows, half_k), BF16), vmem((2, rows, half_k), BF16),
        vmem((8, 2, blk, half_k), BF16),
        vmem((4, DH, width), BF16), vmem((4, 2 * DH, width), BF16), vmem((4, DH, width), BF16),
        vmem((9, 4, blk, width), BF16),
        vmem((9, 8, width), F32), vmem((8, width), F32), vmem((8, width), F32),
        vmem((4, DH, width), F32), vmem((4, DH, width), F32),
        vmem((2, 8, width), F32),
        vmem((8, 8, 128), jnp.int32), vmem((8, 2, 8, 128), jnp.int32),
        vmem((7, 2, half_k, blk), BF16), vmem((7, 2, half_k, blk), BF16),
        vmem((2, half_k, blk), F32),
        vmem((2, rows, half_q), BF16), vmem((2, rows, half_q), BF16),
        vmem((2, 2, rows, half_k), BF16), vmem((2, blk, half_k), BF16),
        dma((8,)), dma((6,)), dma((6,)), dma((8, 2)), dma((8, 2)),
        dma((8, 2)), dma((8, 2)),
        dma((8, 2)), dma((8, 2)),
        dma((7, 2)), dma((7, 2)), dma((6,)), dma((6,)), dma((6,)),
    ]
    like = lambda a: jax.ShapeDtypeStruct(a.shape, a.dtype)
    shapes = (
        like(queries), like(queries), like(resp_keys), like(resp_values),
        like(prompt_keys), like(prompt_values),
    )
    results = pl.pallas_call(
        lambda *refs: kernel(n_grp, heads_per, *refs),
        out_shape=shapes,
        in_specs=[anywhere] * 6 + [pl.BlockSpec(memory_space=pltpu.HBM)] * 2,
        out_specs=(anywhere,) * 6,
        scratch_shapes=scratch,
        compiler_params=pltpu.CompilerParams(
            collective_id=0, has_side_effects=True, vmem_limit_bytes=60 * 2**20
        ),
        name="grpo_attention",
    )(queries, resp_keys, resp_values, prompt_keys, prompt_values, out_grad, lengths, rewards)
    return pl.pallas_call(
        finish,
        out_shape=shapes,
        in_specs=[anywhere] * 6,
        out_specs=(anywhere,) * 6,
        scratch_shapes=[dma((16,))],
        compiler_params=pltpu.CompilerParams(vmem_limit_bytes=60 * 2**20),
        name="write_results",
    )(*results)


def solution(mesh):
    n_grp = mesh.shape["grp"]
    wide = P("grp", "resp", None, None)
    tall = P("grp", "resp", None)
    return jax.shard_map(
        lambda *arrays: on_device(n_grp, *arrays),
        mesh=mesh,
        in_specs=(wide, wide, wide, tall, tall, wide, P("grp", "resp"), P("grp", "resp")),
        out_specs=(wide, wide, wide, wide, tall, tall),
        check_vma=False,
    )
```

```python
import math

import jax
import jax.numpy as jnp
from jax import lax
from jax.experimental import pallas as pl
from jax.experimental.pallas import tpu as pltpu
from jax.sharding import PartitionSpec as P

DH = 128
F32 = jnp.float32
BF16 = jnp.bfloat16
MESH = pl.DeviceIdType.MESH

SLOTS = ((0, 0), (0, 3), (0, 1), (1, 0), (1, 3), (0, 2), (1, 1), (1, 2))
OWN, YM, YP, ZZ, ZYM, YY, ZYP, ZYY = range(8)


def nn(a, b):
    return jnp.dot(a, b, preferred_element_type=F32)


def nt(a, b):
    return lax.dot_general(a, b, (((1,), (1,)), ((), ())), preferred_element_type=F32)


def kernel(
    n_grp, heads_per, q_hbm, rk_hbm, rv_hbm, pk_hbm, pv_hbm, og_hbm, len_ref, rew_ref,
    att_hbm, dq_hbm, drk_hbm, drv_hbm, dpk_hbm, dpv_hbm,
    qn, gn, rkn, rvn, kvn, qT, q2, gT, e_st, m_st, m_cur, l_cur, acc, dqa, aux,
    stat_out, stat_in, snd, rcv, own_part, att_n, dq_n, rg_n, pg_n,
    sem_l, sem_ps, sem_pr, sem_as, sem_ar, sem_bs, sem_br, sem_ss, sem_sr,
    sem_ms, sem_mr, sem_ol, sem_os, sem_or,
):
    rows = qn.shape[1]
    half_q = qn.shape[2]
    half_k = rkn.shape[2]
    piece = pk_hbm.shape[1]
    blk = 2 * piece
    width = heads_per * rows
    inv_root = DH ** (-0.5)
    scale2 = inv_root * math.log2(math.e)
    me = lax.axis_index("resp")
    grp = lax.axis_index("grp")
    z = me // 8
    y = (me // 2) % 4
    c = me % 2

    def at(dz, dy, dc):
        return {"resp": ((z + dz) % 2) * 8 + ((y + dy) % 4) * 2 + (c + dc) % 2}

    def to(src, dst, s_sem, r_sem, target):
        return pltpu.make_async_remote_copy(
            src_ref=src, dst_ref=dst, send_sem=s_sem, recv_sem=r_sem,
            device_id=target, device_id_type=MESH,
        )

    cq = pl.ds(pl.multiple_of(c * half_q, half_q), half_q)
    oq = pl.ds(pl.multiple_of((1 - c) * half_q, half_q), half_q)
    ck = pl.ds(pl.multiple_of(c * half_k, half_k), half_k)
    ok = pl.ds(pl.multiple_of((1 - c) * half_k, half_k), half_k)
    my_rows = pl.ds(pl.multiple_of(c * piece, piece), piece)

    local = [
        pltpu.make_async_copy(pk_hbm.at[0, :, ck], kvn.at[OWN, 0, my_rows, :], sem_l.at[0]),
        pltpu.make_async_copy(pv_hbm.at[0, :, ck], kvn.at[OWN, 1, my_rows, :], sem_l.at[1]),
        pltpu.make_async_copy(q_hbm.at[0, 0, :, cq], qn.at[0], sem_l.at[2]),
        pltpu.make_async_copy(rk_hbm.at[0, 0, :, ck], rkn.at[0], sem_l.at[3]),
        pltpu.make_async_copy(rv_hbm.at[0, 0, :, ck], rvn.at[0], sem_l.at[4]),
        pltpu.make_async_copy(og_hbm.at[0, 0, :, cq], gn.at[0], sem_l.at[5]),
    ]
    for cp in local:
        cp.start()

    twin = at(0, 0, 1)
    z_to, up, down = at(1, 0, 0), at(0, 1, 0), at(0, 3, 0)
    ring = min(4, n_grp)
    base = (grp // ring) * ring
    x_up = {"grp": base + (grp - base + 1) % ring}
    x_down = {"grp": base + (grp - base + ring - 1) % ring}
    across = {"grp": (grp + ring) % n_grp}
    friends = [twin, z_to, up, down]
    if ring == 4:
        friends += [x_up, x_down]
    if n_grp > ring:
        friends.append(across)
    barrier = pltpu.get_barrier_semaphore()
    for friend in friends:
        pl.semaphore_signal(barrier, inc=1, device_id=friend, device_id_type=MESH)

    def turn(src, dst, r):
        for j in range(2):
            for h in range(heads_per):
                dst[2 * r + j, :, h * rows:(h + 1) * rows] = src[
                    r, :, (j * heads_per + h) * DH:(j * heads_per + h + 1) * DH
                ].T

    def split_queries(r):
        for u in (2 * r, 2 * r + 1):
            for h in range(heads_per):
                cols = slice(h * rows, (h + 1) * rows)
                full = qT[u, :, cols].astype(F32) * scale2
                high = full.astype(BF16)
                q2[u, 0:DH, cols] = high
                q2[u, DH:2 * DH, cols] = (full - high.astype(F32)).astype(BF16)

    ones = jnp.ones((16, blk), BF16)

    def forward(units, keys, values, block, first):
        keys = {u: jnp.concatenate([k, k], axis=1) for u, k in keys.items()}
        values = {u: jnp.concatenate([v.T, ones], axis=0) for u, v in values.items()}
        todo = [(u, slice(h * rows, (h + 1) * rows)) for u in units for h in range(heads_per)]
        logits, lows = {}, {}

        def start(i):
            u, cols = todo[i]
            logits[i] = nn(keys[u], q2[u, :, cols])

        def finish(i):
            u, cols = todo[i]
            low, alpha = lows.pop(i)
            part = nn(values[u], low)
            if first:
                l_cur[u:u + 1, cols] = part[DH:DH + 1]
                acc[u, :, cols] = part[0:DH]
            else:
                l_cur[u:u + 1, cols] = l_cur[u:u + 1, cols] * alpha + part[DH:DH + 1]
                acc[u, :, cols] = acc[u, :, cols] * alpha + part[0:DH]

        for i in range(3):
            start(i)
        for i, (u, cols) in enumerate(todo):
            if i + 3 < len(todo):
                start(i + 3)
            s = logits.pop(i)
            if first:
                seen = lax.broadcasted_iota(jnp.int32, s.shape, 0) <= (
                    lax.broadcasted_iota(jnp.int32, s.shape, 1)
                )
                s = jnp.where(seen, s, -jnp.inf)
                m_new = jnp.max(s, axis=0, keepdims=True)
                alpha = None
            else:
                m_old = m_cur[u:u + 1, cols]
                m_new = jnp.maximum(m_old, jnp.max(s, axis=0, keepdims=True))
                alpha = jnp.exp2(m_old - m_new)
            low = jnp.exp2(s - m_new).astype(BF16)
            e_st[block, u, :, cols] = low
            m_cur[u:u + 1, cols] = m_new
            m_st[block, u:u + 1, cols] = m_new
            lows[i] = (low, alpha)
            if i >= 2:
                finish(i - 2)
        for i in sorted(lows):
            finish(i)

    def own_block(r):
        turn(qn, qT, r)
        split_queries(r)
        units = (2 * r, 2 * r + 1)
        forward(
            units,
            {u: rkn[r, :, (u % 2) * DH:(u % 2 + 1) * DH] for u in units},
            {u: rvn[r, :, (u % 2) * DH:(u % 2 + 1) * DH] for u in units},
            n_blocks, True,
        )

    pl.semaphore_wait(barrier, len(friends))

    pair = [
        to(pk_hbm.at[0, :, ok], kvn.at[OWN, 0, my_rows, :], sem_ps.at[0], sem_pr.at[0], twin),
        to(pv_hbm.at[0, :, ok], kvn.at[OWN, 1, my_rows, :], sem_ps.at[1], sem_pr.at[1], twin),
        to(q_hbm.at[0, 0, :, oq], qn.at[1], sem_ps.at[2], sem_pr.at[2], twin),
        to(rk_hbm.at[0, 0, :, ok], rkn.at[1], sem_ps.at[3], sem_pr.at[3], twin),
        to(rv_hbm.at[0, 0, :, ok], rvn.at[1], sem_ps.at[4], sem_pr.at[4], twin),
        to(og_hbm.at[0, 0, :, oq], gn.at[1], sem_ps.at[5], sem_pr.at[5], twin),
    ]
    for cp in pair[:2]:
        cp.start()

    twin_rows = pl.ds(pl.multiple_of((1 - c) * piece, piece), piece)
    ag = {}
    for kv in (0, 1):
        for dst, target in ((YM, up), (YP, down), (ZZ, z_to)):
            ag[dst, kv] = [
                to(
                    (pk_hbm, pv_hbm)[kv].at[0, :, ck], kvn.at[dst, kv, my_rows, :],
                    sem_as.at[dst, kv], sem_ar.at[dst, kv], target,
                ),
                to(
                    kvn.at[OWN, kv, twin_rows, :], kvn.at[dst, kv, twin_rows, :],
                    sem_bs.at[dst, kv], sem_br.at[dst, kv], target,
                ),
            ]
    ag_plan = (
        (YM, YY, 0, up), (YM, ZYM, 0, z_to), (YM, ZYM, 1, z_to),
        (YP, YY, 1, down), (ZZ, ZYP, 0, down), (ZZ, ZYP, 1, down),
        (ZYM, ZYY, 0, up), (ZYM, ZYY, 1, up),
    )
    for src, dst, kv, target in ag_plan:
        ag[dst, kv] = [
            to(kvn.at[src, kv], kvn.at[dst, kv], sem_as.at[dst, kv], sem_ar.at[dst, kv], target)
        ]

    for kv in (0, 1):
        for dst in (YM, YP, ZZ):
            ag[dst, kv][0].start()
    for cp in pair[2:]:
        cp.start()
    for kv in (0, 1):
        local[kv].wait()
        pair[kv].wait_recv()
        for dst in (YM, YP, ZZ):
            ag[dst, kv][1].start()


    hops = [((twin,), False), ((z_to,), False), ((up, down), False), ((up,), True)]
    if ring == 4:
        hops += [((x_up, x_down), False), ((x_up,), True)]
    if n_grp > ring:
        hops.append(((across,), False))

    def hop_copies(n):
        targets, relay = hops[n]
        src = stat_in.at[n - 1, 1] if relay else stat_out.at[n]
        copies = []
        for i, target in enumerate(targets):
            slot = 1 - i if len(targets) == 2 else 0
            copies.append(
                to(src, stat_in.at[n, slot], sem_ss.at[n, slot], sem_sr.at[n, slot], target)
            )
        return copies

    def hop_start(n):
        for cp in hop_copies(n):
            cp.start()

    def hop_end(n):
        for cp in hop_copies(n):
            cp.wait_recv()
        total = stat_out[n]
        for slot in range(len(hops[n][0])):
            total = total + stat_in[n, slot]
        stat_out[n + 1] = total

    row_id = lax.broadcasted_iota(jnp.int32, (8, 128), 0)
    length_own = jnp.broadcast_to(len_ref[...], (8, 128))
    reward_own = jnp.broadcast_to(rew_ref[...], (8, 128))
    stat_out[0] = jnp.where(
        row_id == 0, length_own, jnp.where(row_id == 1, reward_own, reward_own * reward_own)
    )
    hop_start(0)

    n_blocks = 8
    for i in (2, 3, 4):
        local[i].wait()
    own_block(0)

    for i in (2, 3, 4):
        pair[i].wait_recv()
    own_block(1)
    local[5].wait()
    pair[5].wait_recv()
    for r in range(2):
        turn(gn, gT, r)
    hop_end(0)
    hop_start(1)

    def pass_on(waits, starts):
        for key in waits:
            for cp in ag[key]:
                cp.wait_recv()
        for key in starts:
            for cp in ag[key]:
                cp.start()

    @pl.loop(0, n_blocks)
    def forward_step(step):
        @pl.when(step == 1)
        def _():
            pass_on([(YM, 0)], [(YY, 0), (ZYM, 0)])
            pass_on([(ZZ, 0)], [(ZYP, 0)])
            pass_on([(YM, 1)], [(ZYM, 1)])
            pass_on([(YP, 0), (YP, 1)], [(YY, 1)])
            pass_on([(ZZ, 1)], [(ZYP, 1)])

        @pl.when(step == 3)
        def _():
            pass_on([(ZYM, 0)], [(ZYY, 0)])

        @pl.when(step == 4)
        def _():
            pass_on([(ZYM, 1)], [(ZYY, 1)])

        @pl.when(step == 5)
        def _():
            pass_on([(YY, 0), (YY, 1)], [])

        @pl.when(step == 6)
        def _():
            pass_on([(ZYP, 0), (ZYP, 1)], [])

        @pl.when(step == 7)
        def _():
            pass_on([(ZYY, 0), (ZYY, 1)], [])

        for n in range(1, len(hops)):
            @pl.when(step == n)
            def _():
                hop_end(n)
                if n + 1 < len(hops):
                    hop_start(n + 1)

        order = (0, 2, 1, 3)
        forward(
            order,
            {u: kvn[step, 0, :, (u % 2) * DH:(u % 2 + 1) * DH] for u in order},
            {u: kvn[step, 1, :, (u % 2) * DH:(u % 2 + 1) * DH] for u in order},
            step, False,
        )

    resp_hops = 4
    sum_one = stat_out[resp_hops, 1:2, :]
    sum_two = stat_out[resp_hops, 2:3, :]
    live = stat_out[len(hops), 0:1, :]
    n_resp = 16
    sum_one = sum_one.astype(F32)
    sum_two = sum_two.astype(F32)
    mean = sum_one / n_resp
    variance = (n_resp * sum_two - sum_one * sum_one) / (n_resp * n_resp)
    spread = jnp.maximum(jnp.sqrt(variance), 1.0)
    norm = (n_grp * n_resp * rows) / live.astype(F32)
    for r in range(2):
        length = stat_out[0, 0:1, :] if r == 0 else stat_in[0, 0, 0:1, :]
        reward = stat_out[0, 1:2, :] if r == 0 else stat_in[0, 0, 1:2, :]
        strength = (reward.astype(F32) - mean) / spread * norm
        weight = jnp.concatenate(
            [
                jnp.where(
                    lax.broadcasted_iota(jnp.int32, (1, 128), 1) + start < length, strength, 0.0
                )
                for start in range(0, rows, 128)
            ],
            axis=1,
        )
        for j in range(2):
            u = 2 * r + j
            for h in range(heads_per):
                cols = slice(h * rows, (h + 1) * rows)
                inv = 1.0 / l_cur[u:u + 1, cols]
                out = (acc[u, :, cols] * inv).astype(BF16)
                q2[u, 0:DH, cols] = out
                delta = jnp.sum(
                    out.astype(F32) * gT[u, :, cols].astype(F32), axis=0, keepdims=True
                )
                aux[0, u:u + 1, cols] = inv * weight
                aux[1, u:u + 1, cols] = delta
                dqa[u, :, cols] = jnp.zeros((DH, rows), F32)

    def backward(units, keys, values, block, place):
        flat = {u: k.T for u, k in keys.items()}
        todo = [(u, h, slice(h * rows, (h + 1) * rows)) for u in units for h in range(heads_per)]
        scaled, shift, dots, lows, sums = {}, {}, {}, {}, {}

        def start(i):
            u, h, cols = todo[i]
            factor = jnp.exp2(m_st[block, u:u + 1, cols] - m_cur[u:u + 1, cols])
            factor = factor * aux[0, u:u + 1, cols]
            scaled[i] = (gT[u, :, cols].astype(F32) * factor).astype(BF16)
            shift[i] = factor * aux[1, u:u + 1, cols]
            dots[i] = nn(values[u], scaled[i])

        def add(key, term):
            sums[key] = sums[key] + term if key in sums else term

        def finish(i):
            u, h, cols = todo[i]
            low = lows.pop(i)
            col = (u % 2) * heads_per + h
            dqa[u, :, cols] = dqa[u, :, cols] + nn(flat[u], low)
            add((place(u), 0), nn(low, qn[u // 2, :, col * DH:(col + 1) * DH]))
            add((place(u), 1), nt(scaled.pop(i), e_st[block, u, :, cols]))

        for i in range(2):
            start(i)
        for i, (u, h, cols) in enumerate(todo):
            if i + 2 < len(todo):
                start(i + 2)
            d = dots.pop(i) - shift.pop(i)
            lows[i] = (e_st[block, u, :, cols].astype(F32) * d).astype(BF16)
            if i >= 1:
                finish(i - 1)
        finish(len(todo) - 1)
        return {
            key: term.T * inv_root if key[1] == 0 else term for key, term in sums.items()
        }

    names = ("m1", "m6", "m3", "m2", "m7", "m5", "m4")
    route = {
        "m1": (down, down), "m6": (up, up), "m3": (down, up), "m2": (z_to, z_to),
        "m7": (z_to, z_to), "m5": (up, up), "m4": (down, down),
    }
    msg = {}
    for n, name in enumerate(names):
        for kv in range(2):
            msg[name, kv] = to(
                snd.at[n, kv], rcv.at[n, kv], sem_ms.at[n, kv], sem_mr.at[n, kv], route[name][kv]
            )

    needs = {
        0: ((), ()), 1: ((), ()), 2: ((), ()), 3: (("m1",), ("m1",)), 4: (("m6",), ("m6",)),
        5: ((), ("m3",)), 6: (("m2", "m3"), ("m2",)),
    }

    @pl.loop(0, n_blocks)
    def backward_step(step):
        block = n_blocks - 1 - step
        order = (0, 2, 1, 3)
        sums = backward(
            order,
            {u: kvn[block, 0, :, (u % 2) * DH:(u % 2 + 1) * DH] for u in order},
            {u: kvn[block, 1, :, (u % 2) * DH:(u % 2 + 1) * DH] for u in order},
            block, lambda u: u % 2,
        )
        total_heads = 4 * heads_per
        for i in range(3):
            head = jnp.minimum(3 * step + i, total_heads - 1)
            u = head // heads_per
            h = head % heads_per
            col = pl.multiple_of(((u % 2) * heads_per + h) * DH, DH)
            att_n[u // 2, :, pl.ds(col, DH)] = q2[
                u, 0:DH, pl.ds(pl.multiple_of(h * rows, rows), rows)
            ].T
        for (j, kv), term in sums.items():
            own_part[kv, j * DH:(j + 1) * DH, :] = term

        for n, name in enumerate(names):
            @pl.when(step == n)
            def _():
                for kv in range(2):
                    total = own_part[kv]
                    for other in needs[n][kv]:
                        msg[other, kv].wait_recv()
                        total = total + rcv[names.index(other), kv].astype(F32)
                    snd[n, kv] = total.astype(BF16)
                    msg[name, kv].start()

    att_own = pltpu.make_async_copy(att_n.at[0], att_hbm.at[0, 0, :, cq], sem_ol.at[0])
    att_twin = to(att_n.at[1], att_hbm.at[0, 0, :, cq], sem_os.at[0], sem_or.at[0], twin)
    att_own.start()
    att_twin.start()

    outs_own = [
        pltpu.make_async_copy(rg_n.at[0, 0], drk_hbm.at[0, 0, :, ck], sem_ol.at[1]),
        pltpu.make_async_copy(rg_n.at[0, 1], drv_hbm.at[0, 0, :, ck], sem_ol.at[2]),
        pltpu.make_async_copy(dq_n.at[0], dq_hbm.at[0, 0, :, cq], sem_ol.at[3]),
    ]
    outs_twin = [
        to(rg_n.at[1, 0], drk_hbm.at[0, 0, :, ck], sem_os.at[1], sem_or.at[1], twin),
        to(rg_n.at[1, 1], drv_hbm.at[0, 0, :, ck], sem_os.at[2], sem_or.at[2], twin),
        to(dq_n.at[1], dq_hbm.at[0, 0, :, cq], sem_os.at[3], sem_or.at[3], twin),
    ]
    for r in (1, 0):
        units = (2 * r, 2 * r + 1)
        sums = backward(
            units,
            {u: rkn[r, :, (u % 2) * DH:(u % 2 + 1) * DH] for u in units},
            {u: rvn[r, :, (u % 2) * DH:(u % 2 + 1) * DH] for u in units},
            n_blocks, lambda u: u,
        )
        for j in range(2):
            for h in range(heads_per):
                col = slice((j * heads_per + h) * DH, (j * heads_per + h + 1) * DH)
                grad = dqa[2 * r + j, :, h * rows:(h + 1) * rows] * inv_root
                dq_n[r, :, col] = grad.astype(BF16).T
        for (u, kv), term in sums.items():
            rg_n[r, kv, :, (u % 2) * DH:(u % 2 + 1) * DH] = term.astype(BF16).T
        for cp in outs_twin if r else outs_own:
            cp.start()

    for kv, out in enumerate((dpk_hbm, dpv_hbm)):
        total = own_part[kv]
        for name in ("m5", "m7", "m4"):
            msg[name, kv].wait_recv()
            total = total + rcv[names.index(name), kv].astype(F32)
        pg_n[kv] = total.astype(BF16).T
        outs_own.append(
            pltpu.make_async_copy(pg_n.at[kv, my_rows, :], out.at[0, :, ck], sem_ol.at[4 + kv])
        )
        outs_twin.append(
            to(
                pg_n.at[kv, twin_rows, :], out.at[0, :, ck],
                sem_os.at[4 + kv], sem_or.at[4 + kv], twin,
            )
        )
        outs_twin[-1].start()
        outs_own[-1].start()

    for cp in [att_own] + outs_own:
        cp.wait()
    for cp in [att_twin] + outs_twin:
        cp.wait()
    stats = [cp for n in range(len(hops)) for cp in hop_copies(n)]
    for cp in pair + stats + sum(ag.values(), []) + list(msg.values()):
        cp.wait_send()


def finish(*refs):
    ins, outs, bufs, (sem_in, sem_out) = refs[:6], refs[6:12], refs[12:18], refs[18:]
    loads, stores = [], []
    for src, dst, buf in zip(ins, outs, bufs):
        total = src.shape[-2]
        pieces = 4 if src.shape[-1] > 1024 else 1
        step = total // pieces
        lead = (0,) * (len(src.shape) - 2)
        for i in range(pieces):
            part = lead + (pl.ds(i * step, step),)
            n = len(loads)
            loads.append(pltpu.make_async_copy(src.at[part], buf.at[part], sem_in.at[n]))
            stores.append(pltpu.make_async_copy(buf.at[part], dst.at[part], sem_out.at[n]))
            loads[-1].start()
    for load, store in zip(loads, stores):
        load.wait()
        store.start()
    for store in stores:
        store.wait()


def on_device(n_grp, queries, resp_keys, resp_values, prompt_keys, prompt_values, out_grad,
              lengths, rewards):
    rows = queries.shape[2]
    half_q = queries.shape[3] // 2
    half_k = resp_keys.shape[3] // 2
    heads_per = half_q // half_k
    piece = prompt_keys.shape[1]
    blk = 2 * piece
    width = heads_per * rows
    anywhere = pl.BlockSpec(memory_space=pl.ANY)
    dma = pltpu.SemaphoreType.DMA
    vmem = pltpu.VMEM
    scratch = [
        vmem((2, rows, half_q), BF16), vmem((2, rows, half_q), BF16),
        vmem((2, rows, half_k), BF16), vmem((2, rows, half_k), BF16),
        vmem((8, 2, blk, half_k), BF16),
        vmem((4, DH, width), BF16), vmem((4, 2 * DH, width), BF16), vmem((4, DH, width), BF16),
        vmem((9, 4, blk, width), BF16),
        vmem((9, 8, width), F32), vmem((8, width), F32), vmem((8, width), F32),
        vmem((4, DH, width), F32), vmem((4, DH, width), F32),
        vmem((2, 8, width), F32),
        vmem((8, 8, 128), jnp.int32), vmem((8, 2, 8, 128), jnp.int32),
        vmem((7, 2, half_k, blk), BF16), vmem((7, 2, half_k, blk), BF16),
        vmem((2, half_k, blk), F32),
        vmem((2, rows, half_q), BF16), vmem((2, rows, half_q), BF16),
        vmem((2, 2, rows, half_k), BF16), vmem((2, blk, half_k), BF16),
        dma((6,)), dma((6,)), dma((6,)), dma((8, 2)), dma((8, 2)),
        dma((8, 2)), dma((8, 2)),
        dma((8, 2)), dma((8, 2)),
        dma((7, 2)), dma((7, 2)), dma((6,)), dma((6,)), dma((6,)),
    ]
    like = lambda a: jax.ShapeDtypeStruct(a.shape, a.dtype)
    shapes = (
        like(queries), like(queries), like(resp_keys), like(resp_values),
        like(prompt_keys), like(prompt_values),
    )
    results = pl.pallas_call(
        lambda *refs: kernel(n_grp, heads_per, *refs),
        out_shape=shapes,
        in_specs=[anywhere] * 6 + [pl.BlockSpec(memory_space=pltpu.VMEM)] * 2,
        out_specs=(anywhere,) * 6,
        scratch_shapes=scratch,
        compiler_params=pltpu.CompilerParams(
            collective_id=0, has_side_effects=True, vmem_limit_bytes=60 * 2**20
        ),
        name="grpo_attention",
    )(queries, resp_keys, resp_values, prompt_keys, prompt_values, out_grad, lengths, rewards)
    return pl.pallas_call(
        finish,
        out_shape=shapes,
        in_specs=[anywhere] * 6,
        out_specs=(anywhere,) * 6,
        scratch_shapes=[vmem(x.shape, x.dtype) for x in shapes] + [dma((12,)), dma((12,))],
        compiler_params=pltpu.CompilerParams(vmem_limit_bytes=60 * 2**20),
        name="write_results",
    )(*results)


def solution(mesh):
    n_grp = mesh.shape["grp"]
    wide = P("grp", "resp", None, None)
    tall = P("grp", "resp", None)
    return jax.shard_map(
        lambda *arrays: on_device(n_grp, *arrays),
        mesh=mesh,
        in_specs=(wide, wide, wide, tall, tall, wide, P("grp", "resp"), P("grp", "resp")),
        out_specs=(wide, wide, wide, wide, tall, tall),
        check_vma=False,
    )
```

```python
import math

import jax
import jax.numpy as jnp
from jax import lax
from jax.experimental import pallas as pl
from jax.experimental.pallas import tpu as pltpu
from jax.sharding import PartitionSpec as P

DH = 128
F32 = jnp.float32
BF16 = jnp.bfloat16
MESH = pl.DeviceIdType.MESH

SLOTS = ((0, 0), (0, 3), (0, 1), (1, 0), (1, 3), (0, 2), (1, 1), (1, 2))
OWN, YM, YP, ZZ, ZYM, YY, ZYP, ZYY = range(8)


def nn(a, b):
    return jnp.dot(a, b, preferred_element_type=F32)


def nt(a, b):
    return lax.dot_general(a, b, (((1,), (1,)), ((), ())), preferred_element_type=F32)


def kernel(
    n_grp, heads_per, q_hbm, rk_hbm, rv_hbm, pk_hbm, pv_hbm, og_hbm, len_ref, rew_ref,
    att_hbm, dq_hbm, drk_hbm, drv_hbm, dpk_hbm, dpv_hbm,
    qn, gn, rkn, rvn, kn, vn, stat_own, qT, q2, gT, e_st, m_st, m_cur, l_cur, acc, dqa, aux,
    stat_out, stat_in, snd, rcv, own_part, att_n, dq_n, rg_n, pg_n,
    sem_l, sem_ps, sem_pr, sem_as, sem_ar, sem_bs, sem_br, sem_ss, sem_sr,
    sem_ms, sem_mr, sem_ol, sem_os, sem_or,
):
    rows = qn.shape[1]
    half_q = qn.shape[2]
    half_k = rkn.shape[2]
    piece = pk_hbm.shape[1]
    blk = 2 * piece
    width = heads_per * rows
    inv_root = DH ** (-0.5)
    scale2 = inv_root * math.log2(math.e)
    me = lax.axis_index("resp")
    grp = lax.axis_index("grp")
    z = me // 8
    y = (me // 2) % 4
    c = me % 2

    def at(dz, dy, dc):
        return {"resp": ((z + dz) % 2) * 8 + ((y + dy) % 4) * 2 + (c + dc) % 2}

    def to(src, dst, s_sem, r_sem, target):
        return pltpu.make_async_remote_copy(
            src_ref=src, dst_ref=dst, send_sem=s_sem, recv_sem=r_sem,
            device_id=target, device_id_type=MESH,
        )

    cq = pl.ds(pl.multiple_of(c * half_q, half_q), half_q)
    oq = pl.ds(pl.multiple_of((1 - c) * half_q, half_q), half_q)
    ck = pl.ds(pl.multiple_of(c * half_k, half_k), half_k)
    ok = pl.ds(pl.multiple_of((1 - c) * half_k, half_k), half_k)
    my_rows = pl.ds(pl.multiple_of(c * piece, piece), piece)
    tall = piece + 16
    my_keys = pl.ds(pl.multiple_of(c * tall, 16), piece)
    my_stats = pl.ds(pl.multiple_of(c * tall + piece, 16), 16)
    my_part, twin_part = [
        [pl.ds(pl.multiple_of(k * size, 16), size) for size in (tall, piece)] for k in (c, 1 - c)
    ]
    ring_kv = (kn, vn)

    local = [
        pltpu.make_async_copy(pk_hbm.at[0, :, ck], kn.at[OWN, my_keys, :], sem_l.at[0]),
        pltpu.make_async_copy(pv_hbm.at[0, :, ck], vn.at[OWN, my_rows, :], sem_l.at[1]),
        pltpu.make_async_copy(q_hbm.at[0, 0, :, cq], qn.at[0], sem_l.at[2]),
        pltpu.make_async_copy(rk_hbm.at[0, 0, :, ck], rkn.at[0], sem_l.at[3]),
        pltpu.make_async_copy(rv_hbm.at[0, 0, :, ck], rvn.at[0], sem_l.at[4]),
        pltpu.make_async_copy(og_hbm.at[0, 0, :, cq], gn.at[0], sem_l.at[5]),
    ]
    for cp in local:
        cp.start()

    twin = at(0, 0, 1)
    z_to, up, down = at(1, 0, 0), at(0, 1, 0), at(0, 3, 0)
    ring = min(4, n_grp)
    base = (grp // ring) * ring
    x_up = {"grp": base + (grp - base + 1) % ring}
    x_down = {"grp": base + (grp - base + ring - 1) % ring}
    across = {"grp": (grp + ring) % n_grp}
    friends = [twin, z_to, up, down]
    if ring == 4:
        friends += [x_up, x_down]
    if n_grp > ring:
        friends.append(across)
    barrier = pltpu.get_barrier_semaphore()
    for friend in friends:
        pl.semaphore_signal(barrier, inc=1, device_id=friend, device_id_type=MESH)

    def turn(src, dst, r):
        for j in range(2):
            for h in range(heads_per):
                dst[2 * r + j, :, h * rows:(h + 1) * rows] = src[
                    r, :, (j * heads_per + h) * DH:(j * heads_per + h + 1) * DH
                ].T

    def split_queries(r):
        for u in (2 * r, 2 * r + 1):
            for h in range(heads_per):
                cols = slice(h * rows, (h + 1) * rows)
                full = qT[u, :, cols].astype(F32) * scale2
                high = full.astype(BF16)
                q2[u, 0:DH, cols] = high
                q2[u, DH:2 * DH, cols] = (full - high.astype(F32)).astype(BF16)

    ones = jnp.ones((16, blk), BF16)

    def forward(units, keys, values, block, first):
        keys = {u: jnp.concatenate([k, k], axis=1) for u, k in keys.items()}
        values = {u: jnp.concatenate([v.T, ones], axis=0) for u, v in values.items()}
        todo = [(u, slice(h * rows, (h + 1) * rows)) for u in units for h in range(heads_per)]
        logits, lows = {}, {}

        def start(i):
            u, cols = todo[i]
            logits[i] = nn(keys[u], q2[u, :, cols])

        def finish(i):
            u, cols = todo[i]
            low, alpha = lows.pop(i)
            part = nn(values[u], low)
            if first:
                l_cur[u:u + 1, cols] = part[DH:DH + 1]
                acc[u, :, cols] = part[0:DH]
            else:
                l_cur[u:u + 1, cols] = l_cur[u:u + 1, cols] * alpha + part[DH:DH + 1]
                acc[u, :, cols] = acc[u, :, cols] * alpha + part[0:DH]

        for i in range(3):
            start(i)
        for i, (u, cols) in enumerate(todo):
            if i + 3 < len(todo):
                start(i + 3)
            s = logits.pop(i)
            if first:
                seen = lax.broadcasted_iota(jnp.int32, s.shape, 0) <= (
                    lax.broadcasted_iota(jnp.int32, s.shape, 1)
                )
                s = jnp.where(seen, s, -jnp.inf)
                m_new = jnp.max(s, axis=0, keepdims=True)
                alpha = None
            else:
                m_old = m_cur[u:u + 1, cols]
                m_new = jnp.maximum(m_old, jnp.max(s, axis=0, keepdims=True))
                alpha = jnp.exp2(m_old - m_new)
            low = jnp.exp2(s - m_new).astype(BF16)
            e_st[block, u, :, cols] = low
            m_cur[u:u + 1, cols] = m_new
            m_st[block, u:u + 1, cols] = m_new
            lows[i] = (low, alpha)
            if i >= 2:
                finish(i - 2)
        for i in sorted(lows):
            finish(i)

    def own_block(r):
        turn(qn, qT, r)
        split_queries(r)
        units = (2 * r, 2 * r + 1)
        forward(
            units,
            {u: rkn[r, :, (u % 2) * DH:(u % 2 + 1) * DH] for u in units},
            {u: rvn[r, :, (u % 2) * DH:(u % 2 + 1) * DH] for u in units},
            n_blocks, True,
        )

    row_id = lax.broadcasted_iota(jnp.int32, stat_own.shape, 0)
    stat_own[...] = jnp.where(
        row_id == 0,
        jnp.broadcast_to(len_ref[...], stat_own.shape),
        jnp.broadcast_to(rew_ref[...], stat_own.shape),
    ).astype(F32).astype(BF16)
    kn[OWN, my_stats, :] = stat_own[...]
    pl.semaphore_wait(barrier, len(friends))

    pair = [
        to(pk_hbm.at[0, :, ok], kn.at[OWN, my_keys, :], sem_ps.at[0], sem_pr.at[0], twin),
        to(pv_hbm.at[0, :, ok], vn.at[OWN, my_rows, :], sem_ps.at[1], sem_pr.at[1], twin),
        to(q_hbm.at[0, 0, :, oq], qn.at[1], sem_ps.at[2], sem_pr.at[2], twin),
        to(rk_hbm.at[0, 0, :, ok], rkn.at[1], sem_ps.at[3], sem_pr.at[3], twin),
        to(rv_hbm.at[0, 0, :, ok], rvn.at[1], sem_ps.at[4], sem_pr.at[4], twin),
        to(og_hbm.at[0, 0, :, oq], gn.at[1], sem_ps.at[5], sem_pr.at[5], twin),
        to(stat_own, kn.at[OWN, my_stats, :], sem_ps.at[6], sem_pr.at[6], twin),
    ]
    for cp in (pair[0], pair[6], pair[1]):
        cp.start()

    ag = {}
    for kv in (0, 1):
        for dst, target in ((YM, up), (YP, down), (ZZ, z_to)):
            ag[dst, kv] = [
                to(
                    ring_kv[kv].at[OWN, part[kv], :], ring_kv[kv].at[dst, part[kv], :],
                    s_sem.at[dst, kv], r_sem.at[dst, kv], target,
                )
                for part, s_sem, r_sem in (
                    (my_part, sem_as, sem_ar), (twin_part, sem_bs, sem_br),
                )
            ]
    ag_plan = (
        (YM, YY, 0, up), (YM, ZYM, 0, z_to), (YM, ZYM, 1, z_to),
        (YP, YY, 1, down), (ZZ, ZYP, 0, down), (ZZ, ZYP, 1, down),
        (ZYM, ZYY, 0, up), (ZYM, ZYY, 1, up),
    )
    for src, dst, kv, target in ag_plan:
        ag[dst, kv] = [
            to(ring_kv[kv].at[src], ring_kv[kv].at[dst], sem_as.at[dst, kv], sem_ar.at[dst, kv], target)
        ]

    for kv in (0, 1):
        local[kv].wait()
        for dst in (YM, YP, ZZ):
            ag[dst, kv][0].start()
    for cp in pair[2:6]:
        cp.start()
    for kv in (0, 1):
        pair[kv].wait_recv()
        if kv == 0:
            pair[6].wait_recv()
        for dst in (YM, YP, ZZ):
            ag[dst, kv][1].start()


    hops = []
    if ring == 4:
        hops += [((x_up, x_down), False), ((x_up,), True)]
    if n_grp > ring:
        hops.append(((across,), False))

    def hop_copies(n):
        targets, relay = hops[n]
        src = stat_in.at[n - 1, 1] if relay else stat_out.at[n]
        copies = []
        for i, target in enumerate(targets):
            slot = 1 - i if len(targets) == 2 else 0
            copies.append(
                to(src, stat_in.at[n, slot], sem_ss.at[n, slot], sem_sr.at[n, slot], target)
            )
        return copies

    def hop_start(n):
        for cp in hop_copies(n):
            cp.start()

    def hop_end(n):
        for cp in hop_copies(n):
            cp.wait_recv()
        total = stat_out[n]
        for slot in range(len(hops[n][0])):
            total = total + stat_in[n, slot]
        stat_out[n + 1] = total

    n_blocks = 8
    for i in (2, 3, 4):
        local[i].wait()
    own_block(0)

    for i in (2, 3, 4):
        pair[i].wait_recv()
    own_block(1)
    local[5].wait()
    pair[5].wait_recv()
    for r in range(2):
        turn(gn, gT, r)
    def keys_of(block, j):
        heads = slice(j * DH, (j + 1) * DH)
        return jnp.concatenate(
            [kn[block, 0:piece, heads], kn[block, tall:tall + piece, heads]], axis=0
        )

    def pass_on(waits, starts):
        for key in waits:
            for cp in ag[key]:
                cp.wait_recv()
        for key in starts:
            for cp in ag[key]:
                cp.start()

    @pl.loop(0, n_blocks)
    def forward_step(step):
        @pl.when(step == 1)
        def _():
            pass_on([(YM, 0)], [(YY, 0), (ZYM, 0)])
            pass_on([(ZZ, 0)], [(ZYP, 0)])
            pass_on([(YM, 1)], [(ZYM, 1)])
            pass_on([(YP, 0), (YP, 1)], [(YY, 1)])
            pass_on([(ZZ, 1)], [(ZYP, 1)])

        @pl.when(step == 3)
        def _():
            pass_on([(ZYM, 0)], [(ZYY, 0)])

        @pl.when(step == 4)
        def _():
            pass_on([(ZYM, 1)], [(ZYY, 1)])

        @pl.when(step == 5)
        def _():
            pass_on([(YY, 0), (YY, 1)], [])

        @pl.when(step == 6)
        def _():
            pass_on([(ZYP, 0), (ZYP, 1)], [])

        @pl.when(step == 7)
        def _():
            pass_on([(ZYY, 0), (ZYY, 1)], [])

        order = (0, 2, 1, 3)
        forward(
            order,
            {u: keys_of(step, u % 2) for u in order},
            {u: vn[step, :, (u % 2) * DH:(u % 2 + 1) * DH] for u in order},
            step, False,
        )

    sum_one = sum_two = live = jnp.zeros((1, 128), F32)
    for slot in range(n_blocks):
        for core in range(2):
            stat = kn[slot, core * tall + piece:(core + 1) * tall, 0:128].astype(F32)
            live = live + stat[0:1]
            sum_one = sum_one + stat[1:2]
            sum_two = sum_two + stat[1:2] * stat[1:2]
    stat_out[0] = jnp.broadcast_to(live, (8, 128))
    if hops:
        hop_start(0)
    n_resp = 16
    mean = sum_one / n_resp
    variance = (n_resp * sum_two - sum_one * sum_one) / (n_resp * n_resp)
    spread = jnp.maximum(jnp.sqrt(variance), 1.0)
    twin_stats = pl.ds(pl.multiple_of((1 - c) * tall + piece, 16), 16)
    for r in range(2):
        stat = stat_own[:, 0:128] if r == 0 else kn[OWN, twin_stats, 0:128]
        length = stat.astype(F32)[0:1].astype(jnp.int32)
        strength = (stat.astype(F32)[1:2] - mean) / spread
        weight = jnp.concatenate(
            [
                jnp.where(
                    lax.broadcasted_iota(jnp.int32, (1, 128), 1) + start < length, strength, 0.0
                )
                for start in range(0, rows, 128)
            ],
            axis=1,
        )
        for j in range(2):
            u = 2 * r + j
            for h in range(heads_per):
                cols = slice(h * rows, (h + 1) * rows)
                inv = 1.0 / l_cur[u:u + 1, cols]
                out = (acc[u, :, cols] * inv).astype(BF16)
                q2[u, 0:DH, cols] = out
                delta = jnp.sum(
                    out.astype(F32) * gT[u, :, cols].astype(F32), axis=0, keepdims=True
                )
                aux[0, u:u + 1, cols] = inv * weight
                aux[1, u:u + 1, cols] = delta
                dqa[u, :, cols] = jnp.zeros((DH, rows), F32)

    def backward(units, keys, values, block, place):
        flat = {u: k.T for u, k in keys.items()}
        todo = [(u, h, slice(h * rows, (h + 1) * rows)) for u in units for h in range(heads_per)]
        scaled, shift, dots, lows, sums = {}, {}, {}, {}, {}

        def start(i):
            u, h, cols = todo[i]
            factor = jnp.exp2(m_st[block, u:u + 1, cols] - m_cur[u:u + 1, cols])
            factor = factor * aux[0, u:u + 1, cols]
            scaled[i] = (gT[u, :, cols].astype(F32) * factor).astype(BF16)
            shift[i] = factor * aux[1, u:u + 1, cols]
            dots[i] = nn(values[u], scaled[i])

        def add(key, term):
            sums[key] = sums[key] + term if key in sums else term

        def finish(i):
            u, h, cols = todo[i]
            low = lows.pop(i)
            col = (u % 2) * heads_per + h
            dqa[u, :, cols] = dqa[u, :, cols] + nn(flat[u], low)
            add((place(u), 0), nn(low, qn[u // 2, :, col * DH:(col + 1) * DH]))
            add((place(u), 1), nt(scaled.pop(i), e_st[block, u, :, cols]))

        for i in range(2):
            start(i)
        for i, (u, h, cols) in enumerate(todo):
            if i + 2 < len(todo):
                start(i + 2)
            d = dots.pop(i) - shift.pop(i)
            lows[i] = (e_st[block, u, :, cols].astype(F32) * d).astype(BF16)
            if i >= 1:
                finish(i - 1)
        finish(len(todo) - 1)
        return {
            key: term.T * inv_root if key[1] == 0 else term for key, term in sums.items()
        }

    names = ("m1", "m6", "m3", "m2", "m7", "m5", "m4")
    route = {
        "m1": (down, down), "m6": (up, up), "m3": (down, up), "m2": (z_to, z_to),
        "m7": (z_to, z_to), "m5": (up, up), "m4": (down, down),
    }
    msg = {}
    for n, name in enumerate(names):
        for kv in range(2):
            msg[name, kv] = to(
                snd.at[n, kv], rcv.at[n, kv], sem_ms.at[n, kv], sem_mr.at[n, kv], route[name][kv]
            )

    needs = {
        0: ((), ()), 1: ((), ()), 2: ((), ()), 3: (("m1",), ("m1",)), 4: (("m6",), ("m6",)),
        5: ((), ("m3",)), 6: (("m2", "m3"), ("m2",)),
    }

    @pl.loop(0, n_blocks)
    def backward_step(step):
        for n in range(len(hops)):
            @pl.when(step == 2 * (n + 1))
            def _():
                hop_end(n)
                if n + 1 < len(hops):
                    hop_start(n + 1)

        block = n_blocks - 1 - step
        order = (0, 2, 1, 3)
        sums = backward(
            order,
            {u: keys_of(block, u % 2) for u in order},
            {u: vn[block, :, (u % 2) * DH:(u % 2 + 1) * DH] for u in order},
            block, lambda u: u % 2,
        )
        total_heads = 4 * heads_per
        for i in range(3):
            head = jnp.minimum(3 * step + i, total_heads - 1)
            u = head // heads_per
            h = head % heads_per
            col = pl.multiple_of(((u % 2) * heads_per + h) * DH, DH)
            att_n[u // 2, :, pl.ds(col, DH)] = q2[
                u, 0:DH, pl.ds(pl.multiple_of(h * rows, rows), rows)
            ].T
        for (j, kv), term in sums.items():
            own_part[kv, j * DH:(j + 1) * DH, :] = term

        for n, name in enumerate(names):
            @pl.when(step == n)
            def _():
                for kv in range(2):
                    total = own_part[kv]
                    for other in needs[n][kv]:
                        msg[other, kv].wait_recv()
                        total = total + rcv[names.index(other), kv].astype(F32)
                    snd[n, kv] = total.astype(BF16)
                    msg[name, kv].start()

    att_own = pltpu.make_async_copy(att_n.at[0], att_hbm.at[0, 0, :, cq], sem_ol.at[0])
    att_twin = to(att_n.at[1], att_hbm.at[0, 0, :, cq], sem_os.at[0], sem_or.at[0], twin)
    att_own.start()
    att_twin.start()

    norm = (n_grp * n_resp * rows) / stat_out[len(hops), 0:1, :]
    norm_rows = jnp.concatenate([norm] * (rows // 128), axis=1)

    outs_own = [
        pltpu.make_async_copy(rg_n.at[0, 0], drk_hbm.at[0, 0, :, ck], sem_ol.at[1]),
        pltpu.make_async_copy(rg_n.at[0, 1], drv_hbm.at[0, 0, :, ck], sem_ol.at[2]),
        pltpu.make_async_copy(dq_n.at[0], dq_hbm.at[0, 0, :, cq], sem_ol.at[3]),
    ]
    outs_twin = [
        to(rg_n.at[1, 0], drk_hbm.at[0, 0, :, ck], sem_os.at[1], sem_or.at[1], twin),
        to(rg_n.at[1, 1], drv_hbm.at[0, 0, :, ck], sem_os.at[2], sem_or.at[2], twin),
        to(dq_n.at[1], dq_hbm.at[0, 0, :, cq], sem_os.at[3], sem_or.at[3], twin),
    ]
    for r in (1, 0):
        units = (2 * r, 2 * r + 1)
        sums = backward(
            units,
            {u: rkn[r, :, (u % 2) * DH:(u % 2 + 1) * DH] for u in units},
            {u: rvn[r, :, (u % 2) * DH:(u % 2 + 1) * DH] for u in units},
            n_blocks, lambda u: u,
        )
        for j in range(2):
            for h in range(heads_per):
                col = slice((j * heads_per + h) * DH, (j * heads_per + h + 1) * DH)
                grad = dqa[2 * r + j, :, h * rows:(h + 1) * rows] * (norm_rows * inv_root)
                dq_n[r, :, col] = grad.astype(BF16).T
        for (u, kv), term in sums.items():
            rg_n[r, kv, :, (u % 2) * DH:(u % 2 + 1) * DH] = (term * norm_rows).astype(BF16).T
        for cp in outs_twin if r else outs_own:
            cp.start()

    twin_rows = pl.ds(pl.multiple_of((1 - c) * piece, piece), piece)
    for kv, out in enumerate((dpk_hbm, dpv_hbm)):
        total = own_part[kv]
        for name in ("m5", "m7", "m4"):
            msg[name, kv].wait_recv()
            total = total + rcv[names.index(name), kv].astype(F32)
        pg_n[kv] = (total * norm_rows).astype(BF16).T
        outs_own.append(
            pltpu.make_async_copy(pg_n.at[kv, my_rows, :], out.at[0, :, ck], sem_ol.at[4 + kv])
        )
        outs_twin.append(
            to(
                pg_n.at[kv, twin_rows, :], out.at[0, :, ck],
                sem_os.at[4 + kv], sem_or.at[4 + kv], twin,
            )
        )
        outs_twin[-1].start()
        outs_own[-1].start()

    for cp in [att_own] + outs_own:
        cp.wait()
    for cp in [att_twin] + outs_twin:
        cp.wait()
    stats = [cp for n in range(len(hops)) for cp in hop_copies(n)]
    for cp in pair + stats + sum(ag.values(), []) + list(msg.values()):
        cp.wait_send()


def finish(*refs):
    ins, outs, bufs, (sem_in, sem_out) = refs[:6], refs[6:12], refs[12:18], refs[18:]
    loads, stores = [], []
    for src, dst, buf in zip(ins, outs, bufs):
        total = src.shape[-2]
        pieces = 4 if src.shape[-1] > 1024 else 1
        step = total // pieces
        lead = (0,) * (len(src.shape) - 2)
        for i in range(pieces):
            part = lead + (pl.ds(i * step, step),)
            n = len(loads)
            loads.append(pltpu.make_async_copy(src.at[part], buf.at[part], sem_in.at[n]))
            stores.append(pltpu.make_async_copy(buf.at[part], dst.at[part], sem_out.at[n]))
            loads[-1].start()
    for load, store in zip(loads, stores):
        load.wait()
        store.start()
    for store in stores:
        store.wait()


def on_device(n_grp, queries, resp_keys, resp_values, prompt_keys, prompt_values, out_grad,
              lengths, rewards):
    rows = queries.shape[2]
    half_q = queries.shape[3] // 2
    half_k = resp_keys.shape[3] // 2
    heads_per = half_q // half_k
    piece = prompt_keys.shape[1]
    blk = 2 * piece
    width = heads_per * rows
    anywhere = pl.BlockSpec(memory_space=pl.ANY)
    dma = pltpu.SemaphoreType.DMA
    vmem = pltpu.VMEM
    scratch = [
        vmem((2, rows, half_q), BF16), vmem((2, rows, half_q), BF16),
        vmem((2, rows, half_k), BF16), vmem((2, rows, half_k), BF16),
        vmem((8, blk + 32, half_k), BF16), vmem((8, blk, half_k), BF16),
        vmem((16, half_k), BF16),
        vmem((4, DH, width), BF16), vmem((4, 2 * DH, width), BF16), vmem((4, DH, width), BF16),
        vmem((9, 4, blk, width), BF16),
        vmem((9, 8, width), F32), vmem((8, width), F32), vmem((8, width), F32),
        vmem((4, DH, width), F32), vmem((4, DH, width), F32),
        vmem((2, 8, width), F32),
        vmem((8, 8, 128), F32), vmem((8, 2, 8, 128), F32),
        vmem((7, 2, half_k, blk), BF16), vmem((7, 2, half_k, blk), BF16),
        vmem((2, half_k, blk), F32),
        vmem((2, rows, half_q), BF16), vmem((2, rows, half_q), BF16),
        vmem((2, 2, rows, half_k), BF16), vmem((2, blk, half_k), BF16),
        dma((6,)), dma((7,)), dma((7,)), dma((8, 2)), dma((8, 2)),
        dma((8, 2)), dma((8, 2)),
        dma((8, 2)), dma((8, 2)),
        dma((7, 2)), dma((7, 2)), dma((6,)), dma((6,)), dma((6,)),
    ]
    like = lambda a: jax.ShapeDtypeStruct(a.shape, a.dtype)
    shapes = (
        like(queries), like(queries), like(resp_keys), like(resp_values),
        like(prompt_keys), like(prompt_values),
    )
    results = pl.pallas_call(
        lambda *refs: kernel(n_grp, heads_per, *refs),
        out_shape=shapes,
        in_specs=[anywhere] * 6 + [pl.BlockSpec(memory_space=pltpu.VMEM)] * 2,
        out_specs=(anywhere,) * 6,
        scratch_shapes=scratch,
        compiler_params=pltpu.CompilerParams(
            collective_id=0, has_side_effects=True, vmem_limit_bytes=60 * 2**20
        ),
        name="grpo_attention",
    )(queries, resp_keys, resp_values, prompt_keys, prompt_values, out_grad, lengths, rewards)
    return pl.pallas_call(
        finish,
        out_shape=shapes,
        in_specs=[anywhere] * 6,
        out_specs=(anywhere,) * 6,
        scratch_shapes=[vmem(x.shape, x.dtype) for x in shapes] + [dma((12,)), dma((12,))],
        compiler_params=pltpu.CompilerParams(vmem_limit_bytes=60 * 2**20),
        name="write_results",
    )(*results)


def solution(mesh):
    n_grp = mesh.shape["grp"]
    wide = P("grp", "resp", None, None)
    tall = P("grp", "resp", None)
    return jax.shard_map(
        lambda *arrays: on_device(n_grp, *arrays),
        mesh=mesh,
        in_specs=(wide, wide, wide, tall, tall, wide, P("grp", "resp"), P("grp", "resp")),
        out_specs=(wide, wide, wide, wide, tall, tall),
        check_vma=False,
    )
```

```python
import math

import jax
import jax.numpy as jnp
from jax import lax
from jax.experimental import pallas as pl
from jax.experimental.pallas import tpu as pltpu
from jax.sharding import PartitionSpec as P

DH = 128
F32 = jnp.float32
BF16 = jnp.bfloat16
MESH = pl.DeviceIdType.MESH

SLOTS = ((0, 0), (0, 3), (0, 1), (1, 0), (1, 3), (0, 2), (1, 1), (1, 2))
OWN, YM, YP, ZZ, ZYM, YY, ZYP, ZYY = range(8)


def nn(a, b):
    return jnp.dot(a, b, preferred_element_type=F32)


def nt(a, b):
    return lax.dot_general(a, b, (((1,), (1,)), ((), ())), preferred_element_type=F32)


def kernel(
    n_grp, heads_per, q_hbm, rk_hbm, rv_hbm, pk_hbm, pv_hbm, og_hbm, len_ref, rew_ref,
    att_hbm, dq_hbm, drk_hbm, drv_hbm, dpk_hbm, dpv_hbm,
    qn, gn, rkn, rvn, kn, vn, stat_own, qT, q2, gT, e_st, m_st, m_cur, l_cur, acc, dqa, aux,
    stat_out, stat_in, snd, rcv, own_part, att_n, dq_n, rg_n, pg_n,
    sem_l, sem_ps, sem_pr, sem_as, sem_ar, sem_bs, sem_br, sem_ss, sem_sr,
    sem_ms, sem_mr, sem_ol, sem_os, sem_or,
):
    rows = qn.shape[1]
    half_q = qn.shape[2]
    half_k = rkn.shape[2]
    piece = pk_hbm.shape[1]
    blk = 2 * piece
    width = heads_per * rows
    inv_root = DH ** (-0.5)
    scale2 = inv_root * math.log2(math.e)
    me = lax.axis_index("resp")
    grp = lax.axis_index("grp")
    z = me // 8
    y = (me // 2) % 4
    c = me % 2

    def at(dz, dy, dc):
        return {"resp": ((z + dz) % 2) * 8 + ((y + dy) % 4) * 2 + (c + dc) % 2}

    def to(src, dst, s_sem, r_sem, target):
        return pltpu.make_async_remote_copy(
            src_ref=src, dst_ref=dst, send_sem=s_sem, recv_sem=r_sem,
            device_id=target, device_id_type=MESH,
        )

    cq = pl.ds(pl.multiple_of(c * half_q, half_q), half_q)
    oq = pl.ds(pl.multiple_of((1 - c) * half_q, half_q), half_q)
    ck = pl.ds(pl.multiple_of(c * half_k, half_k), half_k)
    ok = pl.ds(pl.multiple_of((1 - c) * half_k, half_k), half_k)
    my_rows = pl.ds(pl.multiple_of(c * piece, piece), piece)
    tall = piece + 16
    my_keys = pl.ds(pl.multiple_of(c * tall, 16), piece)
    my_stats = pl.ds(pl.multiple_of(c * tall + piece, 16), 16)
    my_part, twin_part = [
        [pl.ds(pl.multiple_of(k * size, 16), size) for size in (tall, piece)] for k in (c, 1 - c)
    ]
    ring_kv = (kn, vn)

    local = [
        pltpu.make_async_copy(pk_hbm.at[0, :, ck], kn.at[OWN, my_keys, :], sem_l.at[0]),
        pltpu.make_async_copy(pv_hbm.at[0, :, ck], vn.at[OWN, my_rows, :], sem_l.at[1]),
        pltpu.make_async_copy(q_hbm.at[0, 0, :, cq], qn.at[0], sem_l.at[2]),
        pltpu.make_async_copy(rk_hbm.at[0, 0, :, ck], rkn.at[0], sem_l.at[3]),
        pltpu.make_async_copy(rv_hbm.at[0, 0, :, ck], rvn.at[0], sem_l.at[4]),
        pltpu.make_async_copy(og_hbm.at[0, 0, :, cq], gn.at[0], sem_l.at[5]),
    ]
    for cp in local:
        cp.start()

    twin = at(0, 0, 1)
    z_to, up, down = at(1, 0, 0), at(0, 1, 0), at(0, 3, 0)
    ring = min(4, n_grp)
    base = (grp // ring) * ring
    x_up = {"grp": base + (grp - base + 1) % ring}
    x_down = {"grp": base + (grp - base + ring - 1) % ring}
    across = {"grp": (grp + ring) % n_grp}
    friends = [twin, z_to, up, down]
    if ring == 4:
        friends += [x_up, x_down]
    if n_grp > ring:
        friends.append(across)
    barrier = pltpu.get_barrier_semaphore()
    for friend in friends:
        pl.semaphore_signal(barrier, inc=1, device_id=friend, device_id_type=MESH)

    def turn(src, dst, r):
        for j in range(2):
            for h in range(heads_per):
                dst[2 * r + j, :, h * rows:(h + 1) * rows] = src[
                    r, :, (j * heads_per + h) * DH:(j * heads_per + h + 1) * DH
                ].T

    def split_queries(r):
        for u in (2 * r, 2 * r + 1):
            for h in range(heads_per):
                cols = slice(h * rows, (h + 1) * rows)
                full = qT[u, :, cols].astype(F32) * scale2
                high = full.astype(BF16)
                q2[u, 0:DH, cols] = high
                q2[u, DH:2 * DH, cols] = (full - high.astype(F32)).astype(BF16)

    ones = jnp.ones((16, blk), BF16)

    def forward(units, keys, values, block, first):
        keys = {u: jnp.concatenate([k, k], axis=1) for u, k in keys.items()}
        values = {u: jnp.concatenate([v.T, ones], axis=0) for u, v in values.items()}
        todo = [(u, slice(h * rows, (h + 1) * rows)) for u in units for h in range(heads_per)]
        logits, lows = {}, {}

        def start(i):
            u, cols = todo[i]
            logits[i] = nn(keys[u], q2[u, :, cols])

        def finish(i):
            u, cols = todo[i]
            low, alpha = lows.pop(i)
            part = nn(values[u], low)
            if first:
                l_cur[u:u + 1, cols] = part[DH:DH + 1]
                acc[u, :, cols] = part[0:DH]
            else:
                l_cur[u:u + 1, cols] = l_cur[u:u + 1, cols] * alpha + part[DH:DH + 1]
                acc[u, :, cols] = acc[u, :, cols] * alpha + part[0:DH]

        for i in range(3):
            start(i)
        for i, (u, cols) in enumerate(todo):
            if i + 3 < len(todo):
                start(i + 3)
            s = logits.pop(i)
            if first:
                seen = lax.broadcasted_iota(jnp.int32, s.shape, 0) <= (
                    lax.broadcasted_iota(jnp.int32, s.shape, 1)
                )
                s = jnp.where(seen, s, -jnp.inf)
                m_new = jnp.max(s, axis=0, keepdims=True)
                alpha = None
            else:
                m_old = m_cur[u:u + 1, cols]
                m_new = jnp.maximum(m_old, jnp.max(s, axis=0, keepdims=True))
                alpha = jnp.exp2(m_old - m_new)
            low = jnp.exp2(s - m_new).astype(BF16)
            e_st[block, u, :, cols] = low
            m_cur[u:u + 1, cols] = m_new
            m_st[block, u:u + 1, cols] = m_new
            lows[i] = (low, alpha)
            if i >= 2:
                finish(i - 2)
        for i in sorted(lows):
            finish(i)

    def own_block(r):
        turn(qn, qT, r)
        split_queries(r)
        units = (2 * r, 2 * r + 1)
        forward(
            units,
            {u: rkn[r, :, (u % 2) * DH:(u % 2 + 1) * DH] for u in units},
            {u: rvn[r, :, (u % 2) * DH:(u % 2 + 1) * DH] for u in units},
            n_blocks, True,
        )

    row_id = lax.broadcasted_iota(jnp.int32, stat_own.shape, 0)
    stat_own[...] = jnp.where(
        row_id == 0,
        jnp.broadcast_to(len_ref[...], stat_own.shape),
        jnp.broadcast_to(rew_ref[...], stat_own.shape),
    ).astype(F32).astype(BF16)
    kn[OWN, my_stats, :] = stat_own[...]
    pl.semaphore_wait(barrier, len(friends))

    pair = [
        to(pk_hbm.at[0, :, ok], kn.at[OWN, my_keys, :], sem_ps.at[0], sem_pr.at[0], twin),
        to(pv_hbm.at[0, :, ok], vn.at[OWN, my_rows, :], sem_ps.at[1], sem_pr.at[1], twin),
        to(q_hbm.at[0, 0, :, oq], qn.at[1], sem_ps.at[2], sem_pr.at[2], twin),
        to(rk_hbm.at[0, 0, :, ok], rkn.at[1], sem_ps.at[3], sem_pr.at[3], twin),
        to(rv_hbm.at[0, 0, :, ok], rvn.at[1], sem_ps.at[4], sem_pr.at[4], twin),
        to(og_hbm.at[0, 0, :, oq], gn.at[1], sem_ps.at[5], sem_pr.at[5], twin),
        to(stat_own, kn.at[OWN, my_stats, :], sem_ps.at[6], sem_pr.at[6], twin),
    ]
    for cp in (pair[0], pair[6], pair[1]):
        cp.start()

    ag = {}
    for kv in (0, 1):
        for dst, target in ((YM, up), (YP, down), (ZZ, z_to)):
            ag[dst, kv] = [
                to(
                    ring_kv[kv].at[OWN, part[kv], :], ring_kv[kv].at[dst, part[kv], :],
                    s_sem.at[dst, kv], r_sem.at[dst, kv], target,
                )
                for part, s_sem, r_sem in (
                    (my_part, sem_as, sem_ar), (twin_part, sem_bs, sem_br),
                )
            ]
    ag_plan = (
        (YM, YY, 0, up), (YM, ZYM, 0, z_to), (YM, ZYM, 1, z_to),
        (YP, YY, 1, down), (ZZ, ZYP, 0, down), (ZZ, ZYP, 1, down),
        (ZYM, ZYY, 0, up), (ZYM, ZYY, 1, up),
    )
    for src, dst, kv, target in ag_plan:
        ag[dst, kv] = [
            to(ring_kv[kv].at[src], ring_kv[kv].at[dst], sem_as.at[dst, kv], sem_ar.at[dst, kv], target)
        ]

    for kv in (0, 1):
        local[kv].wait()
        for dst in (YM, YP, ZZ):
            ag[dst, kv][0].start()
    for cp in pair[2:6]:
        cp.start()
    for kv in (0, 1):
        pair[kv].wait_recv()
        if kv == 0:
            pair[6].wait_recv()
        for dst in (YM, YP, ZZ):
            ag[dst, kv][1].start()


    hops = []
    if ring == 4:
        hops += [((x_up, x_down), False), ((x_up,), True)]
    if n_grp > ring:
        hops.append(((across,), False))
    n_cross = len(hops)
    hops += [((twin,), False), ((z_to,), False), ((up, down), False), ((up,), True)]
    hop_marks = (-2, -1, 3, 4, 5, 6, 8)[3 - n_cross:]

    def hop_at(mark):
        for n, own_mark in enumerate(hop_marks):
            if own_mark == mark:
                hop_end(n)
                if n + 1 < len(hops):
                    hop_start(n + 1)

    def hop_copies(n):
        targets, relay = hops[n]
        src = stat_in.at[n - 1, 1] if relay else stat_out.at[n]
        copies = []
        for i, target in enumerate(targets):
            slot = 1 - i if len(targets) == 2 else 0
            copies.append(
                to(src, stat_in.at[n, slot], sem_ss.at[n, slot], sem_sr.at[n, slot], target)
            )
        return copies

    def hop_start(n):
        for cp in hop_copies(n):
            cp.start()

    def hop_end(n):
        for cp in hop_copies(n):
            cp.wait_recv()
        total = stat_out[n]
        for slot in range(len(hops[n][0])):
            total = total + stat_in[n, slot]
        stat_out[n + 1] = total

    stat_out[0] = jnp.broadcast_to(len_ref[...], (8, 128)).astype(F32)
    hop_start(0)

    n_blocks = 8
    for i in (2, 3, 4):
        local[i].wait()
    own_block(0)

    for i in (2, 3, 4):
        pair[i].wait_recv()
    own_block(1)
    local[5].wait()
    pair[5].wait_recv()
    for r in range(2):
        turn(gn, gT, r)
    hop_at(-2)
    def keys_of(block, j):
        heads = slice(j * DH, (j + 1) * DH)
        return jnp.concatenate(
            [kn[block, 0:piece, heads], kn[block, tall:tall + piece, heads]], axis=0
        )

    def pass_on(waits, starts):
        for key in waits:
            for cp in ag[key]:
                cp.wait_recv()
        for key in starts:
            for cp in ag[key]:
                cp.start()

    @pl.loop(0, n_blocks)
    def forward_step(step):
        @pl.when(step == 1)
        def _():
            pass_on([(YM, 0)], [(YY, 0), (ZYM, 0)])
            pass_on([(ZZ, 0)], [(ZYP, 0)])
            pass_on([(YM, 1)], [(ZYM, 1)])
            pass_on([(YP, 0), (YP, 1)], [(YY, 1)])
            pass_on([(ZZ, 1)], [(ZYP, 1)])

        @pl.when(step == 3)
        def _():
            pass_on([(ZYM, 0)], [(ZYY, 0)])

        @pl.when(step == 4)
        def _():
            pass_on([(ZYM, 1)], [(ZYY, 1)])

        @pl.when(step == 5)
        def _():
            pass_on([(YY, 0), (YY, 1)], [])

        @pl.when(step == 6)
        def _():
            pass_on([(ZYP, 0), (ZYP, 1)], [])

        @pl.when(step == 7)
        def _():
            pass_on([(ZYY, 0), (ZYY, 1)], [])

        order = (0, 2, 1, 3)
        forward(
            order,
            {u: keys_of(step, u % 2) for u in order},
            {u: vn[step, :, (u % 2) * DH:(u % 2 + 1) * DH] for u in order},
            step, False,
        )

    hop_at(-1)
    sum_one = sum_two = jnp.zeros((1, 128), F32)
    for slot in range(n_blocks):
        for core in range(2):
            stat = kn[slot, core * tall + piece:(core + 1) * tall, 0:128].astype(F32)
            sum_one = sum_one + stat[1:2]
            sum_two = sum_two + stat[1:2] * stat[1:2]
    n_resp = 16
    mean = sum_one / n_resp
    variance = (n_resp * sum_two - sum_one * sum_one) / (n_resp * n_resp)
    spread = jnp.maximum(jnp.sqrt(variance), 1.0)
    twin_stats = pl.ds(pl.multiple_of((1 - c) * tall + piece, 16), 16)
    for r in range(2):
        stat = stat_own[:, 0:128] if r == 0 else kn[OWN, twin_stats, 0:128]
        length = stat.astype(F32)[0:1].astype(jnp.int32)
        strength = (stat.astype(F32)[1:2] - mean) / spread
        weight = jnp.concatenate(
            [
                jnp.where(
                    lax.broadcasted_iota(jnp.int32, (1, 128), 1) + start < length, strength, 0.0
                )
                for start in range(0, rows, 128)
            ],
            axis=1,
        )
        for j in range(2):
            u = 2 * r + j
            for h in range(heads_per):
                cols = slice(h * rows, (h + 1) * rows)
                inv = 1.0 / l_cur[u:u + 1, cols]
                out = (acc[u, :, cols] * inv).astype(BF16)
                q2[u, 0:DH, cols] = out
                delta = jnp.sum(
                    out.astype(F32) * gT[u, :, cols].astype(F32), axis=0, keepdims=True
                )
                aux[0, u:u + 1, cols] = inv * weight
                aux[1, u:u + 1, cols] = delta
                dqa[u, :, cols] = jnp.zeros((DH, rows), F32)

    def backward(units, keys, values, block, place):
        flat = {u: k.T for u, k in keys.items()}
        todo = [(u, h, slice(h * rows, (h + 1) * rows)) for u in units for h in range(heads_per)]
        scaled, shift, dots, lows, sums = {}, {}, {}, {}, {}

        def start(i):
            u, h, cols = todo[i]
            factor = jnp.exp2(m_st[block, u:u + 1, cols] - m_cur[u:u + 1, cols])
            factor = factor * aux[0, u:u + 1, cols]
            scaled[i] = (gT[u, :, cols].astype(F32) * factor).astype(BF16)
            shift[i] = factor * aux[1, u:u + 1, cols]
            dots[i] = nn(values[u], scaled[i])

        def add(key, term):
            sums[key] = sums[key] + term if key in sums else term

        def finish(i):
            u, h, cols = todo[i]
            low = lows.pop(i)
            col = (u % 2) * heads_per + h
            dqa[u, :, cols] = dqa[u, :, cols] + nn(flat[u], low)
            add((place(u), 0), nn(low, qn[u // 2, :, col * DH:(col + 1) * DH]))
            add((place(u), 1), nt(scaled.pop(i), e_st[block, u, :, cols]))

        for i in range(2):
            start(i)
        for i, (u, h, cols) in enumerate(todo):
            if i + 2 < len(todo):
                start(i + 2)
            d = dots.pop(i) - shift.pop(i)
            lows[i] = (e_st[block, u, :, cols].astype(F32) * d).astype(BF16)
            if i >= 1:
                finish(i - 1)
        finish(len(todo) - 1)
        return {
            key: term.T * inv_root if key[1] == 0 else term for key, term in sums.items()
        }

    names = ("m1", "m6", "m3", "m2", "m7", "m5", "m4")
    route = {
        "m1": (down, down), "m6": (up, up), "m3": (down, up), "m2": (z_to, z_to),
        "m7": (z_to, z_to), "m5": (up, up), "m4": (down, down),
    }
    msg = {}
    for n, name in enumerate(names):
        for kv in range(2):
            msg[name, kv] = to(
                snd.at[n, kv], rcv.at[n, kv], sem_ms.at[n, kv], sem_mr.at[n, kv], route[name][kv]
            )

    needs = {
        0: ((), ()), 1: ((), ()), 2: ((), ()), 3: (("m1",), ("m1",)), 4: (("m6",), ("m6",)),
        5: ((), ("m3",)), 6: (("m2", "m3"), ("m2",)),
    }

    @pl.loop(0, n_blocks)
    def backward_step(step):
        for mark in hop_marks:
            if 0 <= mark < n_blocks:
                @pl.when(step == mark)
                def _():
                    hop_at(mark)

        block = n_blocks - 1 - step
        order = (0, 2, 1, 3)
        sums = backward(
            order,
            {u: keys_of(block, u % 2) for u in order},
            {u: vn[block, :, (u % 2) * DH:(u % 2 + 1) * DH] for u in order},
            block, lambda u: u % 2,
        )
        total_heads = 4 * heads_per
        for i in range(3):
            head = jnp.minimum(3 * step + i, total_heads - 1)
            u = head // heads_per
            h = head % heads_per
            col = pl.multiple_of(((u % 2) * heads_per + h) * DH, DH)
            att_n[u // 2, :, pl.ds(col, DH)] = q2[
                u, 0:DH, pl.ds(pl.multiple_of(h * rows, rows), rows)
            ].T
        for (j, kv), term in sums.items():
            own_part[kv, j * DH:(j + 1) * DH, :] = term

        for n, name in enumerate(names):
            @pl.when(step == n)
            def _():
                for kv in range(2):
                    total = own_part[kv]
                    for other in needs[n][kv]:
                        msg[other, kv].wait_recv()
                        total = total + rcv[names.index(other), kv].astype(F32)
                    snd[n, kv] = total.astype(BF16)
                    msg[name, kv].start()

    att_own = pltpu.make_async_copy(att_n.at[0], att_hbm.at[0, 0, :, cq], sem_ol.at[0])
    att_twin = to(att_n.at[1], att_hbm.at[0, 0, :, cq], sem_os.at[0], sem_or.at[0], twin)
    att_own.start()
    att_twin.start()

    outs_own = [
        pltpu.make_async_copy(rg_n.at[0, 0], drk_hbm.at[0, 0, :, ck], sem_ol.at[1]),
        pltpu.make_async_copy(rg_n.at[0, 1], drv_hbm.at[0, 0, :, ck], sem_ol.at[2]),
        pltpu.make_async_copy(dq_n.at[0], dq_hbm.at[0, 0, :, cq], sem_ol.at[3]),
    ]
    outs_twin = [
        to(rg_n.at[1, 0], drk_hbm.at[0, 0, :, ck], sem_os.at[1], sem_or.at[1], twin),
        to(rg_n.at[1, 1], drv_hbm.at[0, 0, :, ck], sem_os.at[2], sem_or.at[2], twin),
        to(dq_n.at[1], dq_hbm.at[0, 0, :, cq], sem_os.at[3], sem_or.at[3], twin),
    ]
    for r in (1, 0):
        units = (2 * r, 2 * r + 1)
        sums = backward(
            units,
            {u: rkn[r, :, (u % 2) * DH:(u % 2 + 1) * DH] for u in units},
            {u: rvn[r, :, (u % 2) * DH:(u % 2 + 1) * DH] for u in units},
            n_blocks, lambda u: u,
        )
        if r == 1:
            hop_at(n_blocks)
            norm = (n_grp * n_resp * rows) / stat_out[len(hops), 0:1, :]
            norm_rows = jnp.concatenate([norm] * (rows // 128), axis=1)
        for j in range(2):
            for h in range(heads_per):
                col = slice((j * heads_per + h) * DH, (j * heads_per + h + 1) * DH)
                grad = dqa[2 * r + j, :, h * rows:(h + 1) * rows] * (norm_rows * inv_root)
                dq_n[r, :, col] = grad.astype(BF16).T
        for (u, kv), term in sums.items():
            rg_n[r, kv, :, (u % 2) * DH:(u % 2 + 1) * DH] = (term * norm_rows).astype(BF16).T
        for cp in outs_twin if r else outs_own:
            cp.start()

    twin_rows = pl.ds(pl.multiple_of((1 - c) * piece, piece), piece)
    for kv, out in enumerate((dpk_hbm, dpv_hbm)):
        total = own_part[kv]
        for name in ("m5", "m7", "m4"):
            msg[name, kv].wait_recv()
            total = total + rcv[names.index(name), kv].astype(F32)
        pg_n[kv] = (total * norm_rows).astype(BF16).T
        outs_own.append(
            pltpu.make_async_copy(pg_n.at[kv, my_rows, :], out.at[0, :, ck], sem_ol.at[4 + kv])
        )
        outs_twin.append(
            to(
                pg_n.at[kv, twin_rows, :], out.at[0, :, ck],
                sem_os.at[4 + kv], sem_or.at[4 + kv], twin,
            )
        )
        outs_twin[-1].start()
        outs_own[-1].start()

    for cp in [att_own] + outs_own:
        cp.wait()
    for cp in [att_twin] + outs_twin:
        cp.wait()
    stats = [cp for n in range(len(hops)) for cp in hop_copies(n)]
    for cp in pair + stats + sum(ag.values(), []) + list(msg.values()):
        cp.wait_send()


def finish(*refs):
    ins, outs, bufs, (sem_in, sem_out) = refs[:6], refs[6:12], refs[12:18], refs[18:]
    loads, stores = [], []
    for src, dst, buf in zip(ins, outs, bufs):
        total = src.shape[-2]
        pieces = 4 if src.shape[-1] > 1024 else 1
        step = total // pieces
        lead = (0,) * (len(src.shape) - 2)
        for i in range(pieces):
            part = lead + (pl.ds(i * step, step),)
            n = len(loads)
            loads.append(pltpu.make_async_copy(src.at[part], buf.at[part], sem_in.at[n]))
            stores.append(pltpu.make_async_copy(buf.at[part], dst.at[part], sem_out.at[n]))
            loads[-1].start()
    for load, store in zip(loads, stores):
        load.wait()
        store.start()
    for store in stores:
        store.wait()


def on_device(n_grp, queries, resp_keys, resp_values, prompt_keys, prompt_values, out_grad,
              lengths, rewards):
    rows = queries.shape[2]
    half_q = queries.shape[3] // 2
    half_k = resp_keys.shape[3] // 2
    heads_per = half_q // half_k
    piece = prompt_keys.shape[1]
    blk = 2 * piece
    width = heads_per * rows
    anywhere = pl.BlockSpec(memory_space=pl.ANY)
    dma = pltpu.SemaphoreType.DMA
    vmem = pltpu.VMEM
    scratch = [
        vmem((2, rows, half_q), BF16), vmem((2, rows, half_q), BF16),
        vmem((2, rows, half_k), BF16), vmem((2, rows, half_k), BF16),
        vmem((8, blk + 32, half_k), BF16), vmem((8, blk, half_k), BF16),
        vmem((16, half_k), BF16),
        vmem((4, DH, width), BF16), vmem((4, 2 * DH, width), BF16), vmem((4, DH, width), BF16),
        vmem((9, 4, blk, width), BF16),
        vmem((9, 8, width), F32), vmem((8, width), F32), vmem((8, width), F32),
        vmem((4, DH, width), F32), vmem((4, DH, width), F32),
        vmem((2, 8, width), F32),
        vmem((8, 8, 128), F32), vmem((8, 2, 8, 128), F32),
        vmem((7, 2, half_k, blk), BF16), vmem((7, 2, half_k, blk), BF16),
        vmem((2, half_k, blk), F32),
        vmem((2, rows, half_q), BF16), vmem((2, rows, half_q), BF16),
        vmem((2, 2, rows, half_k), BF16), vmem((2, blk, half_k), BF16),
        dma((6,)), dma((7,)), dma((7,)), dma((8, 2)), dma((8, 2)),
        dma((8, 2)), dma((8, 2)),
        dma((8, 2)), dma((8, 2)),
        dma((7, 2)), dma((7, 2)), dma((6,)), dma((6,)), dma((6,)),
    ]
    like = lambda a: jax.ShapeDtypeStruct(a.shape, a.dtype)
    shapes = (
        like(queries), like(queries), like(resp_keys), like(resp_values),
        like(prompt_keys), like(prompt_values),
    )
    results = pl.pallas_call(
        lambda *refs: kernel(n_grp, heads_per, *refs),
        out_shape=shapes,
        in_specs=[anywhere] * 6 + [pl.BlockSpec(memory_space=pltpu.VMEM)] * 2,
        out_specs=(anywhere,) * 6,
        scratch_shapes=scratch,
        compiler_params=pltpu.CompilerParams(
            collective_id=0, has_side_effects=True, vmem_limit_bytes=60 * 2**20
        ),
        name="grpo_attention",
    )(queries, resp_keys, resp_values, prompt_keys, prompt_values, out_grad, lengths, rewards)
    return pl.pallas_call(
        finish,
        out_shape=shapes,
        in_specs=[anywhere] * 6,
        out_specs=(anywhere,) * 6,
        scratch_shapes=[vmem(x.shape, x.dtype) for x in shapes] + [dma((12,)), dma((12,))],
        compiler_params=pltpu.CompilerParams(vmem_limit_bytes=60 * 2**20),
        name="write_results",
    )(*results)


def solution(mesh):
    n_grp = mesh.shape["grp"]
    wide = P("grp", "resp", None, None)
    tall = P("grp", "resp", None)
    return jax.shard_map(
        lambda *arrays: on_device(n_grp, *arrays),
        mesh=mesh,
        in_specs=(wide, wide, wide, tall, tall, wide, P("grp", "resp"), P("grp", "resp")),
        out_specs=(wide, wide, wide, wide, tall, tall),
        check_vma=False,
    )
```

```python
import math

import jax
import jax.numpy as jnp
from jax import lax
from jax.experimental import pallas as pl
from jax.experimental.pallas import tpu as pltpu
from jax.sharding import PartitionSpec as P

DH = 128
F32 = jnp.float32
BF16 = jnp.bfloat16
MESH = pl.DeviceIdType.MESH

SLOTS = ((0, 0), (0, 3), (0, 1), (1, 0), (1, 3), (0, 2), (1, 1), (1, 2))
OWN, YM, YP, ZZ, ZYM, YY, ZYP, ZYY = range(8)


def nn(a, b):
    return jnp.dot(a, b, preferred_element_type=F32)


def nt(a, b):
    return lax.dot_general(a, b, (((1,), (1,)), ((), ())), preferred_element_type=F32)


def kernel(
    n_grp, heads_per, q_hbm, rk_hbm, rv_hbm, pk_hbm, pv_hbm, og_hbm, len_ref, rew_ref,
    att_hbm, dq_hbm, drk_hbm, drv_hbm, dpk_hbm, dpv_hbm,
    qn, gn, rkn, rvn, kn, vn, stat_own, qT, q2, gT, e_st, m_st, m_cur, l_cur, acc, dqa, aux,
    stat_out, stat_in, snd, rcv, own_part, att_n, dq_n, rg_n, pg_n,
    sem_l, sem_ps, sem_pr, sem_as, sem_ar, sem_bs, sem_br, sem_ss, sem_sr,
    sem_ms, sem_mr, sem_ol, sem_os, sem_or,
):
    rows = qn.shape[1]
    half_q = qn.shape[2]
    half_k = rkn.shape[2]
    piece = pk_hbm.shape[1]
    blk = 2 * piece
    width = heads_per * rows
    inv_root = DH ** (-0.5)
    scale2 = inv_root * math.log2(math.e)
    me = lax.axis_index("resp")
    grp = lax.axis_index("grp")
    z = me // 8
    y = (me // 2) % 4
    c = me % 2

    def at(dz, dy, dc):
        return {"resp": ((z + dz) % 2) * 8 + ((y + dy) % 4) * 2 + (c + dc) % 2}

    def to(src, dst, s_sem, r_sem, target):
        return pltpu.make_async_remote_copy(
            src_ref=src, dst_ref=dst, send_sem=s_sem, recv_sem=r_sem,
            device_id=target, device_id_type=MESH,
        )

    cq = pl.ds(pl.multiple_of(c * half_q, half_q), half_q)
    oq = pl.ds(pl.multiple_of((1 - c) * half_q, half_q), half_q)
    ck = pl.ds(pl.multiple_of(c * half_k, half_k), half_k)
    ok = pl.ds(pl.multiple_of((1 - c) * half_k, half_k), half_k)
    my_rows = pl.ds(pl.multiple_of(c * piece, piece), piece)
    tall = piece + 16
    my_keys = pl.ds(pl.multiple_of(c * tall, 16), piece)
    my_stats = pl.ds(pl.multiple_of(c * tall + piece, 16), 16)
    my_part, twin_part = [
        [pl.ds(pl.multiple_of(k * size, 16), size) for size in (tall, piece)] for k in (c, 1 - c)
    ]
    ring_kv = (kn, vn)

    local = [
        pltpu.make_async_copy(pk_hbm.at[0, :, ck], kn.at[OWN, my_keys, :], sem_l.at[0]),
        pltpu.make_async_copy(pv_hbm.at[0, :, ck], vn.at[OWN, my_rows, :], sem_l.at[1]),
        pltpu.make_async_copy(q_hbm.at[0, 0, :, cq], qn.at[0], sem_l.at[2]),
        pltpu.make_async_copy(rk_hbm.at[0, 0, :, ck], rkn.at[0], sem_l.at[3]),
        pltpu.make_async_copy(rv_hbm.at[0, 0, :, ck], rvn.at[0], sem_l.at[4]),
        pltpu.make_async_copy(og_hbm.at[0, 0, :, cq], gn.at[0], sem_l.at[5]),
    ]
    for cp in local:
        cp.start()

    twin = at(0, 0, 1)
    z_to, up, down = at(1, 0, 0), at(0, 1, 0), at(0, 3, 0)
    groups = [{"grp": (grp + dg) % n_grp} for dg in range(1, n_grp)]
    friends = [twin, z_to, up, down] + groups
    barrier = pltpu.get_barrier_semaphore()
    for friend in friends:
        pl.semaphore_signal(barrier, inc=1, device_id=friend, device_id_type=MESH)

    def turn(src, dst, r):
        for j in range(2):
            for h in range(heads_per):
                dst[2 * r + j, :, h * rows:(h + 1) * rows] = src[
                    r, :, (j * heads_per + h) * DH:(j * heads_per + h + 1) * DH
                ].T

    def split_queries(r):
        for u in (2 * r, 2 * r + 1):
            for h in range(heads_per):
                cols = slice(h * rows, (h + 1) * rows)
                full = qT[u, :, cols].astype(F32) * scale2
                high = full.astype(BF16)
                q2[u, 0:DH, cols] = high
                q2[u, DH:2 * DH, cols] = (full - high.astype(F32)).astype(BF16)

    ones = jnp.ones((16, blk), BF16)

    def forward(units, keys, values, block, first):
        keys = {u: jnp.concatenate([k, k], axis=1) for u, k in keys.items()}
        values = {u: jnp.concatenate([v.T, ones], axis=0) for u, v in values.items()}
        todo = [(u, slice(h * rows, (h + 1) * rows)) for u in units for h in range(heads_per)]
        logits, lows = {}, {}

        def start(i):
            u, cols = todo[i]
            logits[i] = nn(keys[u], q2[u, :, cols])

        def finish(i):
            u, cols = todo[i]
            low, alpha = lows.pop(i)
            part = nn(values[u], low)
            if first:
                l_cur[u:u + 1, cols] = part[DH:DH + 1]
                acc[u, :, cols] = part[0:DH]
            else:
                l_cur[u:u + 1, cols] = l_cur[u:u + 1, cols] * alpha + part[DH:DH + 1]
                acc[u, :, cols] = acc[u, :, cols] * alpha + part[0:DH]

        for i in range(3):
            start(i)
        for i, (u, cols) in enumerate(todo):
            if i + 3 < len(todo):
                start(i + 3)
            s = logits.pop(i)
            if first:
                seen = lax.broadcasted_iota(jnp.int32, s.shape, 0) <= (
                    lax.broadcasted_iota(jnp.int32, s.shape, 1)
                )
                s = jnp.where(seen, s, -jnp.inf)
                m_new = jnp.max(s, axis=0, keepdims=True)
                alpha = None
            else:
                m_old = m_cur[u:u + 1, cols]
                m_new = jnp.maximum(m_old, jnp.max(s, axis=0, keepdims=True))
                alpha = jnp.exp2(m_old - m_new)
            low = jnp.exp2(s - m_new).astype(BF16)
            e_st[block, u, :, cols] = low
            m_cur[u:u + 1, cols] = m_new
            m_st[block, u:u + 1, cols] = m_new
            lows[i] = (low, alpha)
            if i >= 2:
                finish(i - 2)
        for i in sorted(lows):
            finish(i)

    def own_block(r):
        turn(qn, qT, r)
        split_queries(r)
        units = (2 * r, 2 * r + 1)
        forward(
            units,
            {u: rkn[r, :, (u % 2) * DH:(u % 2 + 1) * DH] for u in units},
            {u: rvn[r, :, (u % 2) * DH:(u % 2 + 1) * DH] for u in units},
            n_blocks, True,
        )

    row_id = lax.broadcasted_iota(jnp.int32, stat_own.shape, 0)
    stat_own[...] = jnp.where(
        row_id == 0,
        jnp.broadcast_to(len_ref[...], stat_own.shape),
        jnp.broadcast_to(rew_ref[...], stat_own.shape),
    ).astype(F32).astype(BF16)
    kn[OWN, my_stats, :] = stat_own[...]
    pl.semaphore_wait(barrier, len(friends))

    pair = [
        to(pk_hbm.at[0, :, ok], kn.at[OWN, my_keys, :], sem_ps.at[0], sem_pr.at[0], twin),
        to(pv_hbm.at[0, :, ok], vn.at[OWN, my_rows, :], sem_ps.at[1], sem_pr.at[1], twin),
        to(q_hbm.at[0, 0, :, oq], qn.at[1], sem_ps.at[2], sem_pr.at[2], twin),
        to(rk_hbm.at[0, 0, :, ok], rkn.at[1], sem_ps.at[3], sem_pr.at[3], twin),
        to(rv_hbm.at[0, 0, :, ok], rvn.at[1], sem_ps.at[4], sem_pr.at[4], twin),
        to(og_hbm.at[0, 0, :, oq], gn.at[1], sem_ps.at[5], sem_pr.at[5], twin),
        to(stat_own, kn.at[OWN, my_stats, :], sem_ps.at[6], sem_pr.at[6], twin),
    ]
    for cp in (pair[0], pair[6], pair[1]):
        cp.start()

    ag = {}
    for kv in (0, 1):
        for dst, target in ((YM, up), (YP, down), (ZZ, z_to)):
            ag[dst, kv] = [
                to(
                    ring_kv[kv].at[OWN, part[kv], :], ring_kv[kv].at[dst, part[kv], :],
                    s_sem.at[dst, kv], r_sem.at[dst, kv], target,
                )
                for part, s_sem, r_sem in (
                    (my_part, sem_as, sem_ar), (twin_part, sem_bs, sem_br),
                )
            ]
    ag_plan = (
        (YM, YY, 0, up), (YM, ZYM, 0, z_to), (YM, ZYM, 1, z_to),
        (YP, YY, 1, down), (ZZ, ZYP, 0, down), (ZZ, ZYP, 1, down),
        (ZYM, ZYY, 0, up), (ZYM, ZYY, 1, up),
    )
    for src, dst, kv, target in ag_plan:
        ag[dst, kv] = [
            to(ring_kv[kv].at[src], ring_kv[kv].at[dst], sem_as.at[dst, kv], sem_ar.at[dst, kv], target)
        ]

    for kv in (0, 1):
        local[kv].wait()
        for dst in (YM, YP, ZZ):
            ag[dst, kv][0].start()
    for cp in pair[2:6]:
        cp.start()
    for kv in (0, 1):
        pair[kv].wait_recv()
        if kv == 0:
            pair[6].wait_recv()
        for dst in (YM, YP, ZZ):
            ag[dst, kv][1].start()


    n_blocks = 8
    for i in (2, 3, 4):
        local[i].wait()
    own_block(0)

    for i in (2, 3, 4):
        pair[i].wait_recv()
    own_block(1)
    local[5].wait()
    pair[5].wait_recv()
    for r in range(2):
        turn(gn, gT, r)
    def keys_of(block, j):
        heads = slice(j * DH, (j + 1) * DH)
        return jnp.concatenate(
            [kn[block, 0:piece, heads], kn[block, tall:tall + piece, heads]], axis=0
        )

    def pass_on(waits, starts):
        for key in waits:
            for cp in ag[key]:
                cp.wait_recv()
        for key in starts:
            for cp in ag[key]:
                cp.start()

    @pl.loop(0, n_blocks)
    def forward_step(step):
        @pl.when(step == 1)
        def _():
            pass_on([(YM, 0)], [(YY, 0), (ZYM, 0)])
            pass_on([(ZZ, 0)], [(ZYP, 0)])
            pass_on([(YM, 1)], [(ZYM, 1)])
            pass_on([(YP, 0), (YP, 1)], [(YY, 1)])
            pass_on([(ZZ, 1)], [(ZYP, 1)])

        @pl.when(step == 3)
        def _():
            pass_on([(ZYM, 0)], [(ZYY, 0)])

        @pl.when(step == 4)
        def _():
            pass_on([(ZYM, 1)], [(ZYY, 1)])

        @pl.when(step == 5)
        def _():
            pass_on([(YY, 0), (YY, 1)], [])

        @pl.when(step == 6)
        def _():
            pass_on([(ZYP, 0), (ZYP, 1)], [])

        @pl.when(step == 7)
        def _():
            pass_on([(ZYY, 0), (ZYY, 1)], [])

        order = (0, 2, 1, 3)
        forward(
            order,
            {u: keys_of(step, u % 2) for u in order},
            {u: vn[step, :, (u % 2) * DH:(u % 2 + 1) * DH] for u in order},
            step, False,
        )

    sum_one = sum_two = live = jnp.zeros((1, 128), F32)
    for slot in range(n_blocks):
        for core in range(2):
            stat = kn[slot, core * tall + piece:(core + 1) * tall, 0:128].astype(F32)
            live = live + stat[0:1]
            sum_one = sum_one + stat[1:2]
            sum_two = sum_two + stat[1:2] * stat[1:2]
    stat_out[...] = jnp.broadcast_to(live, (8, 128))
    counts = [
        to(
            stat_out, stat_in.at[n_grp - dg], sem_ss.at[n_grp - dg], sem_sr.at[n_grp - dg],
            groups[dg - 1],
        )
        for dg in range(1, n_grp)
    ]
    for cp in counts:
        cp.start()
    n_resp = 16
    mean = sum_one / n_resp
    variance = (n_resp * sum_two - sum_one * sum_one) / (n_resp * n_resp)
    spread = jnp.maximum(jnp.sqrt(variance), 1.0)
    twin_stats = pl.ds(pl.multiple_of((1 - c) * tall + piece, 16), 16)
    for r in range(2):
        stat = stat_own[:, 0:128] if r == 0 else kn[OWN, twin_stats, 0:128]
        length = stat.astype(F32)[0:1].astype(jnp.int32)
        strength = (stat.astype(F32)[1:2] - mean) / spread
        weight = jnp.concatenate(
            [
                jnp.where(
                    lax.broadcasted_iota(jnp.int32, (1, 128), 1) + start < length, strength, 0.0
                )
                for start in range(0, rows, 128)
            ],
            axis=1,
        )
        for j in range(2):
            u = 2 * r + j
            for h in range(heads_per):
                cols = slice(h * rows, (h + 1) * rows)
                inv = 1.0 / l_cur[u:u + 1, cols]
                out = (acc[u, :, cols] * inv).astype(BF16)
                q2[u, 0:DH, cols] = out
                delta = jnp.sum(
                    out.astype(F32) * gT[u, :, cols].astype(F32), axis=0, keepdims=True
                )
                aux[0, u:u + 1, cols] = inv * weight
                aux[1, u:u + 1, cols] = delta
                dqa[u, :, cols] = jnp.zeros((DH, rows), F32)

    def backward(units, keys, values, block, place):
        flat = {u: k.T for u, k in keys.items()}
        todo = [(u, h, slice(h * rows, (h + 1) * rows)) for u in units for h in range(heads_per)]
        scaled, shift, dots, lows, sums = {}, {}, {}, {}, {}

        def start(i):
            u, h, cols = todo[i]
            factor = jnp.exp2(m_st[block, u:u + 1, cols] - m_cur[u:u + 1, cols])
            factor = factor * aux[0, u:u + 1, cols]
            scaled[i] = (gT[u, :, cols].astype(F32) * factor).astype(BF16)
            shift[i] = factor * aux[1, u:u + 1, cols]
            dots[i] = nn(values[u], scaled[i])

        def add(key, term):
            sums[key] = sums[key] + term if key in sums else term

        def finish(i):
            u, h, cols = todo[i]
            low = lows.pop(i)
            col = (u % 2) * heads_per + h
            dqa[u, :, cols] = dqa[u, :, cols] + nn(flat[u], low)
            add((place(u), 0), nn(low, qn[u // 2, :, col * DH:(col + 1) * DH]))
            add((place(u), 1), nt(scaled.pop(i), e_st[block, u, :, cols]))

        for i in range(2):
            start(i)
        for i, (u, h, cols) in enumerate(todo):
            if i + 2 < len(todo):
                start(i + 2)
            d = dots.pop(i) - shift.pop(i)
            lows[i] = (e_st[block, u, :, cols].astype(F32) * d).astype(BF16)
            if i >= 1:
                finish(i - 1)
        finish(len(todo) - 1)
        return {
            key: term.T * inv_root if key[1] == 0 else term for key, term in sums.items()
        }

    names = ("m1", "m6", "m3", "m2", "m7", "m5", "m4")
    route = {
        "m1": (down, down), "m6": (up, up), "m3": (down, up), "m2": (z_to, z_to),
        "m7": (z_to, z_to), "m5": (up, up), "m4": (down, down),
    }
    msg = {}
    for n, name in enumerate(names):
        for kv in range(2):
            msg[name, kv] = to(
                snd.at[n, kv], rcv.at[n, kv], sem_ms.at[n, kv], sem_mr.at[n, kv], route[name][kv]
            )

    needs = {
        0: ((), ()), 1: ((), ()), 2: ((), ()), 3: (("m1",), ("m1",)), 4: (("m6",), ("m6",)),
        5: ((), ("m3",)), 6: (("m2", "m3"), ("m2",)),
    }

    @pl.loop(0, n_blocks)
    def backward_step(step):
        block = n_blocks - 1 - step
        order = (0, 2, 1, 3)
        sums = backward(
            order,
            {u: keys_of(block, u % 2) for u in order},
            {u: vn[block, :, (u % 2) * DH:(u % 2 + 1) * DH] for u in order},
            block, lambda u: u % 2,
        )
        total_heads = 4 * heads_per
        for i in range(3):
            head = jnp.minimum(3 * step + i, total_heads - 1)
            u = head // heads_per
            h = head % heads_per
            col = pl.multiple_of(((u % 2) * heads_per + h) * DH, DH)
            att_n[u // 2, :, pl.ds(col, DH)] = q2[
                u, 0:DH, pl.ds(pl.multiple_of(h * rows, rows), rows)
            ].T
        for (j, kv), term in sums.items():
            own_part[kv, j * DH:(j + 1) * DH, :] = term

        for n, name in enumerate(names):
            @pl.when(step == n)
            def _():
                for kv in range(2):
                    total = own_part[kv]
                    for other in needs[n][kv]:
                        msg[other, kv].wait_recv()
                        total = total + rcv[names.index(other), kv].astype(F32)
                    snd[n, kv] = total.astype(BF16)
                    msg[name, kv].start()

    att_own = pltpu.make_async_copy(att_n.at[0], att_hbm.at[0, 0, :, cq], sem_ol.at[0])
    att_twin = to(att_n.at[1], att_hbm.at[0, 0, :, cq], sem_os.at[0], sem_or.at[0], twin)
    att_own.start()
    att_twin.start()

    outs_own = [
        pltpu.make_async_copy(rg_n.at[0, 0], drk_hbm.at[0, 0, :, ck], sem_ol.at[1]),
        pltpu.make_async_copy(rg_n.at[0, 1], drv_hbm.at[0, 0, :, ck], sem_ol.at[2]),
        pltpu.make_async_copy(dq_n.at[0], dq_hbm.at[0, 0, :, cq], sem_ol.at[3]),
    ]
    outs_twin = [
        to(rg_n.at[1, 0], drk_hbm.at[0, 0, :, ck], sem_os.at[1], sem_or.at[1], twin),
        to(rg_n.at[1, 1], drv_hbm.at[0, 0, :, ck], sem_os.at[2], sem_or.at[2], twin),
        to(dq_n.at[1], dq_hbm.at[0, 0, :, cq], sem_os.at[3], sem_or.at[3], twin),
    ]
    for r in (1, 0):
        units = (2 * r, 2 * r + 1)
        sums = backward(
            units,
            {u: rkn[r, :, (u % 2) * DH:(u % 2 + 1) * DH] for u in units},
            {u: rvn[r, :, (u % 2) * DH:(u % 2 + 1) * DH] for u in units},
            n_blocks, lambda u: u,
        )
        if r == 1:
            for cp in counts:
                cp.wait_recv()
            for slot in range(1, n_grp):
                live = live + stat_in[slot, 0:1, :]
            norm = (n_grp * n_resp * rows) / live
            norm_rows = jnp.concatenate([norm] * (rows // 128), axis=1)
        for j in range(2):
            for h in range(heads_per):
                col = slice((j * heads_per + h) * DH, (j * heads_per + h + 1) * DH)
                grad = dqa[2 * r + j, :, h * rows:(h + 1) * rows] * (norm_rows * inv_root)
                dq_n[r, :, col] = grad.astype(BF16).T
        for (u, kv), term in sums.items():
            rg_n[r, kv, :, (u % 2) * DH:(u % 2 + 1) * DH] = (term * norm_rows).astype(BF16).T
        for cp in outs_twin if r else outs_own:
            cp.start()

    twin_rows = pl.ds(pl.multiple_of((1 - c) * piece, piece), piece)
    for kv, out in enumerate((dpk_hbm, dpv_hbm)):
        total = own_part[kv]
        for name in ("m5", "m7", "m4"):
            msg[name, kv].wait_recv()
            total = total + rcv[names.index(name), kv].astype(F32)
        pg_n[kv] = (total * norm_rows).astype(BF16).T
        outs_own.append(
            pltpu.make_async_copy(pg_n.at[kv, my_rows, :], out.at[0, :, ck], sem_ol.at[4 + kv])
        )
        outs_twin.append(
            to(
                pg_n.at[kv, twin_rows, :], out.at[0, :, ck],
                sem_os.at[4 + kv], sem_or.at[4 + kv], twin,
            )
        )
        outs_twin[-1].start()
        outs_own[-1].start()

    for cp in [att_own] + outs_own:
        cp.wait()
    for cp in [att_twin] + outs_twin:
        cp.wait()
    for cp in pair + counts + sum(ag.values(), []) + list(msg.values()):
        cp.wait_send()


def finish(*refs):
    ins, outs, bufs, (sem_in, sem_out) = refs[:6], refs[6:12], refs[12:18], refs[18:]
    loads, stores = [], []
    for src, dst, buf in zip(ins, outs, bufs):
        total = src.shape[-2]
        pieces = 4 if src.shape[-1] > 1024 else 1
        step = total // pieces
        lead = (0,) * (len(src.shape) - 2)
        for i in range(pieces):
            part = lead + (pl.ds(i * step, step),)
            n = len(loads)
            loads.append(pltpu.make_async_copy(src.at[part], buf.at[part], sem_in.at[n]))
            stores.append(pltpu.make_async_copy(buf.at[part], dst.at[part], sem_out.at[n]))
            loads[-1].start()
    for load, store in zip(loads, stores):
        load.wait()
        store.start()
    for store in stores:
        store.wait()


def on_device(n_grp, queries, resp_keys, resp_values, prompt_keys, prompt_values, out_grad,
              lengths, rewards):
    rows = queries.shape[2]
    half_q = queries.shape[3] // 2
    half_k = resp_keys.shape[3] // 2
    heads_per = half_q // half_k
    piece = prompt_keys.shape[1]
    blk = 2 * piece
    width = heads_per * rows
    anywhere = pl.BlockSpec(memory_space=pl.ANY)
    dma = pltpu.SemaphoreType.DMA
    vmem = pltpu.VMEM
    scratch = [
        vmem((2, rows, half_q), BF16), vmem((2, rows, half_q), BF16),
        vmem((2, rows, half_k), BF16), vmem((2, rows, half_k), BF16),
        vmem((8, blk + 32, half_k), BF16), vmem((8, blk, half_k), BF16),
        vmem((16, half_k), BF16),
        vmem((4, DH, width), BF16), vmem((4, 2 * DH, width), BF16), vmem((4, DH, width), BF16),
        vmem((9, 4, blk, width), BF16),
        vmem((9, 8, width), F32), vmem((8, width), F32), vmem((8, width), F32),
        vmem((4, DH, width), F32), vmem((4, DH, width), F32),
        vmem((2, 8, width), F32),
        vmem((8, 128), F32), vmem((n_grp, 8, 128), F32),
        vmem((7, 2, half_k, blk), BF16), vmem((7, 2, half_k, blk), BF16),
        vmem((2, half_k, blk), F32),
        vmem((2, rows, half_q), BF16), vmem((2, rows, half_q), BF16),
        vmem((2, 2, rows, half_k), BF16), vmem((2, blk, half_k), BF16),
        dma((6,)), dma((7,)), dma((7,)), dma((8, 2)), dma((8, 2)),
        dma((8, 2)), dma((8, 2)), dma((n_grp,)), dma((n_grp,)),
        dma((7, 2)), dma((7, 2)), dma((6,)), dma((6,)), dma((6,)),
    ]
    like = lambda a: jax.ShapeDtypeStruct(a.shape, a.dtype)
    shapes = (
        like(queries), like(queries), like(resp_keys), like(resp_values),
        like(prompt_keys), like(prompt_values),
    )
    results = pl.pallas_call(
        lambda *refs: kernel(n_grp, heads_per, *refs),
        out_shape=shapes,
        in_specs=[anywhere] * 6 + [pl.BlockSpec(memory_space=pltpu.VMEM)] * 2,
        out_specs=(anywhere,) * 6,
        scratch_shapes=scratch,
        compiler_params=pltpu.CompilerParams(
            collective_id=0, has_side_effects=True, vmem_limit_bytes=60 * 2**20
        ),
        name="grpo_attention",
    )(queries, resp_keys, resp_values, prompt_keys, prompt_values, out_grad, lengths, rewards)
    return pl.pallas_call(
        finish,
        out_shape=shapes,
        in_specs=[anywhere] * 6,
        out_specs=(anywhere,) * 6,
        scratch_shapes=[vmem(x.shape, x.dtype) for x in shapes] + [dma((12,)), dma((12,))],
        compiler_params=pltpu.CompilerParams(vmem_limit_bytes=60 * 2**20),
        name="write_results",
    )(*results)


def solution(mesh):
    n_grp = mesh.shape["grp"]
    wide = P("grp", "resp", None, None)
    tall = P("grp", "resp", None)
    return jax.shard_map(
        lambda *arrays: on_device(n_grp, *arrays),
        mesh=mesh,
        in_specs=(wide, wide, wide, tall, tall, wide, P("grp", "resp"), P("grp", "resp")),
        out_specs=(wide, wide, wide, wide, tall, tall),
        check_vma=False,
    )
```

```python
import math

import jax
import jax.numpy as jnp
from jax import lax
from jax.experimental import pallas as pl
from jax.experimental.pallas import tpu as pltpu
from jax.sharding import PartitionSpec as P

DH = 128
F32 = jnp.float32
BF16 = jnp.bfloat16
MESH = pl.DeviceIdType.MESH

SLOTS = ((0, 0), (0, 3), (0, 1), (1, 0), (1, 3), (0, 2), (1, 1), (1, 2))
OWN, YM, YP, ZZ, ZYM, YY, ZYP, ZYY = range(8)


def nn(a, b):
    return jnp.dot(a, b, preferred_element_type=F32)


def nt(a, b):
    return lax.dot_general(a, b, (((1,), (1,)), ((), ())), preferred_element_type=F32)


def kernel(
    n_grp, heads_per, q_hbm, rk_hbm, rv_hbm, pk_hbm, pv_hbm, og_hbm, len_ref, rew_ref,
    att_hbm, dq_hbm, drk_hbm, drv_hbm, dpk_hbm, dpv_hbm,
    qn, gn, rkn, rvn, kn, vn, stat_own, qT, q2, gT, e_st, m_st, m_cur, l_cur, acc, dqa, aux,
    stat_out, stat_in, stat_all, snd, rcv, own_part, att_n, dq_n, rg_n, pg_n,
    sem_l, sem_ps, sem_pr, sem_as, sem_ar, sem_bs, sem_br, sem_ss, sem_sr,
    sem_ms, sem_mr, sem_ol, sem_os, sem_or,
):
    rows = qn.shape[1]
    half_q = qn.shape[2]
    half_k = rkn.shape[2]
    piece = pk_hbm.shape[1]
    blk = 2 * piece
    width = heads_per * rows
    inv_root = DH ** (-0.5)
    scale2 = inv_root * math.log2(math.e)
    me = lax.axis_index("resp")
    grp = lax.axis_index("grp")
    z = me // 8
    y = (me // 2) % 4
    c = me % 2

    def at(dz, dy, dc):
        return {"resp": ((z + dz) % 2) * 8 + ((y + dy) % 4) * 2 + (c + dc) % 2}

    def to(src, dst, s_sem, r_sem, target):
        return pltpu.make_async_remote_copy(
            src_ref=src, dst_ref=dst, send_sem=s_sem, recv_sem=r_sem,
            device_id=target, device_id_type=MESH,
        )

    cq = pl.ds(pl.multiple_of(c * half_q, half_q), half_q)
    oq = pl.ds(pl.multiple_of((1 - c) * half_q, half_q), half_q)
    ck = pl.ds(pl.multiple_of(c * half_k, half_k), half_k)
    ok = pl.ds(pl.multiple_of((1 - c) * half_k, half_k), half_k)
    my_rows = pl.ds(pl.multiple_of(c * piece, piece), piece)
    tall = piece + 16
    my_keys = pl.ds(pl.multiple_of(c * tall, 16), piece)
    my_stats = pl.ds(pl.multiple_of(c * tall + piece, 16), 16)
    my_part, twin_part = [
        [pl.ds(pl.multiple_of(k * size, 16), size) for size in (tall, piece)] for k in (c, 1 - c)
    ]
    ring_kv = (kn, vn)

    local = [
        pltpu.make_async_copy(pk_hbm.at[0, :, ck], kn.at[OWN, my_keys, :], sem_l.at[0]),
        pltpu.make_async_copy(pv_hbm.at[0, :, ck], vn.at[OWN, my_rows, :], sem_l.at[1]),
        pltpu.make_async_copy(q_hbm.at[0, 0, :, cq], qn.at[0], sem_l.at[2]),
        pltpu.make_async_copy(rk_hbm.at[0, 0, :, ck], rkn.at[0], sem_l.at[3]),
        pltpu.make_async_copy(rv_hbm.at[0, 0, :, ck], rvn.at[0], sem_l.at[4]),
        pltpu.make_async_copy(og_hbm.at[0, 0, :, cq], gn.at[0], sem_l.at[5]),
    ]
    for cp in local:
        cp.start()

    twin = at(0, 0, 1)
    z_to, up, down = at(1, 0, 0), at(0, 1, 0), at(0, 3, 0)
    groups = [{"grp": (grp + dg) % n_grp} for dg in range(1, n_grp)]
    friends = [twin, z_to, up, down]
    barrier = pltpu.get_barrier_semaphore()
    for friend in friends:
        pl.semaphore_signal(barrier, inc=1, device_id=friend, device_id_type=MESH)

    @pl.when(grp == 0)
    def _():
        for group in groups:
            pl.semaphore_signal(barrier, inc=1, device_id=group, device_id_type=MESH)

    def turn(src, dst, r):
        for j in range(2):
            for h in range(heads_per):
                dst[2 * r + j, :, h * rows:(h + 1) * rows] = src[
                    r, :, (j * heads_per + h) * DH:(j * heads_per + h + 1) * DH
                ].T

    def split_queries(r):
        for u in (2 * r, 2 * r + 1):
            for h in range(heads_per):
                cols = slice(h * rows, (h + 1) * rows)
                full = qT[u, :, cols].astype(F32) * scale2
                high = full.astype(BF16)
                q2[u, 0:DH, cols] = high
                q2[u, DH:2 * DH, cols] = (full - high.astype(F32)).astype(BF16)

    ones = jnp.ones((16, blk), BF16)

    def forward(units, keys, values, block, first):
        keys = {u: jnp.concatenate([k, k], axis=1) for u, k in keys.items()}
        values = {u: jnp.concatenate([v.T, ones], axis=0) for u, v in values.items()}
        todo = [(u, slice(h * rows, (h + 1) * rows)) for u in units for h in range(heads_per)]
        logits, lows = {}, {}

        def start(i):
            u, cols = todo[i]
            logits[i] = nn(keys[u], q2[u, :, cols])

        def finish(i):
            u, cols = todo[i]
            low, alpha = lows.pop(i)
            part = nn(values[u], low)
            if first:
                l_cur[u:u + 1, cols] = part[DH:DH + 1]
                acc[u, :, cols] = part[0:DH]
            else:
                l_cur[u:u + 1, cols] = l_cur[u:u + 1, cols] * alpha + part[DH:DH + 1]
                acc[u, :, cols] = acc[u, :, cols] * alpha + part[0:DH]

        for i in range(3):
            start(i)
        for i, (u, cols) in enumerate(todo):
            if i + 3 < len(todo):
                start(i + 3)
            s = logits.pop(i)
            if first:
                seen = lax.broadcasted_iota(jnp.int32, s.shape, 0) <= (
                    lax.broadcasted_iota(jnp.int32, s.shape, 1)
                )
                s = jnp.where(seen, s, -jnp.inf)
                m_new = jnp.max(s, axis=0, keepdims=True)
                alpha = None
            else:
                m_old = m_cur[u:u + 1, cols]
                m_new = jnp.maximum(m_old, jnp.max(s, axis=0, keepdims=True))
                alpha = jnp.exp2(m_old - m_new)
            low = jnp.exp2(s - m_new).astype(BF16)
            e_st[block, u, :, cols] = low
            m_cur[u:u + 1, cols] = m_new
            m_st[block, u:u + 1, cols] = m_new
            lows[i] = (low, alpha)
            if i >= 2:
                finish(i - 2)
        for i in sorted(lows):
            finish(i)

    def own_block(r):
        turn(qn, qT, r)
        split_queries(r)
        units = (2 * r, 2 * r + 1)
        forward(
            units,
            {u: rkn[r, :, (u % 2) * DH:(u % 2 + 1) * DH] for u in units},
            {u: rvn[r, :, (u % 2) * DH:(u % 2 + 1) * DH] for u in units},
            n_blocks, True,
        )

    row_id = lax.broadcasted_iota(jnp.int32, stat_own.shape, 0)
    stat_own[...] = jnp.where(
        row_id == 0,
        jnp.broadcast_to(len_ref[...], stat_own.shape),
        jnp.broadcast_to(rew_ref[...], stat_own.shape),
    ).astype(F32).astype(BF16)
    kn[OWN, my_stats, :] = stat_own[...]
    pl.semaphore_wait(barrier, len(friends) + jnp.minimum(grp, 1))

    pair = [
        to(pk_hbm.at[0, :, ok], kn.at[OWN, my_keys, :], sem_ps.at[0], sem_pr.at[0], twin),
        to(pv_hbm.at[0, :, ok], vn.at[OWN, my_rows, :], sem_ps.at[1], sem_pr.at[1], twin),
        to(q_hbm.at[0, 0, :, oq], qn.at[1], sem_ps.at[2], sem_pr.at[2], twin),
        to(rk_hbm.at[0, 0, :, ok], rkn.at[1], sem_ps.at[3], sem_pr.at[3], twin),
        to(rv_hbm.at[0, 0, :, ok], rvn.at[1], sem_ps.at[4], sem_pr.at[4], twin),
        to(og_hbm.at[0, 0, :, oq], gn.at[1], sem_ps.at[5], sem_pr.at[5], twin),
        to(stat_own, kn.at[OWN, my_stats, :], sem_ps.at[6], sem_pr.at[6], twin),
    ]
    for cp in (pair[0], pair[6], pair[1]):
        cp.start()

    ag = {}
    for kv in (0, 1):
        for dst, target in ((YM, up), (YP, down), (ZZ, z_to)):
            ag[dst, kv] = [
                to(
                    ring_kv[kv].at[OWN, part[kv], :], ring_kv[kv].at[dst, part[kv], :],
                    s_sem.at[dst, kv], r_sem.at[dst, kv], target,
                )
                for part, s_sem, r_sem in (
                    (my_part, sem_as, sem_ar), (twin_part, sem_bs, sem_br),
                )
            ]
    ag_plan = (
        (YM, YY, 0, up), (YM, ZYM, 0, z_to), (YM, ZYM, 1, z_to),
        (YP, YY, 1, down), (ZZ, ZYP, 0, down), (ZZ, ZYP, 1, down),
        (ZYM, ZYY, 0, up), (ZYM, ZYY, 1, up),
    )
    for src, dst, kv, target in ag_plan:
        ag[dst, kv] = [
            to(ring_kv[kv].at[src], ring_kv[kv].at[dst], sem_as.at[dst, kv], sem_ar.at[dst, kv], target)
        ]

    for kv in (0, 1):
        local[kv].wait()
        for dst in (YM, YP, ZZ):
            ag[dst, kv][0].start()
    for cp in pair[2:6]:
        cp.start()
    for kv in (0, 1):
        pair[kv].wait_recv()
        if kv == 0:
            pair[6].wait_recv()
        for dst in (YM, YP, ZZ):
            ag[dst, kv][1].start()


    n_blocks = 8
    for i in (2, 3, 4):
        local[i].wait()
    own_block(0)

    for i in (2, 3, 4):
        pair[i].wait_recv()
    own_block(1)
    local[5].wait()
    pair[5].wait_recv()
    for r in range(2):
        turn(gn, gT, r)
    dqa[...] = jnp.zeros_like(dqa)
    def keys_of(block, j):
        heads = slice(j * DH, (j + 1) * DH)
        return jnp.concatenate(
            [kn[block, 0:piece, heads], kn[block, tall:tall + piece, heads]], axis=0
        )

    def pass_on(waits, starts):
        for key in waits:
            for cp in ag[key]:
                cp.wait_recv()
        for key in starts:
            for cp in ag[key]:
                cp.start()

    @pl.loop(0, n_blocks)
    def forward_step(step):
        @pl.when(step == 1)
        def _():
            pass_on([(YM, 0)], [(YY, 0), (ZYM, 0)])
            pass_on([(ZZ, 0)], [(ZYP, 0)])
            pass_on([(YM, 1)], [(ZYM, 1)])
            pass_on([(YP, 0), (YP, 1)], [(YY, 1)])
            pass_on([(ZZ, 1)], [(ZYP, 1)])

        @pl.when(step == 3)
        def _():
            pass_on([(ZYM, 0)], [(ZYY, 0)])

        @pl.when(step == 4)
        def _():
            pass_on([(ZYM, 1)], [(ZYY, 1)])

        @pl.when(step == 5)
        def _():
            pass_on([(YY, 0), (YY, 1)], [])

        @pl.when(step == 6)
        def _():
            pass_on([(ZYP, 0), (ZYP, 1)], [])

        @pl.when(step == 7)
        def _():
            pass_on([(ZYY, 0), (ZYY, 1)], [])

        order = (0, 2, 1, 3)
        forward(
            order,
            {u: keys_of(step, u % 2) for u in order},
            {u: vn[step, :, (u % 2) * DH:(u % 2 + 1) * DH] for u in order},
            step, False,
        )

    sum_one = sum_two = live = jnp.zeros((1, 128), F32)
    for slot in range(n_blocks):
        for core in range(2):
            stat = kn[slot, core * tall + piece:(core + 1) * tall, 0:128].astype(F32)
            live = live + stat[0:1]
            sum_one = sum_one + stat[1:2]
            sum_two = sum_two + stat[1:2] * stat[1:2]
    stat_out[...] = jnp.broadcast_to(live, (8, 128))

    def count_in(slot):
        return to(
            stat_out, stat_in.at[slot], sem_ss.at[0], sem_sr.at[slot], {"grp": jnp.zeros_like(grp)}
        )

    def count_back(n):
        return to(stat_all, stat_all, sem_ss.at[n], sem_sr.at[0], groups[n - 1])

    @pl.when(grp != 0)
    def _():
        count_in(grp).start()

    n_resp = 16
    mean = sum_one / n_resp
    variance = (n_resp * sum_two - sum_one * sum_one) / (n_resp * n_resp)
    spread = jnp.maximum(jnp.sqrt(variance), 1.0)
    twin_stats = pl.ds(pl.multiple_of((1 - c) * tall + piece, 16), 16)
    for r in range(2):
        stat = stat_own[:, 0:128] if r == 0 else kn[OWN, twin_stats, 0:128]
        length = stat.astype(F32)[0:1].astype(jnp.int32)
        strength = (stat.astype(F32)[1:2] - mean) / spread
        weight = jnp.concatenate(
            [
                jnp.where(
                    lax.broadcasted_iota(jnp.int32, (1, 128), 1) + start < length, strength, 0.0
                )
                for start in range(0, rows, 128)
            ],
            axis=1,
        )
        for j in range(2):
            u = 2 * r + j
            for h in range(heads_per):
                cols = slice(h * rows, (h + 1) * rows)
                inv = 1.0 / l_cur[u:u + 1, cols]
                out = (acc[u, :, cols] * inv).astype(BF16)
                q2[u, 0:DH, cols] = out
                delta = jnp.sum(
                    out.astype(F32) * gT[u, :, cols].astype(F32), axis=0, keepdims=True
                )
                aux[0, u:u + 1, cols] = inv * weight
                aux[1, u:u + 1, cols] = delta

    def backward(units, keys, values, block, place):
        flat = {u: k.T for u, k in keys.items()}
        todo = [(u, h, slice(h * rows, (h + 1) * rows)) for u in units for h in range(heads_per)]
        scaled, shift, dots, lows, sums = {}, {}, {}, {}, {}

        def start(i):
            u, h, cols = todo[i]
            factor = jnp.exp2(m_st[block, u:u + 1, cols] - m_cur[u:u + 1, cols])
            factor = factor * aux[0, u:u + 1, cols]
            scaled[i] = (gT[u, :, cols].astype(F32) * factor).astype(BF16)
            shift[i] = factor * aux[1, u:u + 1, cols]
            dots[i] = nn(values[u], scaled[i])

        def add(key, term):
            sums[key] = sums[key] + term if key in sums else term

        def finish(i):
            u, h, cols = todo[i]
            low = lows.pop(i)
            col = (u % 2) * heads_per + h
            dqa[u, :, cols] = dqa[u, :, cols] + nn(flat[u], low)
            add((place(u), 0), nn(low, qn[u // 2, :, col * DH:(col + 1) * DH]))
            add((place(u), 1), nt(scaled.pop(i), e_st[block, u, :, cols]))

        for i in range(2):
            start(i)
        for i, (u, h, cols) in enumerate(todo):
            if i + 2 < len(todo):
                start(i + 2)
            d = dots.pop(i) - shift.pop(i)
            lows[i] = (e_st[block, u, :, cols].astype(F32) * d).astype(BF16)
            if i >= 1:
                finish(i - 1)
        finish(len(todo) - 1)
        return {
            key: term.T * inv_root if key[1] == 0 else term for key, term in sums.items()
        }

    names = ("m1", "m6", "m3", "m2", "m7", "m5", "m4")
    route = {
        "m1": (down, down), "m6": (up, up), "m3": (down, up), "m2": (z_to, z_to),
        "m7": (z_to, z_to), "m5": (up, up), "m4": (down, down),
    }
    msg = {}
    for n, name in enumerate(names):
        for kv in range(2):
            msg[name, kv] = to(
                snd.at[n, kv], rcv.at[n, kv], sem_ms.at[n, kv], sem_mr.at[n, kv], route[name][kv]
            )

    needs = {
        0: ((), ()), 1: ((), ()), 2: ((), ()), 3: (("m1",), ("m1",)), 4: (("m6",), ("m6",)),
        5: ((), ("m3",)), 6: (("m2", "m3"), ("m2",)),
    }

    @pl.loop(0, n_blocks)
    def backward_step(step):
        @pl.when((step == 5) & (grp == 0))
        def _():
            total = stat_out[...]
            for slot in range(1, n_grp):
                count_in(slot).wait_recv()
                total = total + stat_in[slot]
            stat_all[...] = total
            for n in range(1, n_grp):
                count_back(n).start()

        block = n_blocks - 1 - step
        order = (0, 2, 1, 3)
        sums = backward(
            order,
            {u: keys_of(block, u % 2) for u in order},
            {u: vn[block, :, (u % 2) * DH:(u % 2 + 1) * DH] for u in order},
            block, lambda u: u % 2,
        )
        total_heads = 4 * heads_per
        for i in range(3):
            head = jnp.minimum(3 * step + i, total_heads - 1)
            u = head // heads_per
            h = head % heads_per
            col = pl.multiple_of(((u % 2) * heads_per + h) * DH, DH)
            att_n[u // 2, :, pl.ds(col, DH)] = q2[
                u, 0:DH, pl.ds(pl.multiple_of(h * rows, rows), rows)
            ].T
        for (j, kv), term in sums.items():
            own_part[kv, j * DH:(j + 1) * DH, :] = term

        for n, name in enumerate(names):
            @pl.when(step == n)
            def _():
                for kv in range(2):
                    total = own_part[kv]
                    for other in needs[n][kv]:
                        msg[other, kv].wait_recv()
                        total = total + rcv[names.index(other), kv].astype(F32)
                    snd[n, kv] = total.astype(BF16)
                    msg[name, kv].start()

    att_own = pltpu.make_async_copy(att_n.at[0], att_hbm.at[0, 0, :, cq], sem_ol.at[0])
    att_twin = to(att_n.at[1], att_hbm.at[0, 0, :, cq], sem_os.at[0], sem_or.at[0], twin)
    att_own.start()
    att_twin.start()

    outs_own = [
        pltpu.make_async_copy(rg_n.at[0, 0], drk_hbm.at[0, 0, :, ck], sem_ol.at[1]),
        pltpu.make_async_copy(rg_n.at[0, 1], drv_hbm.at[0, 0, :, ck], sem_ol.at[2]),
        pltpu.make_async_copy(dq_n.at[0], dq_hbm.at[0, 0, :, cq], sem_ol.at[3]),
    ]
    outs_twin = [
        to(rg_n.at[1, 0], drk_hbm.at[0, 0, :, ck], sem_os.at[1], sem_or.at[1], twin),
        to(rg_n.at[1, 1], drv_hbm.at[0, 0, :, ck], sem_os.at[2], sem_or.at[2], twin),
        to(dq_n.at[1], dq_hbm.at[0, 0, :, cq], sem_os.at[3], sem_or.at[3], twin),
    ]
    for r in (1, 0):
        units = (2 * r, 2 * r + 1)
        sums = backward(
            units,
            {u: rkn[r, :, (u % 2) * DH:(u % 2 + 1) * DH] for u in units},
            {u: rvn[r, :, (u % 2) * DH:(u % 2 + 1) * DH] for u in units},
            n_blocks, lambda u: u,
        )
        if r == 1:
            @pl.when(grp != 0)
            def _():
                count_back(1).wait_recv()

            norm = (n_grp * n_resp * rows) / stat_all[0:1, :]
            norm_rows = jnp.concatenate([norm] * (rows // 128), axis=1)
        for j in range(2):
            for h in range(heads_per):
                col = slice((j * heads_per + h) * DH, (j * heads_per + h + 1) * DH)
                grad = dqa[2 * r + j, :, h * rows:(h + 1) * rows] * (norm_rows * inv_root)
                dq_n[r, :, col] = grad.astype(BF16).T
        for (u, kv), term in sums.items():
            rg_n[r, kv, :, (u % 2) * DH:(u % 2 + 1) * DH] = (term * norm_rows).astype(BF16).T
        for cp in outs_twin if r else outs_own:
            cp.start()

    twin_rows = pl.ds(pl.multiple_of((1 - c) * piece, piece), piece)
    for kv, out in enumerate((dpk_hbm, dpv_hbm)):
        total = own_part[kv]
        for name in ("m5", "m7", "m4"):
            msg[name, kv].wait_recv()
            total = total + rcv[names.index(name), kv].astype(F32)
        pg_n[kv] = (total * norm_rows).astype(BF16).T
        outs_own.append(
            pltpu.make_async_copy(pg_n.at[kv, my_rows, :], out.at[0, :, ck], sem_ol.at[4 + kv])
        )
        outs_twin.append(
            to(
                pg_n.at[kv, twin_rows, :], out.at[0, :, ck],
                sem_os.at[4 + kv], sem_or.at[4 + kv], twin,
            )
        )
        outs_twin[-1].start()
        outs_own[-1].start()

    for cp in [att_own] + outs_own:
        cp.wait()
    for cp in [att_twin] + outs_twin:
        cp.wait()
    @pl.when(grp != 0)
    def _():
        count_in(grp).wait_send()

    @pl.when(grp == 0)
    def _():
        for n in range(1, n_grp):
            count_back(n).wait_send()

    for cp in pair + sum(ag.values(), []) + list(msg.values()):
        cp.wait_send()


def finish(*refs):
    ins, outs, bufs, (sem_in, sem_out) = refs[:6], refs[6:12], refs[12:18], refs[18:]
    loads, stores = [], []
    for src, dst, buf in zip(ins, outs, bufs):
        total = src.shape[-2]
        pieces = 4 if src.shape[-1] > 1024 else 1
        step = total // pieces
        lead = (0,) * (len(src.shape) - 2)
        for i in range(pieces):
            part = lead + (pl.ds(i * step, step),)
            n = len(loads)
            loads.append(pltpu.make_async_copy(src.at[part], buf.at[part], sem_in.at[n]))
            stores.append(pltpu.make_async_copy(buf.at[part], dst.at[part], sem_out.at[n]))
            loads[-1].start()
    for load, store in zip(loads, stores):
        load.wait()
        store.start()
    for store in stores:
        store.wait()


def on_device(n_grp, queries, resp_keys, resp_values, prompt_keys, prompt_values, out_grad,
              lengths, rewards):
    rows = queries.shape[2]
    half_q = queries.shape[3] // 2
    half_k = resp_keys.shape[3] // 2
    heads_per = half_q // half_k
    piece = prompt_keys.shape[1]
    blk = 2 * piece
    width = heads_per * rows
    anywhere = pl.BlockSpec(memory_space=pl.ANY)
    dma = pltpu.SemaphoreType.DMA
    vmem = pltpu.VMEM
    scratch = [
        vmem((2, rows, half_q), BF16), vmem((2, rows, half_q), BF16),
        vmem((2, rows, half_k), BF16), vmem((2, rows, half_k), BF16),
        vmem((8, blk + 32, half_k), BF16), vmem((8, blk, half_k), BF16),
        vmem((16, half_k), BF16),
        vmem((4, DH, width), BF16), vmem((4, 2 * DH, width), BF16), vmem((4, DH, width), BF16),
        vmem((9, 4, blk, width), BF16),
        vmem((9, 8, width), F32), vmem((8, width), F32), vmem((8, width), F32),
        vmem((4, DH, width), F32), vmem((4, DH, width), F32),
        vmem((2, 8, width), F32),
        vmem((8, 128), F32), vmem((n_grp, 8, 128), F32), vmem((8, 128), F32),
        vmem((7, 2, half_k, blk), BF16), vmem((7, 2, half_k, blk), BF16),
        vmem((2, half_k, blk), F32),
        vmem((2, rows, half_q), BF16), vmem((2, rows, half_q), BF16),
        vmem((2, 2, rows, half_k), BF16), vmem((2, blk, half_k), BF16),
        dma((6,)), dma((7,)), dma((7,)), dma((8, 2)), dma((8, 2)),
        dma((8, 2)), dma((8, 2)), dma((n_grp,)), dma((n_grp,)),
        dma((7, 2)), dma((7, 2)), dma((6,)), dma((6,)), dma((6,)),
    ]
    like = lambda a: jax.ShapeDtypeStruct(a.shape, a.dtype)
    shapes = (
        like(queries), like(queries), like(resp_keys), like(resp_values),
        like(prompt_keys), like(prompt_values),
    )
    results = pl.pallas_call(
        lambda *refs: kernel(n_grp, heads_per, *refs),
        out_shape=shapes,
        in_specs=[anywhere] * 6 + [pl.BlockSpec(memory_space=pltpu.VMEM)] * 2,
        out_specs=(anywhere,) * 6,
        scratch_shapes=scratch,
        compiler_params=pltpu.CompilerParams(
            collective_id=0, has_side_effects=True, vmem_limit_bytes=60 * 2**20
        ),
        name="grpo_attention",
    )(queries, resp_keys, resp_values, prompt_keys, prompt_values, out_grad, lengths, rewards)
    return pl.pallas_call(
        finish,
        out_shape=shapes,
        in_specs=[anywhere] * 6,
        out_specs=(anywhere,) * 6,
        scratch_shapes=[vmem(x.shape, x.dtype) for x in shapes] + [dma((12,)), dma((12,))],
        compiler_params=pltpu.CompilerParams(vmem_limit_bytes=60 * 2**20),
        name="write_results",
    )(*results)


def solution(mesh):
    n_grp = mesh.shape["grp"]
    wide = P("grp", "resp", None, None)
    tall = P("grp", "resp", None)
    return jax.shard_map(
        lambda *arrays: on_device(n_grp, *arrays),
        mesh=mesh,
        in_specs=(wide, wide, wide, tall, tall, wide, P("grp", "resp"), P("grp", "resp")),
        out_specs=(wide, wide, wide, wide, tall, tall),
        check_vma=False,
    )
```

```python
import math

import jax
import jax.numpy as jnp
from jax import lax
from jax.experimental import pallas as pl
from jax.experimental.pallas import tpu as pltpu
from jax.sharding import PartitionSpec as P

DH = 128
F32 = jnp.float32
BF16 = jnp.bfloat16
MESH = pl.DeviceIdType.MESH

SLOTS = ((0, 0), (0, 3), (0, 1), (1, 0), (1, 3), (0, 2), (1, 1), (1, 2))
OWN, YM, YP, ZZ, ZYM, YY, ZYP, ZYY = range(8)


def nn(a, b):
    return jnp.dot(a, b, preferred_element_type=F32)


def nt(a, b):
    return lax.dot_general(a, b, (((1,), (1,)), ((), ())), preferred_element_type=F32)


def kernel(
    n_grp, heads_per, q_hbm, rk_hbm, rv_hbm, pk_hbm, pv_hbm, og_hbm, len_ref, rew_ref,
    att_hbm, dq_hbm, drk_hbm, drv_hbm, dpk_hbm, dpv_hbm,
    qn, gn, rkn, rvn, kn, vn, stat_own, qT, q2, gT, e_st, m_st, m_cur, l_cur, acc, dqa, aux,
    stat_out, stat_in, stat_all, snd, rcv, own_part, att_n, dq_n, rg_n, pg_n,
    sem_l, sem_ps, sem_pr, sem_as, sem_ar, sem_bs, sem_br, sem_ss, sem_sr,
    sem_ms, sem_mr, sem_ol, sem_os, sem_or,
):
    rows = qn.shape[1]
    half_q = qn.shape[2]
    half_k = rkn.shape[2]
    piece = pk_hbm.shape[1]
    blk = 2 * piece
    width = heads_per * rows
    inv_root = DH ** (-0.5)
    scale2 = inv_root * math.log2(math.e)
    me = lax.axis_index("resp")
    grp = lax.axis_index("grp")
    z = me // 8
    y = (me // 2) % 4
    c = me % 2

    def at(dz, dy, dc):
        return {"resp": ((z + dz) % 2) * 8 + ((y + dy) % 4) * 2 + (c + dc) % 2}

    def to(src, dst, s_sem, r_sem, target):
        return pltpu.make_async_remote_copy(
            src_ref=src, dst_ref=dst, send_sem=s_sem, recv_sem=r_sem,
            device_id=target, device_id_type=MESH,
        )

    cq = pl.ds(pl.multiple_of(c * half_q, half_q), half_q)
    oq = pl.ds(pl.multiple_of((1 - c) * half_q, half_q), half_q)
    ck = pl.ds(pl.multiple_of(c * half_k, half_k), half_k)
    ok = pl.ds(pl.multiple_of((1 - c) * half_k, half_k), half_k)
    my_rows = pl.ds(pl.multiple_of(c * piece, piece), piece)
    tall = piece + 16
    my_keys = pl.ds(pl.multiple_of(c * tall, 16), piece)
    my_stats = pl.ds(pl.multiple_of(c * tall + piece, 16), 16)
    twin_part = [pl.ds(pl.multiple_of((1 - c) * size, 16), size) for size in (tall, piece)]
    ring_kv = (kn, vn)

    local = [
        pltpu.make_async_copy(pk_hbm.at[0, :, ck], kn.at[OWN, my_keys, :], sem_l.at[0]),
        pltpu.make_async_copy(pv_hbm.at[0, :, ck], vn.at[OWN, my_rows, :], sem_l.at[1]),
        pltpu.make_async_copy(q_hbm.at[0, 0, :, cq], qn.at[0], sem_l.at[2]),
        pltpu.make_async_copy(rk_hbm.at[0, 0, :, ck], rkn.at[0], sem_l.at[3]),
        pltpu.make_async_copy(rv_hbm.at[0, 0, :, ck], rvn.at[0], sem_l.at[4]),
        pltpu.make_async_copy(og_hbm.at[0, 0, :, cq], gn.at[0], sem_l.at[5]),
    ]
    for cp in local:
        cp.start()

    twin = at(0, 0, 1)
    z_to, up, down = at(1, 0, 0), at(0, 1, 0), at(0, 3, 0)
    groups = [{"grp": (grp + dg) % n_grp} for dg in range(1, n_grp)]
    friends = [twin, z_to, up, down]
    barrier = pltpu.get_barrier_semaphore()
    for friend in friends:
        pl.semaphore_signal(barrier, inc=1, device_id=friend, device_id_type=MESH)

    @pl.when(grp == 0)
    def _():
        for group in groups:
            pl.semaphore_signal(barrier, inc=1, device_id=group, device_id_type=MESH)

    def turn(src, dst, r):
        for j in range(2):
            for h in range(heads_per):
                dst[2 * r + j, :, h * rows:(h + 1) * rows] = src[
                    r, :, (j * heads_per + h) * DH:(j * heads_per + h + 1) * DH
                ].T

    def split_queries(r):
        for u in (2 * r, 2 * r + 1):
            for h in range(heads_per):
                cols = slice(h * rows, (h + 1) * rows)
                full = qT[u, :, cols].astype(F32) * scale2
                high = full.astype(BF16)
                q2[u, 0:DH, cols] = high
                q2[u, DH:2 * DH, cols] = (full - high.astype(F32)).astype(BF16)

    ones = jnp.ones((16, blk), BF16)

    def forward(units, keys, values, block, first):
        keys = {u: jnp.concatenate([k, k], axis=1) for u, k in keys.items()}
        values = {u: jnp.concatenate([v.T, ones], axis=0) for u, v in values.items()}
        todo = [(u, slice(h * rows, (h + 1) * rows)) for u in units for h in range(heads_per)]
        logits, lows = {}, {}

        def start(i):
            u, cols = todo[i]
            logits[i] = nn(keys[u], q2[u, :, cols])

        def finish(i):
            u, cols = todo[i]
            low, alpha = lows.pop(i)
            part = nn(values[u], low)
            if first:
                l_cur[u:u + 1, cols] = part[DH:DH + 1]
                acc[u, :, cols] = part[0:DH]
            else:
                l_cur[u:u + 1, cols] = l_cur[u:u + 1, cols] * alpha + part[DH:DH + 1]
                acc[u, :, cols] = acc[u, :, cols] * alpha + part[0:DH]

        for i in range(3):
            start(i)
        for i, (u, cols) in enumerate(todo):
            if i + 3 < len(todo):
                start(i + 3)
            s = logits.pop(i)
            if first:
                seen = lax.broadcasted_iota(jnp.int32, s.shape, 0) <= (
                    lax.broadcasted_iota(jnp.int32, s.shape, 1)
                )
                s = jnp.where(seen, s, -jnp.inf)
                m_new = jnp.max(s, axis=0, keepdims=True)
                alpha = None
            else:
                m_old = m_cur[u:u + 1, cols]
                m_new = jnp.maximum(m_old, jnp.max(s, axis=0, keepdims=True))
                alpha = jnp.exp2(m_old - m_new)
            low = jnp.exp2(s - m_new).astype(BF16)
            e_st[block, u, :, cols] = low
            m_cur[u:u + 1, cols] = m_new
            m_st[block, u:u + 1, cols] = m_new
            lows[i] = (low, alpha)
            if i >= 2:
                finish(i - 2)
        for i in sorted(lows):
            finish(i)

    def own_block(r):
        turn(qn, qT, r)
        split_queries(r)
        units = (2 * r, 2 * r + 1)
        forward(
            units,
            {u: rkn[r, :, (u % 2) * DH:(u % 2 + 1) * DH] for u in units},
            {u: rvn[r, :, (u % 2) * DH:(u % 2 + 1) * DH] for u in units},
            n_blocks, True,
        )

    row_id = lax.broadcasted_iota(jnp.int32, stat_own.shape, 0)
    stat_own[...] = jnp.where(
        row_id == 0,
        jnp.broadcast_to(len_ref[...], stat_own.shape),
        jnp.broadcast_to(rew_ref[...], stat_own.shape),
    ).astype(F32).astype(BF16)
    kn[OWN, my_stats, :] = stat_own[...]
    pl.semaphore_wait(barrier, len(friends) + jnp.minimum(grp, 1))

    pair = [
        to(pk_hbm.at[0, :, ok], kn.at[OWN, my_keys, :], sem_ps.at[0], sem_pr.at[0], twin),
        to(pv_hbm.at[0, :, ok], vn.at[OWN, my_rows, :], sem_ps.at[1], sem_pr.at[1], twin),
        to(q_hbm.at[0, 0, :, oq], qn.at[1], sem_ps.at[2], sem_pr.at[2], twin),
        to(rk_hbm.at[0, 0, :, ok], rkn.at[1], sem_ps.at[3], sem_pr.at[3], twin),
        to(rv_hbm.at[0, 0, :, ok], rvn.at[1], sem_ps.at[4], sem_pr.at[4], twin),
        to(og_hbm.at[0, 0, :, oq], gn.at[1], sem_ps.at[5], sem_pr.at[5], twin),
        to(stat_own, kn.at[OWN, my_stats, :], sem_ps.at[6], sem_pr.at[6], twin),
    ]
    for cp in (pair[0], pair[6], pair[1]):
        cp.start()

    ag = {}
    for kv in (0, 1):
        for dst, target in ((YM, up), (YP, down), (ZZ, z_to)):
            ag[dst, kv] = [
                to(
                    (pk_hbm, pv_hbm)[kv].at[0, :, ck],
                    ring_kv[kv].at[dst, (my_keys, my_rows)[kv], :],
                    sem_as.at[dst, kv], sem_ar.at[dst, kv], target,
                ),
                to(
                    ring_kv[kv].at[OWN, twin_part[kv], :], ring_kv[kv].at[dst, twin_part[kv], :],
                    sem_bs.at[dst, kv], sem_br.at[dst, kv], target,
                ),
            ]
            if kv == 0:
                ag[dst, kv].append(
                    to(
                        stat_own, kn.at[dst, my_stats, :], sem_ss.at[n_grp + dst],
                        sem_sr.at[n_grp + dst], target,
                    )
                )
    ag_plan = (
        (YM, YY, 0, up), (YM, ZYM, 0, z_to), (YM, ZYM, 1, z_to),
        (YP, YY, 1, down), (ZZ, ZYP, 0, down), (ZZ, ZYP, 1, down),
        (ZYM, ZYY, 0, up), (ZYM, ZYY, 1, up),
    )
    for src, dst, kv, target in ag_plan:
        ag[dst, kv] = [
            to(ring_kv[kv].at[src], ring_kv[kv].at[dst], sem_as.at[dst, kv], sem_ar.at[dst, kv], target)
        ]

    for kv in (0, 1):
        for dst in (YM, YP, ZZ):
            ag[dst, kv][0].start()
    for cp in pair[2:6]:
        cp.start()
    for dst in (YM, YP, ZZ):
        ag[dst, 0][2].start()
    for kv in (0, 1):
        local[kv].wait()
        pair[kv].wait_recv()
        if kv == 0:
            pair[6].wait_recv()
        for dst in (YM, YP, ZZ):
            ag[dst, kv][1].start()


    n_blocks = 8
    for i in (2, 3, 4):
        local[i].wait()
    own_block(0)

    for i in (2, 3, 4):
        pair[i].wait_recv()
    own_block(1)
    local[5].wait()
    pair[5].wait_recv()
    for r in range(2):
        turn(gn, gT, r)
    dqa[...] = jnp.zeros_like(dqa)
    def keys_of(block, j):
        heads = slice(j * DH, (j + 1) * DH)
        return jnp.concatenate(
            [kn[block, 0:piece, heads], kn[block, tall:tall + piece, heads]], axis=0
        )

    def pass_on(waits, starts):
        for key in waits:
            for cp in ag[key]:
                cp.wait_recv()
        for key in starts:
            for cp in ag[key]:
                cp.start()

    @pl.loop(0, n_blocks)
    def forward_step(step):
        @pl.when(step == 1)
        def _():
            pass_on([(YM, 0)], [(YY, 0), (ZYM, 0)])
            pass_on([(ZZ, 0)], [(ZYP, 0)])
            pass_on([(YM, 1)], [(ZYM, 1)])
            pass_on([(YP, 0), (YP, 1)], [(YY, 1)])
            pass_on([(ZZ, 1)], [(ZYP, 1)])

        @pl.when(step == 3)
        def _():
            pass_on([(ZYM, 0)], [(ZYY, 0)])

        @pl.when(step == 4)
        def _():
            pass_on([(YY, 0), (YY, 1)], [])

        @pl.when(step == 5)
        def _():
            pass_on([(ZYM, 1)], [(ZYY, 1)])

        @pl.when(step == 6)
        def _():
            pass_on([(ZYP, 0), (ZYP, 1)], [])

        @pl.when(step == 7)
        def _():
            pass_on([(ZYY, 0), (ZYY, 1)], [])

        block = step + ((step // 4) % 2) * (1 - (step % 4) // 2) * (1 - 2 * (step % 2))
        order = (0, 2, 1, 3)
        forward(
            order,
            {u: keys_of(block, u % 2) for u in order},
            {u: vn[block, :, (u % 2) * DH:(u % 2 + 1) * DH] for u in order},
            block, False,
        )

    sum_one = sum_two = live = jnp.zeros((1, 128), F32)
    for slot in range(n_blocks):
        for core in range(2):
            stat = kn[slot, core * tall + piece:(core + 1) * tall, 0:128].astype(F32)
            live = live + stat[0:1]
            sum_one = sum_one + stat[1:2]
            sum_two = sum_two + stat[1:2] * stat[1:2]
    stat_out[...] = jnp.broadcast_to(live, (8, 128))

    def count_in(slot):
        return to(
            stat_out, stat_in.at[slot], sem_ss.at[0], sem_sr.at[slot], {"grp": jnp.zeros_like(grp)}
        )

    def count_back(n):
        return to(stat_all, stat_all, sem_ss.at[n], sem_sr.at[0], groups[n - 1])

    @pl.when(grp != 0)
    def _():
        count_in(grp).start()

    n_resp = 16
    mean = sum_one / n_resp
    variance = (n_resp * sum_two - sum_one * sum_one) / (n_resp * n_resp)
    spread = jnp.maximum(jnp.sqrt(variance), 1.0)
    twin_stats = pl.ds(pl.multiple_of((1 - c) * tall + piece, 16), 16)
    for r in range(2):
        stat = stat_own[:, 0:128] if r == 0 else kn[OWN, twin_stats, 0:128]
        length = stat.astype(F32)[0:1].astype(jnp.int32)
        strength = (stat.astype(F32)[1:2] - mean) / spread
        weight = jnp.concatenate(
            [
                jnp.where(
                    lax.broadcasted_iota(jnp.int32, (1, 128), 1) + start < length, strength, 0.0
                )
                for start in range(0, rows, 128)
            ],
            axis=1,
        )
        for j in range(2):
            u = 2 * r + j
            for h in range(heads_per):
                cols = slice(h * rows, (h + 1) * rows)
                inv = 1.0 / l_cur[u:u + 1, cols]
                out = (acc[u, :, cols] * inv).astype(BF16)
                q2[u, 0:DH, cols] = out
                delta = jnp.sum(
                    out.astype(F32) * gT[u, :, cols].astype(F32), axis=0, keepdims=True
                )
                aux[0, u:u + 1, cols] = inv * weight
                aux[1, u:u + 1, cols] = delta

    def backward(units, keys, values, block, place):
        flat = {u: k.T for u, k in keys.items()}
        todo = [(u, h, slice(h * rows, (h + 1) * rows)) for u in units for h in range(heads_per)]
        scaled, shift, dots, lows, sums = {}, {}, {}, {}, {}

        def start(i):
            u, h, cols = todo[i]
            factor = jnp.exp2(m_st[block, u:u + 1, cols] - m_cur[u:u + 1, cols])
            factor = factor * aux[0, u:u + 1, cols]
            scaled[i] = (gT[u, :, cols].astype(F32) * factor).astype(BF16)
            shift[i] = factor * aux[1, u:u + 1, cols]
            dots[i] = nn(values[u], scaled[i])

        def add(key, term):
            sums[key] = sums[key] + term if key in sums else term

        def finish(i):
            u, h, cols = todo[i]
            low = lows.pop(i)
            col = (u % 2) * heads_per + h
            dqa[u, :, cols] = dqa[u, :, cols] + nn(flat[u], low)
            add((place(u), 0), nn(low, qn[u // 2, :, col * DH:(col + 1) * DH]))
            add((place(u), 1), nt(scaled.pop(i), e_st[block, u, :, cols]))

        for i in range(2):
            start(i)
        for i, (u, h, cols) in enumerate(todo):
            if i + 2 < len(todo):
                start(i + 2)
            d = dots.pop(i) - shift.pop(i)
            lows[i] = (e_st[block, u, :, cols].astype(F32) * d).astype(BF16)
            if i >= 1:
                finish(i - 1)
        finish(len(todo) - 1)
        return sums

    names = ("m1", "m6", "m3", "m2", "m7", "m5", "m4")
    route = {
        "m1": (down, down), "m6": (up, up), "m3": (down, up), "m2": (z_to, z_to),
        "m7": (z_to, z_to), "m5": (up, up), "m4": (down, down),
    }
    msg = {}
    for n, name in enumerate(names):
        for kv in range(2):
            msg[name, kv] = to(
                snd.at[n, kv], rcv.at[n, kv], sem_ms.at[n, kv], sem_mr.at[n, kv], route[name][kv]
            )

    needs = {
        0: ((), ()), 1: ((), ()), 2: ((), ()), 3: (("m1",), ("m1",)), 4: (("m6",), ("m6",)),
        5: ((), ("m3",)), 6: (("m2", "m3"), ("m2",)),
    }

    @pl.loop(0, n_blocks)
    def backward_step(step):
        @pl.when((step == 5) & (grp == 0))
        def _():
            total = stat_out[...]
            for slot in range(1, n_grp):
                count_in(slot).wait_recv()
                total = total + stat_in[slot]
            stat_all[...] = total
            for n in range(1, n_grp):
                count_back(n).start()

        block = n_blocks - 1 - step
        order = (0, 2, 1, 3)
        sums = backward(
            order,
            {u: keys_of(block, u % 2) for u in order},
            {u: vn[block, :, (u % 2) * DH:(u % 2 + 1) * DH] for u in order},
            block, lambda u: u % 2,
        )
        total_heads = 4 * heads_per
        for i in range(3):
            head = jnp.minimum(3 * step + i, total_heads - 1)
            u = head // heads_per
            h = head % heads_per
            col = pl.multiple_of(((u % 2) * heads_per + h) * DH, DH)
            att_n[u // 2, :, pl.ds(col, DH)] = q2[
                u, 0:DH, pl.ds(pl.multiple_of(h * rows, rows), rows)
            ].T
        for (j, kv), term in sums.items():
            if kv == 0:
                own_part[kv, :, j * DH:(j + 1) * DH] = term
            else:
                own_part[kv, j * DH:(j + 1) * DH, :] = term

        for n, name in enumerate(names):
            @pl.when(step == n)
            def _():
                for kv in range(2):
                    total = own_part[kv]
                    for other in needs[n][kv]:
                        msg[other, kv].wait_recv()
                        total = total + rcv[names.index(other), kv].astype(F32)
                    snd[n, kv] = total.astype(BF16)
                    msg[name, kv].start()

    att_own = pltpu.make_async_copy(att_n.at[0], att_hbm.at[0, 0, :, cq], sem_ol.at[0])
    att_twin = to(att_n.at[1], att_hbm.at[0, 0, :, cq], sem_os.at[0], sem_or.at[0], twin)
    att_own.start()
    att_twin.start()

    outs_own = [
        pltpu.make_async_copy(rg_n.at[0, 0], drk_hbm.at[0, 0, :, ck], sem_ol.at[1]),
        pltpu.make_async_copy(rg_n.at[0, 1], drv_hbm.at[0, 0, :, ck], sem_ol.at[2]),
        pltpu.make_async_copy(dq_n.at[0], dq_hbm.at[0, 0, :, cq], sem_ol.at[3]),
    ]
    outs_twin = [
        to(rg_n.at[1, 0], drk_hbm.at[0, 0, :, ck], sem_os.at[1], sem_or.at[1], twin),
        to(rg_n.at[1, 1], drv_hbm.at[0, 0, :, ck], sem_os.at[2], sem_or.at[2], twin),
        to(dq_n.at[1], dq_hbm.at[0, 0, :, cq], sem_os.at[3], sem_or.at[3], twin),
    ]
    for r in (1, 0):
        units = (2 * r, 2 * r + 1)
        sums = backward(
            units,
            {u: rkn[r, :, (u % 2) * DH:(u % 2 + 1) * DH] for u in units},
            {u: rvn[r, :, (u % 2) * DH:(u % 2 + 1) * DH] for u in units},
            n_blocks, lambda u: u,
        )
        if r == 1:
            @pl.when(grp != 0)
            def _():
                count_back(1).wait_recv()

            norm = (n_grp * n_resp * rows) / stat_all[0:1, :]
            norm_rows = jnp.concatenate([norm] * (rows // 128), axis=1)
        for j in range(2):
            for h in range(heads_per):
                col = slice((j * heads_per + h) * DH, (j * heads_per + h + 1) * DH)
                grad = dqa[2 * r + j, :, h * rows:(h + 1) * rows] * (norm_rows * inv_root)
                dq_n[r, :, col] = grad.astype(BF16).T
        for (u, kv), term in sums.items():
            if kv == 0:
                done = (term * (norm * inv_root)).astype(BF16)
            else:
                done = (term * norm_rows).astype(BF16).T
            rg_n[r, kv, :, (u % 2) * DH:(u % 2 + 1) * DH] = done
        for cp in outs_twin if r else outs_own:
            cp.start()

    twin_rows = pl.ds(pl.multiple_of((1 - c) * piece, piece), piece)
    for kv, out in enumerate((dpk_hbm, dpv_hbm)):
        total = own_part[kv]
        for name in ("m5", "m7", "m4"):
            msg[name, kv].wait_recv()
            total = total + rcv[names.index(name), kv].astype(F32)
        if kv == 0:
            pg_n[kv] = (total * (norm_rows * inv_root)).astype(BF16)
        else:
            pg_n[kv] = (total * norm_rows).astype(BF16).T
        outs_own.append(
            pltpu.make_async_copy(pg_n.at[kv, my_rows, :], out.at[0, :, ck], sem_ol.at[4 + kv])
        )
        outs_twin.append(
            to(
                pg_n.at[kv, twin_rows, :], out.at[0, :, ck],
                sem_os.at[4 + kv], sem_or.at[4 + kv], twin,
            )
        )
        outs_twin[-1].start()
        outs_own[-1].start()

    for cp in [att_own] + outs_own:
        cp.wait()
    for cp in [att_twin] + outs_twin:
        cp.wait()
    @pl.when(grp != 0)
    def _():
        count_in(grp).wait_send()

    @pl.when(grp == 0)
    def _():
        for n in range(1, n_grp):
            count_back(n).wait_send()

    for cp in pair + sum(ag.values(), []) + list(msg.values()):
        cp.wait_send()


def finish(*refs):
    ins, outs, bufs, (sem_in, sem_out) = refs[:6], refs[6:12], refs[12:18], refs[18:]
    loads, stores = [], []
    for src, dst, buf in zip(ins, outs, bufs):
        total = src.shape[-2]
        pieces = 4 if src.shape[-1] > 1024 else 1
        step = total // pieces
        lead = (0,) * (len(src.shape) - 2)
        for i in range(pieces):
            part = lead + (pl.ds(i * step, step),)
            n = len(loads)
            loads.append(pltpu.make_async_copy(src.at[part], buf.at[part], sem_in.at[n]))
            stores.append(pltpu.make_async_copy(buf.at[part], dst.at[part], sem_out.at[n]))
            loads[-1].start()
    for load, store in zip(loads, stores):
        load.wait()
        store.start()
    for store in stores:
        store.wait()


def on_device(n_grp, queries, resp_keys, resp_values, prompt_keys, prompt_values, out_grad,
              lengths, rewards):
    rows = queries.shape[2]
    half_q = queries.shape[3] // 2
    half_k = resp_keys.shape[3] // 2
    heads_per = half_q // half_k
    piece = prompt_keys.shape[1]
    blk = 2 * piece
    width = heads_per * rows
    anywhere = pl.BlockSpec(memory_space=pl.ANY)
    dma = pltpu.SemaphoreType.DMA
    vmem = pltpu.VMEM
    scratch = [
        vmem((2, rows, half_q), BF16), vmem((2, rows, half_q), BF16),
        vmem((2, rows, half_k), BF16), vmem((2, rows, half_k), BF16),
        vmem((8, blk + 32, half_k), BF16), vmem((8, blk, half_k), BF16),
        vmem((16, half_k), BF16),
        vmem((4, DH, width), BF16), vmem((4, 2 * DH, width), BF16), vmem((4, DH, width), BF16),
        vmem((9, 4, blk, width), BF16),
        vmem((9, 8, width), F32), vmem((8, width), F32), vmem((8, width), F32),
        vmem((4, DH, width), F32), vmem((4, DH, width), F32),
        vmem((2, 8, width), F32),
        vmem((8, 128), F32), vmem((n_grp, 8, 128), F32), vmem((8, 128), F32),
        vmem((7, 2, half_k, blk), BF16), vmem((7, 2, half_k, blk), BF16),
        vmem((2, half_k, blk), F32),
        vmem((2, rows, half_q), BF16), vmem((2, rows, half_q), BF16),
        vmem((2, 2, rows, half_k), BF16), vmem((2, blk, half_k), BF16),
        dma((6,)), dma((7,)), dma((7,)), dma((8, 2)), dma((8, 2)),
        dma((8, 2)), dma((8, 2)), dma((n_grp + 8,)), dma((n_grp + 8,)),
        dma((7, 2)), dma((7, 2)), dma((6,)), dma((6,)), dma((6,)),
    ]
    like = lambda a: jax.ShapeDtypeStruct(a.shape, a.dtype)
    shapes = (
        like(queries), like(queries), like(resp_keys), like(resp_values),
        like(prompt_keys), like(prompt_values),
    )
    results = pl.pallas_call(
        lambda *refs: kernel(n_grp, heads_per, *refs),
        out_shape=shapes,
        in_specs=[anywhere] * 6 + [pl.BlockSpec(memory_space=pltpu.VMEM)] * 2,
        out_specs=(anywhere,) * 6,
        scratch_shapes=scratch,
        compiler_params=pltpu.CompilerParams(
            collective_id=0, has_side_effects=True, vmem_limit_bytes=60 * 2**20
        ),
        name="grpo_attention",
    )(queries, resp_keys, resp_values, prompt_keys, prompt_values, out_grad, lengths, rewards)
    return pl.pallas_call(
        finish,
        out_shape=shapes,
        in_specs=[anywhere] * 6,
        out_specs=(anywhere,) * 6,
        scratch_shapes=[vmem(x.shape, x.dtype) for x in shapes] + [dma((12,)), dma((12,))],
        compiler_params=pltpu.CompilerParams(vmem_limit_bytes=60 * 2**20),
        name="write_results",
    )(*results)


def solution(mesh):
    n_grp = mesh.shape["grp"]
    wide = P("grp", "resp", None, None)
    tall = P("grp", "resp", None)
    return jax.shard_map(
        lambda *arrays: on_device(n_grp, *arrays),
        mesh=mesh,
        in_specs=(wide, wide, wide, tall, tall, wide, P("grp", "resp"), P("grp", "resp")),
        out_specs=(wide, wide, wide, wide, tall, tall),
        check_vma=False,
    )
```

```python
import math

import jax
import jax.numpy as jnp
from jax import lax
from jax.experimental import pallas as pl
from jax.experimental.pallas import tpu as pltpu
from jax.sharding import PartitionSpec as P

DH = 128
F32 = jnp.float32
BF16 = jnp.bfloat16
MESH = pl.DeviceIdType.MESH

SLOTS = ((0, 0), (0, 3), (0, 1), (1, 0), (1, 3), (0, 2), (1, 1), (1, 2))
OWN, YM, YP, ZZ, ZYM, YY, ZYP, ZYY = range(8)


def nn(a, b):
    return jnp.dot(a, b, preferred_element_type=F32)


def nt(a, b):
    return lax.dot_general(a, b, (((1,), (1,)), ((), ())), preferred_element_type=F32)


def kernel(
    n_grp, heads_per, q_hbm, rk_hbm, rv_hbm, pk_hbm, pv_hbm, og_hbm, len_ref, rew_ref,
    att_hbm, dq_hbm, drk_hbm, drv_hbm, dpk_hbm, dpv_hbm,
    qn, gn, rkn, rvn, kn, vn, stat_own, qT, q2, gT, e_st, m_st, m_cur, l_cur, acc, dqa, aux,
    stat_out, stat_in, stat_all, snd, rcv, own_part, att_n, dq_n, rg_n, pg_n,
    sem_l, sem_ps, sem_pr, sem_as, sem_ar, sem_bs, sem_br, sem_ss, sem_sr,
    sem_ms, sem_mr, sem_ol, sem_os, sem_or,
):
    rows = qn.shape[1]
    half_q = qn.shape[2]
    half_k = rkn.shape[2]
    piece = pk_hbm.shape[1]
    blk = 2 * piece
    width = heads_per * rows
    inv_root = DH ** (-0.5)
    scale2 = inv_root * math.log2(math.e)
    me = lax.axis_index("resp")
    grp = lax.axis_index("grp")
    z = me // 8
    y = (me // 2) % 4
    c = me % 2

    def at(dz, dy, dc):
        return {"resp": ((z + dz) % 2) * 8 + ((y + dy) % 4) * 2 + (c + dc) % 2}

    def to(src, dst, s_sem, r_sem, target):
        return pltpu.make_async_remote_copy(
            src_ref=src, dst_ref=dst, send_sem=s_sem, recv_sem=r_sem,
            device_id=target, device_id_type=MESH,
        )

    cq = pl.ds(pl.multiple_of(c * half_q, half_q), half_q)
    oq = pl.ds(pl.multiple_of((1 - c) * half_q, half_q), half_q)
    ck = pl.ds(pl.multiple_of(c * half_k, half_k), half_k)
    ok = pl.ds(pl.multiple_of((1 - c) * half_k, half_k), half_k)
    my_rows = pl.ds(pl.multiple_of(c * piece, piece), piece)
    tall = piece + 16
    my_keys = pl.ds(pl.multiple_of(c * tall, 16), piece)
    my_stats = pl.ds(pl.multiple_of(c * tall + piece, 16), 16)
    my_part, twin_part = [
        [pl.ds(pl.multiple_of(k * size, 16), size) for size in (tall, piece)] for k in (c, 1 - c)
    ]
    ring_kv = (kn, vn)

    local = [
        pltpu.make_async_copy(pk_hbm.at[0, :, ck], kn.at[OWN, my_keys, :], sem_l.at[0]),
        pltpu.make_async_copy(pv_hbm.at[0, :, ck], vn.at[OWN, my_rows, :], sem_l.at[1]),
        pltpu.make_async_copy(q_hbm.at[0, 0, :, cq], qn.at[0], sem_l.at[2]),
        pltpu.make_async_copy(rk_hbm.at[0, 0, :, ck], rkn.at[0], sem_l.at[3]),
        pltpu.make_async_copy(rv_hbm.at[0, 0, :, ck], rvn.at[0], sem_l.at[4]),
        pltpu.make_async_copy(og_hbm.at[0, 0, :, cq], gn.at[0], sem_l.at[5]),
    ]
    for cp in local:
        cp.start()

    twin = at(0, 0, 1)
    z_to, up, down = at(1, 0, 0), at(0, 1, 0), at(0, 3, 0)
    groups = [{"grp": (grp + dg) % n_grp} for dg in range(1, n_grp)]
    friends = [twin, z_to, up, down]
    barrier = pltpu.get_barrier_semaphore()
    for friend in friends:
        pl.semaphore_signal(barrier, inc=1, device_id=friend, device_id_type=MESH)

    @pl.when(grp == 0)
    def _():
        for group in groups:
            pl.semaphore_signal(barrier, inc=1, device_id=group, device_id_type=MESH)

    def turn(src, dst, r):
        for j in range(2):
            for h in range(heads_per):
                dst[2 * r + j, :, h * rows:(h + 1) * rows] = src[
                    r, :, (j * heads_per + h) * DH:(j * heads_per + h + 1) * DH
                ].T

    def split_queries(r):
        for u in (2 * r, 2 * r + 1):
            for h in range(heads_per):
                cols = slice(h * rows, (h + 1) * rows)
                full = qT[u, :, cols].astype(F32) * scale2
                high = full.astype(BF16)
                q2[u, 0:DH, cols] = high
                q2[u, DH:2 * DH, cols] = (full - high.astype(F32)).astype(BF16)

    ones = jnp.ones((16, blk), BF16)

    def forward(units, keys, values, block, first):
        keys = {u: jnp.concatenate([k, k], axis=1) for u, k in keys.items()}
        values = {u: jnp.concatenate([v.T, ones], axis=0) for u, v in values.items()}
        todo = [(u, slice(h * rows, (h + 1) * rows)) for u in units for h in range(heads_per)]
        logits, lows = {}, {}

        def start(i):
            u, cols = todo[i]
            logits[i] = nn(keys[u], q2[u, :, cols])

        def finish(i):
            u, cols = todo[i]
            low, alpha = lows.pop(i)
            part = nn(values[u], low)
            if first:
                l_cur[u:u + 1, cols] = part[DH:DH + 1]
                acc[u, :, cols] = part[0:DH]
            else:
                l_cur[u:u + 1, cols] = l_cur[u:u + 1, cols] * alpha + part[DH:DH + 1]
                acc[u, :, cols] = acc[u, :, cols] * alpha + part[0:DH]

        for i in range(3):
            start(i)
        for i, (u, cols) in enumerate(todo):
            if i + 3 < len(todo):
                start(i + 3)
            s = logits.pop(i)
            if first:
                seen = lax.broadcasted_iota(jnp.int32, s.shape, 0) <= (
                    lax.broadcasted_iota(jnp.int32, s.shape, 1)
                )
                s = jnp.where(seen, s, -jnp.inf)
                m_new = jnp.max(s, axis=0, keepdims=True)
                alpha = None
            else:
                m_old = m_cur[u:u + 1, cols]
                m_new = jnp.maximum(m_old, jnp.max(s, axis=0, keepdims=True))
                alpha = jnp.exp2(m_old - m_new)
            low = jnp.exp2(s - m_new).astype(BF16)
            e_st[block, u, :, cols] = low
            m_cur[u:u + 1, cols] = m_new
            m_st[block, u:u + 1, cols] = m_new
            lows[i] = (low, alpha)
            if i >= 2:
                finish(i - 2)
        for i in sorted(lows):
            finish(i)

    def own_block(r):
        turn(qn, qT, r)
        split_queries(r)
        units = (2 * r, 2 * r + 1)
        forward(
            units,
            {u: rkn[r, :, (u % 2) * DH:(u % 2 + 1) * DH] for u in units},
            {u: rvn[r, :, (u % 2) * DH:(u % 2 + 1) * DH] for u in units},
            n_blocks, True,
        )

    row_id = lax.broadcasted_iota(jnp.int32, stat_own.shape, 0)
    stat_own[...] = jnp.where(
        row_id == 0,
        jnp.broadcast_to(len_ref[...], stat_own.shape),
        jnp.broadcast_to(rew_ref[...], stat_own.shape),
    ).astype(F32).astype(BF16)
    kn[OWN, my_stats, :] = stat_own[...]
    pl.semaphore_wait(barrier, len(friends) + jnp.minimum(grp, 1))

    pair = [
        to(pk_hbm.at[0, :, ok], kn.at[OWN, my_keys, :], sem_ps.at[0], sem_pr.at[0], twin),
        to(pv_hbm.at[0, :, ok], vn.at[OWN, my_rows, :], sem_ps.at[1], sem_pr.at[1], twin),
        to(q_hbm.at[0, 0, :, oq], qn.at[1], sem_ps.at[2], sem_pr.at[2], twin),
        to(rk_hbm.at[0, 0, :, ok], rkn.at[1], sem_ps.at[3], sem_pr.at[3], twin),
        to(rv_hbm.at[0, 0, :, ok], rvn.at[1], sem_ps.at[4], sem_pr.at[4], twin),
        to(og_hbm.at[0, 0, :, oq], gn.at[1], sem_ps.at[5], sem_pr.at[5], twin),
        to(stat_own, kn.at[OWN, my_stats, :], sem_ps.at[6], sem_pr.at[6], twin),
    ]
    for cp in (pair[0], pair[6], pair[1]):
        cp.start()

    ag = {}
    for kv in (0, 1):
        for dst, target in ((YM, up), (YP, down), (ZZ, z_to)):
            ag[dst, kv] = [
                to(
                    ring_kv[kv].at[OWN, part[kv], :], ring_kv[kv].at[dst, part[kv], :],
                    s_sem.at[dst, kv], r_sem.at[dst, kv], target,
                )
                for part, s_sem, r_sem in (
                    (my_part, sem_as, sem_ar), (twin_part, sem_bs, sem_br),
                )
            ]
    ag_plan = (
        (YM, YY, 0, up), (YM, ZYM, 0, z_to), (YM, ZYM, 1, z_to),
        (YP, YY, 1, down), (ZZ, ZYP, 0, down), (ZZ, ZYP, 1, down),
        (ZYM, ZYY, 0, up), (ZYM, ZYY, 1, up),
    )
    for src, dst, kv, target in ag_plan:
        ag[dst, kv] = [
            to(ring_kv[kv].at[src], ring_kv[kv].at[dst], sem_as.at[dst, kv], sem_ar.at[dst, kv], target)
        ]

    for kv in (0, 1):
        local[kv].wait()
        for dst in (YM, YP, ZZ):
            ag[dst, kv][0].start()
    for cp in pair[2:6]:
        cp.start()
    for kv in (0, 1):
        pair[kv].wait_recv()
        if kv == 0:
            pair[6].wait_recv()
        for dst in (YM, YP, ZZ):
            ag[dst, kv][1].start()


    n_blocks = 8
    for i in (2, 3, 4):
        local[i].wait()
    own_block(0)

    for i in (2, 3, 4):
        pair[i].wait_recv()
    own_block(1)
    local[5].wait()
    pair[5].wait_recv()
    for r in range(2):
        turn(gn, gT, r)
    dqa[...] = jnp.zeros_like(dqa)
    def keys_of(block, j):
        heads = slice(j * DH, (j + 1) * DH)
        return jnp.concatenate(
            [kn[block, 0:piece, heads], kn[block, tall:tall + piece, heads]], axis=0
        )

    def pass_on(waits, starts):
        for key in waits:
            for cp in ag[key]:
                cp.wait_recv()
        for key in starts:
            for cp in ag[key]:
                cp.start()

    @pl.loop(0, n_blocks)
    def forward_step(step):
        @pl.when(step == 1)
        def _():
            pass_on([(YM, 0)], [(YY, 0), (ZYM, 0)])
            pass_on([(ZZ, 0)], [(ZYP, 0)])
            pass_on([(YM, 1)], [(ZYM, 1)])
            pass_on([(YP, 0), (YP, 1)], [(YY, 1)])
            pass_on([(ZZ, 1)], [(ZYP, 1)])

        @pl.when(step == 3)
        def _():
            pass_on([(ZYM, 0)], [(ZYY, 0)])

        @pl.when(step == 4)
        def _():
            pass_on([(ZYM, 1)], [(ZYY, 1)])

        @pl.when(step == 5)
        def _():
            pass_on([(YY, 0), (YY, 1)], [])

        @pl.when(step == 6)
        def _():
            pass_on([(ZYP, 0), (ZYP, 1)], [])

        @pl.when(step == 7)
        def _():
            pass_on([(ZYY, 0), (ZYY, 1)], [])

        order = (0, 2, 1, 3)
        forward(
            order,
            {u: keys_of(step, u % 2) for u in order},
            {u: vn[step, :, (u % 2) * DH:(u % 2 + 1) * DH] for u in order},
            step, False,
        )

    sum_one = sum_two = live = jnp.zeros((1, 128), F32)
    for slot in range(n_blocks):
        for core in range(2):
            stat = kn[slot, core * tall + piece:(core + 1) * tall, 0:128].astype(F32)
            live = live + stat[0:1]
            sum_one = sum_one + stat[1:2]
            sum_two = sum_two + stat[1:2] * stat[1:2]
    stat_out[...] = jnp.broadcast_to(live, (8, 128))

    def count_in(slot):
        return to(
            stat_out, stat_in.at[slot], sem_ss.at[0], sem_sr.at[slot], {"grp": jnp.zeros_like(grp)}
        )

    def count_back(n):
        return to(stat_all, stat_all, sem_ss.at[n], sem_sr.at[0], groups[n - 1])

    @pl.when(grp != 0)
    def _():
        count_in(grp).start()

    n_resp = 16
    mean = sum_one / n_resp
    variance = (n_resp * sum_two - sum_one * sum_one) / (n_resp * n_resp)
    spread = jnp.maximum(jnp.sqrt(variance), 1.0)
    twin_stats = pl.ds(pl.multiple_of((1 - c) * tall + piece, 16), 16)
    for r in range(2):
        stat = stat_own[:, 0:128] if r == 0 else kn[OWN, twin_stats, 0:128]
        length = stat.astype(F32)[0:1].astype(jnp.int32)
        strength = (stat.astype(F32)[1:2] - mean) / spread
        weight = jnp.concatenate(
            [
                jnp.where(
                    lax.broadcasted_iota(jnp.int32, (1, 128), 1) + start < length, strength, 0.0
                )
                for start in range(0, rows, 128)
            ],
            axis=1,
        )
        for j in range(2):
            u = 2 * r + j
            for h in range(heads_per):
                cols = slice(h * rows, (h + 1) * rows)
                inv = 1.0 / l_cur[u:u + 1, cols]
                out = (acc[u, :, cols] * inv).astype(BF16)
                q2[u, 0:DH, cols] = out
                delta = jnp.sum(
                    out.astype(F32) * gT[u, :, cols].astype(F32), axis=0, keepdims=True
                )
                aux[0, u:u + 1, cols] = inv * weight
                aux[1, u:u + 1, cols] = delta

    def backward(units, keys, values, block, place):
        flat = {u: k.T for u, k in keys.items()}
        todo = [(u, h, slice(h * rows, (h + 1) * rows)) for u in units for h in range(heads_per)]
        scaled, shift, dots, lows, sums = {}, {}, {}, {}, {}

        def start(i):
            u, h, cols = todo[i]
            factor = jnp.exp2(m_st[block, u:u + 1, cols] - m_cur[u:u + 1, cols])
            factor = factor * aux[0, u:u + 1, cols]
            scaled[i] = (gT[u, :, cols].astype(F32) * factor).astype(BF16)
            shift[i] = factor * aux[1, u:u + 1, cols]
            dots[i] = nn(values[u], scaled[i])

        def add(key, term):
            sums[key] = sums[key] + term if key in sums else term

        def finish(i):
            u, h, cols = todo[i]
            low = lows.pop(i)
            col = (u % 2) * heads_per + h
            dqa[u, :, cols] = dqa[u, :, cols] + nn(flat[u], low)
            add((place(u), 0), nn(low, qn[u // 2, :, col * DH:(col + 1) * DH]))
            add((place(u), 1), nt(scaled.pop(i), e_st[block, u, :, cols]))

        for i in range(2):
            start(i)
        for i, (u, h, cols) in enumerate(todo):
            if i + 2 < len(todo):
                start(i + 2)
            d = dots.pop(i) - shift.pop(i)
            lows[i] = (e_st[block, u, :, cols].astype(F32) * d).astype(BF16)
            if i >= 1:
                finish(i - 1)
        finish(len(todo) - 1)
        return sums

    names = ("m1", "m6", "m3", "m2", "m7", "m5", "m4")
    route = {
        "m1": (down, down), "m6": (up, up), "m3": (down, up), "m2": (z_to, z_to),
        "m7": (z_to, z_to), "m5": (up, up), "m4": (down, down),
    }
    msg = {}
    for n, name in enumerate(names):
        for kv in range(2):
            msg[name, kv] = to(
                snd.at[n, kv], rcv.at[n, kv], sem_ms.at[n, kv], sem_mr.at[n, kv], route[name][kv]
            )

    needs = {
        0: ((), ()), 1: ((), ()), 2: ((), ()), 3: (("m1",), ("m1",)), 4: (("m6",), ("m6",)),
        5: ((), ("m3",)), 6: (("m2", "m3"), ("m2",)),
    }

    @pl.loop(0, n_blocks)
    def backward_step(step):
        @pl.when((step == 5) & (grp == 0))
        def _():
            total = stat_out[...]
            for slot in range(1, n_grp):
                count_in(slot).wait_recv()
                total = total + stat_in[slot]
            stat_all[...] = total
            for n in range(1, n_grp):
                count_back(n).start()

        block = n_blocks - 1 - step
        order = (0, 2, 1, 3)
        sums = backward(
            order,
            {u: keys_of(block, u % 2) for u in order},
            {u: vn[block, :, (u % 2) * DH:(u % 2 + 1) * DH] for u in order},
            block, lambda u: u % 2,
        )
        total_heads = 4 * heads_per
        for i in range(3):
            head = jnp.minimum(3 * step + i, total_heads - 1)
            u = head // heads_per
            h = head % heads_per
            col = pl.multiple_of(((u % 2) * heads_per + h) * DH, DH)
            att_n[u // 2, :, pl.ds(col, DH)] = q2[
                u, 0:DH, pl.ds(pl.multiple_of(h * rows, rows), rows)
            ].T
        for (j, kv), term in sums.items():
            if kv == 0:
                own_part[kv, :, j * DH:(j + 1) * DH] = term
            else:
                own_part[kv, j * DH:(j + 1) * DH, :] = term

        for n, name in enumerate(names):
            @pl.when(step == n)
            def _():
                for kv in range(2):
                    total = own_part[kv]
                    for other in needs[n][kv]:
                        msg[other, kv].wait_recv()
                        total = total + rcv[names.index(other), kv].astype(F32)
                    snd[n, kv] = total.astype(BF16)
                    msg[name, kv].start()

    att_own = pltpu.make_async_copy(att_n.at[0], att_hbm.at[0, 0, :, cq], sem_ol.at[0])
    att_twin = to(att_n.at[1], att_hbm.at[0, 0, :, cq], sem_os.at[0], sem_or.at[0], twin)
    att_own.start()
    att_twin.start()

    outs_own = [
        pltpu.make_async_copy(rg_n.at[0, 0], drk_hbm.at[0, 0, :, ck], sem_ol.at[1]),
        pltpu.make_async_copy(rg_n.at[0, 1], drv_hbm.at[0, 0, :, ck], sem_ol.at[2]),
        pltpu.make_async_copy(dq_n.at[0], dq_hbm.at[0, 0, :, cq], sem_ol.at[3]),
    ]
    outs_twin = [
        to(rg_n.at[1, 0], drk_hbm.at[0, 0, :, ck], sem_os.at[1], sem_or.at[1], twin),
        to(rg_n.at[1, 1], drv_hbm.at[0, 0, :, ck], sem_os.at[2], sem_or.at[2], twin),
        to(dq_n.at[1], dq_hbm.at[0, 0, :, cq], sem_os.at[3], sem_or.at[3], twin),
    ]
    for r in (1, 0):
        units = (2 * r, 2 * r + 1)
        sums = backward(
            units,
            {u: rkn[r, :, (u % 2) * DH:(u % 2 + 1) * DH] for u in units},
            {u: rvn[r, :, (u % 2) * DH:(u % 2 + 1) * DH] for u in units},
            n_blocks, lambda u: u,
        )
        if r == 1:
            @pl.when(grp != 0)
            def _():
                count_back(1).wait_recv()

            norm = (n_grp * n_resp * rows) / stat_all[0:1, :]
            norm_rows = jnp.concatenate([norm] * (rows // 128), axis=1)
        for j in range(2):
            for h in range(heads_per):
                col = slice((j * heads_per + h) * DH, (j * heads_per + h + 1) * DH)
                grad = dqa[2 * r + j, :, h * rows:(h + 1) * rows] * (norm_rows * inv_root)
                dq_n[r, :, col] = grad.astype(BF16).T
        for (u, kv), term in sums.items():
            if kv == 0:
                done = (term * (norm * inv_root)).astype(BF16)
            else:
                done = (term * norm_rows).astype(BF16).T
            rg_n[r, kv, :, (u % 2) * DH:(u % 2 + 1) * DH] = done
        for cp in outs_twin if r else outs_own:
            cp.start()

    twin_rows = pl.ds(pl.multiple_of((1 - c) * piece, piece), piece)
    for kv, out in enumerate((dpk_hbm, dpv_hbm)):
        total = own_part[kv]
        for name in ("m5", "m7", "m4"):
            msg[name, kv].wait_recv()
            total = total + rcv[names.index(name), kv].astype(F32)
        if kv == 0:
            pg_n[kv] = (total * (norm_rows * inv_root)).astype(BF16)
        else:
            pg_n[kv] = (total * norm_rows).astype(BF16).T
        outs_own.append(
            pltpu.make_async_copy(pg_n.at[kv, my_rows, :], out.at[0, :, ck], sem_ol.at[4 + kv])
        )
        outs_twin.append(
            to(
                pg_n.at[kv, twin_rows, :], out.at[0, :, ck],
                sem_os.at[4 + kv], sem_or.at[4 + kv], twin,
            )
        )
        outs_twin[-1].start()
        outs_own[-1].start()

    for cp in [att_own] + outs_own:
        cp.wait()
    for cp in [att_twin] + outs_twin:
        cp.wait()
    @pl.when(grp != 0)
    def _():
        count_in(grp).wait_send()

    @pl.when(grp == 0)
    def _():
        for n in range(1, n_grp):
            count_back(n).wait_send()

    for cp in pair + sum(ag.values(), []) + list(msg.values()):
        cp.wait_send()


def finish(*refs):
    ins, outs, bufs, (sem_in, sem_out) = refs[:6], refs[6:12], refs[12:18], refs[18:]
    loads, stores = [], []
    for src, dst, buf in zip(ins, outs, bufs):
        total = src.shape[-2]
        pieces = 4 if src.shape[-1] > 1024 else 1
        step = total // pieces
        lead = (0,) * (len(src.shape) - 2)
        for i in range(pieces):
            part = lead + (pl.ds(i * step, step),)
            n = len(loads)
            loads.append(pltpu.make_async_copy(src.at[part], buf.at[part], sem_in.at[n]))
            stores.append(pltpu.make_async_copy(buf.at[part], dst.at[part], sem_out.at[n]))
            loads[-1].start()
    for load, store in zip(loads, stores):
        load.wait()
        store.start()
    for store in stores:
        store.wait()


def on_device(n_grp, queries, resp_keys, resp_values, prompt_keys, prompt_values, out_grad,
              lengths, rewards):
    rows = queries.shape[2]
    half_q = queries.shape[3] // 2
    half_k = resp_keys.shape[3] // 2
    heads_per = half_q // half_k
    piece = prompt_keys.shape[1]
    blk = 2 * piece
    width = heads_per * rows
    anywhere = pl.BlockSpec(memory_space=pl.ANY)
    dma = pltpu.SemaphoreType.DMA
    vmem = pltpu.VMEM
    scratch = [
        vmem((2, rows, half_q), BF16), vmem((2, rows, half_q), BF16),
        vmem((2, rows, half_k), BF16), vmem((2, rows, half_k), BF16),
        vmem((8, blk + 32, half_k), BF16), vmem((8, blk, half_k), BF16),
        vmem((16, half_k), BF16),
        vmem((4, DH, width), BF16), vmem((4, 2 * DH, width), BF16), vmem((4, DH, width), BF16),
        vmem((9, 4, blk, width), BF16),
        vmem((9, 8, width), F32), vmem((8, width), F32), vmem((8, width), F32),
        vmem((4, DH, width), F32), vmem((4, DH, width), F32),
        vmem((2, 8, width), F32),
        vmem((8, 128), F32), vmem((n_grp, 8, 128), F32), vmem((8, 128), F32),
        vmem((7, 2, half_k, blk), BF16), vmem((7, 2, half_k, blk), BF16),
        vmem((2, half_k, blk), F32),
        vmem((2, rows, half_q), BF16), vmem((2, rows, half_q), BF16),
        vmem((2, 2, rows, half_k), BF16), vmem((2, blk, half_k), BF16),
        dma((6,)), dma((7,)), dma((7,)), dma((8, 2)), dma((8, 2)),
        dma((8, 2)), dma((8, 2)), dma((n_grp,)), dma((n_grp,)),
        dma((7, 2)), dma((7, 2)), dma((6,)), dma((6,)), dma((6,)),
    ]
    like = lambda a: jax.ShapeDtypeStruct(a.shape, a.dtype)
    shapes = (
        like(queries), like(queries), like(resp_keys), like(resp_values),
        like(prompt_keys), like(prompt_values),
    )
    results = pl.pallas_call(
        lambda *refs: kernel(n_grp, heads_per, *refs),
        out_shape=shapes,
        in_specs=[anywhere] * 6 + [pl.BlockSpec(memory_space=pltpu.VMEM)] * 2,
        out_specs=(anywhere,) * 6,
        scratch_shapes=scratch,
        compiler_params=pltpu.CompilerParams(
            collective_id=0, has_side_effects=True, vmem_limit_bytes=60 * 2**20
        ),
        name="grpo_attention",
    )(queries, resp_keys, resp_values, prompt_keys, prompt_values, out_grad, lengths, rewards)
    return pl.pallas_call(
        finish,
        out_shape=shapes,
        in_specs=[anywhere] * 6,
        out_specs=(anywhere,) * 6,
        scratch_shapes=[vmem(x.shape, x.dtype) for x in shapes] + [dma((12,)), dma((12,))],
        compiler_params=pltpu.CompilerParams(vmem_limit_bytes=60 * 2**20),
        name="write_results",
    )(*results)


def solution(mesh):
    n_grp = mesh.shape["grp"]
    wide = P("grp", "resp", None, None)
    tall = P("grp", "resp", None)
    return jax.shard_map(
        lambda *arrays: on_device(n_grp, *arrays),
        mesh=mesh,
        in_specs=(wide, wide, wide, tall, tall, wide, P("grp", "resp"), P("grp", "resp")),
        out_specs=(wide, wide, wide, wide, tall, tall),
        check_vma=False,
    )
```
